256 devices in a mesh: gx: 32 (over z, x_hi, core), gz: 8 (over x_lo, y).
Axes of the slice: x: 4 (x_hi: 2, x_lo: 2; x = x_hi * 2 + x_lo), y: 4, z: 8, core: 2. Of those that a mesh axis runs over, the one named last changes fastest.
Arguments:
- residual: float32 [224, 112, 512], P('gx', 'gz'), may hold values from -3 to 3
- layer_heights: float32 [73], replicated, may hold values from 0.25 to 1
Outputs:
- correction: float32 [224, 112, 512], P('gx', 'gz')
The draws below stay inside these ranges and needn't reach their ends.
All inputs are finite; a program needn't handle non-finite values.
Results may differ from the reference program's by a relative error of at most 0.0003.
Values sent between devices are 32-bit elements; how exact they have to be, the bound alone decides.
No kernel may reach another device: no remote copies, remote signals or barrier semaphores. Data moves between devices by JAX's collectives and lax.ppermute only.
A program may use at most 128 MiB of HBM per device.

```python
import math
import jax
import jax.numpy as jnp
import numpy as np
from jax import lax

WALL_LAYERS = 73
SMOOTH_STEPS = 3
COARSE_STEPS = 12
STREAM_ELEMENTS = 32
SPAN_ELEMENTS = 16


def draw_residual(key, part):
    key = jax.random.fold_in(key, 11)
    domain_extent = (STREAM_ELEMENTS * 7, SPAN_ELEMENTS * 7, WALL_LAYERS * 7 + 1)
    return jnp.clip(0.5 * jax.random.normal(key, domain_extent, jnp.float32), -3.0, 3.0)


def setup_inputs(seed: int = 0) -> dict:
    streams_of = jax.random.split(jax.random.key(seed), 3)
    return {
        "residual": draw_residual(jax.random.fold_in(streams_of[2], 71), 0),
        "layer_heights": jnp.clip(jnp.exp(jax.random.uniform(streams_of[1], (WALL_LAYERS,), jnp.float32, math.log(0.25), math.log(1.0))), 0.25, 1.0),
    }


highest = lax.Precision.HIGHEST
screen_shift = 0.02
smooth_floor = 0.1
coarse_floor = 0.01


def main_diagonal(matrix):
    indices = np.arange(matrix.shape[0])
    return matrix[indices, indices]


def legendre_values(points, degree):
    columns = [np.ones(points.shape), points]
    for degree_now in range(2, degree + 1):
        columns.append(((2 * degree_now - 1) * points * columns[-1] - (degree_now - 1) * columns[-2]) / degree_now)
    return np.stack(columns[: degree + 1], axis=1)


def gll_tables(degree):
    gll_nodes = -np.cos(np.pi * np.arange(degree + 1) / degree)
    for newton_step in range(100):
        values = legendre_values(gll_nodes, degree)
        gll_nodes = gll_nodes - (gll_nodes * values[:, degree] - values[:, degree - 1]) / ((degree + 1) * values[:, degree])
    leading = legendre_values(gll_nodes, degree)[:, degree]
    weights = 2.0 / (degree * (degree + 1) * leading ** 2)
    differ = np.zeros((degree + 1, degree + 1))
    for row_index in range(degree + 1):
        for col_index in range(degree + 1):
            if row_index != col_index:
                differ[row_index, col_index] = leading[row_index] / (leading[col_index] * (gll_nodes[row_index] - gll_nodes[col_index]))
    differ[0, 0] = -degree * (degree + 1) / 4.0
    differ[degree, degree] = degree * (degree + 1) / 4.0
    stiffness = differ.T @ (weights[:, None] * differ)
    return gll_nodes, weights, stiffness


def interp_table(fine_degree, coarse_degree):
    fine_nodes = gll_tables(fine_degree)[0]
    coarse_nodes = gll_tables(coarse_degree)[0]
    lagrange = np.ones((fine_degree + 1, coarse_degree + 1))
    for col_index in range(coarse_degree + 1):
        for other_node in range(coarse_degree + 1):
            if other_node != col_index:
                lagrange[:, col_index] *= (fine_nodes - coarse_nodes[other_node]) / (coarse_nodes[col_index] - coarse_nodes[other_node])
    return jnp.asarray(lagrange, jnp.float32)


def along(matrix, values, direction):
    letters = "abcde"[: values.ndim]
    result = letters[:direction] + "z" + letters[direction + 1:]
    formula = "z" + letters[direction] + "," + letters + "->" + result
    return jnp.einsum(formula, matrix, values, precision=highest)


def blocks_of(extended, direction, degree):
    layout = extended.shape
    length = layout[direction] - 1
    elements = length // degree
    leading = lax.slice_in_dim(extended, 0, length, axis=direction)
    leading = leading.reshape(layout[:direction] + (elements, degree) + layout[direction + 1:])
    trailing = lax.slice_in_dim(extended, degree, length + 1, stride=degree, axis=direction)
    trailing = trailing.reshape(layout[:direction] + (elements, 1) + layout[direction + 1:])
    return jnp.concatenate([leading, trailing], axis=direction + 1)


def assemble(element_values, direction, degree):
    layout = element_values.shape
    before = layout[:direction]
    after = layout[direction + 2:]
    elements = layout[direction]
    leading = lax.slice_in_dim(element_values, 0, degree, axis=direction + 1)
    trailing = lax.slice_in_dim(element_values, degree, degree + 1, axis=direction + 1)
    spare_block = jnp.zeros(before + (1, degree) + after, element_values.dtype)
    spare_end = jnp.zeros(before + (1, 1) + after, element_values.dtype)
    leading = jnp.concatenate([leading, spare_block], axis=direction)
    trailing = jnp.concatenate([spare_end, trailing], axis=direction)
    if degree > 1:
        filler = jnp.zeros(before + (elements + 1, degree - 1) + after, element_values.dtype)
        trailing = jnp.concatenate([trailing, filler], axis=direction + 1)
    merged = (leading + trailing).reshape(before + ((elements + 1) * degree,) + after)
    return lax.slice_in_dim(merged, 0, elements * degree + 1, axis=direction)


def element_stiff(extended, direction, degree, stiffness, factor):
    products = along(stiffness, blocks_of(extended, direction, degree), direction + 1)
    return assemble(products * factor, direction, degree)


def stay_put(face_plane, offset):
    return face_plane


def fold_back(summed, direction, length, neighbour):
    interior = lax.slice_in_dim(summed, 0, length, axis=direction)
    returned = neighbour(lax.slice_in_dim(summed, length, length + 1, axis=direction), 1)
    return jnp.concatenate([lax.slice_in_dim(interior, 0, 1, axis=direction) + returned, lax.slice_in_dim(interior, 1, length, axis=direction)], axis=direction)


def periodic_stiff(field, direction, degree, stiffness, neighbour):
    length = field.shape[direction]
    front_plane = lax.slice_in_dim(field, 0, 1, axis=direction)
    extended = jnp.concatenate([field, neighbour(front_plane, -1)], axis=direction)
    summed = element_stiff(extended, direction, degree, stiffness, 2.0)
    return fold_back(summed, direction, length, neighbour)


def periodic_line(degree, elements):
    weights, stiffness = gll_tables(degree)[1:]
    row_absolute = np.abs(stiffness).sum(axis=1)
    diag_entries = main_diagonal(stiffness)
    mass = np.tile(0.5 * weights[:degree], elements)
    diagonal = np.tile(2.0 * diag_entries[:degree], elements)
    spread = np.tile(2.0 * row_absolute[:degree], elements)
    mass[::degree] = weights[0]
    diagonal[::degree] = 2.0 * (stiffness[0, 0] + stiffness[degree, degree])
    spread[::degree] = 2.0 * (row_absolute[0] + row_absolute[degree])
    return jnp.asarray(mass, jnp.float32), jnp.asarray(diagonal, jnp.float32), float(np.max(spread / diagonal))


def wall_line(degree, heights):
    weights, stiffness = gll_tables(degree)[1:]
    half_height = (0.5 * heights)[:, None]
    weight_row = jnp.asarray(weights, jnp.float32)[None, :]
    diag_row = jnp.asarray(main_diagonal(stiffness), jnp.float32)[None, :]
    absolute_row = jnp.asarray(np.abs(stiffness).sum(axis=1), jnp.float32)[None, :]
    mass = assemble(half_height * weight_row, 0, degree)
    diagonal = assemble(diag_row / half_height, 0, degree)
    spread = assemble(absolute_row / half_height, 0, degree)
    return mass, diagonal, jnp.max(spread / diagonal)


def level_tables(degree, x_elements, z_elements, heights):
    mass_x, diag_x, ratio_x = periodic_line(degree, x_elements)
    mass_z, diag_z, ratio_z = periodic_line(degree, z_elements)
    mass_y, diag_y, ratio_y = wall_line(degree, heights)
    along_x = mass_x[:, None, None]
    along_z = mass_z[None, :, None]
    along_y = mass_y[None, None, :]
    diagonal = diag_x[:, None, None] * (along_z * along_y) + diag_z[None, :, None] * (along_x * along_y)
    diagonal = diagonal + diag_y[None, None, :] * (along_x * along_z) + screen_shift * (along_x * along_z * along_y)
    return {"degree": degree, "stiffness": jnp.asarray(gll_tables(degree)[2], jnp.float32),
            "wall_factor": (1.0 / (0.5 * heights)).reshape(1, 1, -1, 1),
            "mass_x": along_x, "mass_z": along_z, "mass_y": along_y,
            "inverse_diag": 1.0 / diagonal,
            "bound": jnp.maximum(ratio_y, max(1.0, ratio_x, ratio_z))}


def combine(field, along_x, along_z, along_y, data):
    mass_x = data["mass_x"]
    mass_z = data["mass_z"]
    mass_y = data["mass_y"]
    result = along_x * (mass_z * mass_y) + along_z * (mass_x * mass_y) + along_y * (mass_x * mass_z)
    return result + screen_shift * (mass_x * mass_z * mass_y) * field


def operate(field, data, x_move, z_move):
    degree = data["degree"]
    stiffness = data["stiffness"]
    along_x = periodic_stiff(field, 0, degree, stiffness, x_move)
    along_z = periodic_stiff(field, 1, degree, stiffness, z_move)
    along_y = element_stiff(field, 2, degree, stiffness, data["wall_factor"])
    return combine(field, along_x, along_z, along_y, data)


def chebyshev(source, start_iterate, sweeps, floor_frac, data, apply_fn):
    upper = data["bound"]
    centre = upper * (1.0 + floor_frac) / 2.0
    half_width = upper * (1.0 - floor_frac) / 2.0
    spread_ratio = centre / half_width
    factor_now = 1.0 / spread_ratio
    if start_iterate is None:
        remainder = source
        iterate = None
    else:
        remainder = source - apply_fn(start_iterate)
        iterate = start_iterate
    update = data["inverse_diag"] * remainder / centre
    for sweep_index in range(sweeps):
        iterate = update if iterate is None else iterate + update
        if sweep_index + 1 < sweeps:
            remainder = remainder - apply_fn(update)
            factor_next = 1.0 / (2.0 * spread_ratio - factor_now)
            update = factor_next * factor_now * update + (2.0 * factor_next / half_width) * data["inverse_diag"] * remainder
            factor_now = factor_next
    return iterate


def prolong_line(extended, direction, lagrange, coarse_degree, fine_degree):
    blocks = blocks_of(extended, direction, coarse_degree)
    fine_blocks = along(lagrange[:fine_degree], blocks, direction + 1)
    layout = fine_blocks.shape
    return fine_blocks.reshape(layout[:direction] + (layout[direction] * fine_degree,) + layout[direction + 2:])


def prolong_periodic(coarse_field, direction, lagrange, coarse_degree, fine_degree, neighbour):
    front_plane = lax.slice_in_dim(coarse_field, 0, 1, axis=direction)
    extended = jnp.concatenate([coarse_field, neighbour(front_plane, -1)], axis=direction)
    return prolong_line(extended, direction, lagrange, coarse_degree, fine_degree)


def prolong_wall(coarse_field, lagrange, coarse_degree, fine_degree):
    blocks = blocks_of(coarse_field, 2, coarse_degree)
    fine_blocks = along(lagrange, blocks, 3)
    layout = fine_blocks.shape
    leading = fine_blocks[:, :, :, :fine_degree].reshape(layout[0], layout[1], layout[2] * fine_degree)
    closing = fine_blocks[:, :, -1, fine_degree:]
    return jnp.concatenate([leading, closing], axis=2)


def prolong(coarse_field, lagrange, coarse_degree, fine_degree, x_move, z_move):
    widened = prolong_periodic(coarse_field, 0, lagrange, coarse_degree, fine_degree, x_move)
    widened = prolong_periodic(widened, 1, lagrange, coarse_degree, fine_degree, z_move)
    return prolong_wall(widened, lagrange, coarse_degree, fine_degree)


def restrict_line(fine_field, direction, lagrange, coarse_degree, fine_degree):
    layout = fine_field.shape
    elements = layout[direction] // fine_degree
    blocks = fine_field.reshape(layout[:direction] + (elements, fine_degree) + layout[direction + 1:])
    coarse_blocks = along(lagrange[:fine_degree].T, blocks, direction + 1)
    return assemble(coarse_blocks, direction, coarse_degree)


def restrict_periodic(fine_field, direction, lagrange, coarse_degree, fine_degree, neighbour):
    summed = restrict_line(fine_field, direction, lagrange, coarse_degree, fine_degree)
    return fold_back(summed, direction, summed.shape[direction] - 1, neighbour)


def restrict_wall(fine_field, lagrange, coarse_degree, fine_degree):
    summed = restrict_line(fine_field[:, :, :-1], 2, lagrange, coarse_degree, fine_degree)
    return jnp.concatenate([summed[:, :, :-1], summed[:, :, -1:] + fine_field[:, :, -1:]], axis=2)


def restrict(fine_field, lagrange, coarse_degree, fine_degree, x_move, z_move):
    narrowed = restrict_wall(fine_field, lagrange, coarse_degree, fine_degree)
    narrowed = restrict_periodic(narrowed, 1, lagrange, coarse_degree, fine_degree, z_move)
    return restrict_periodic(narrowed, 0, lagrange, coarse_degree, fine_degree, x_move)


def reference(residual, layer_heights):
    finest_level = level_tables(7, STREAM_ELEMENTS, SPAN_ELEMENTS, layer_heights)
    middle_level = level_tables(3, STREAM_ELEMENTS, SPAN_ELEMENTS, layer_heights)
    lowest_level = level_tables(1, STREAM_ELEMENTS, SPAN_ELEMENTS, layer_heights)
    lagrange_fine = interp_table(7, 3)
    lagrange_mid = interp_table(3, 1)

    def apply_fine(field):
        return operate(field, finest_level, stay_put, stay_put)

    def apply_mid(field):
        return operate(field, middle_level, stay_put, stay_put)

    def apply_low(field):
        return operate(field, lowest_level, stay_put, stay_put)

    smoothed_fine = chebyshev(residual, None, SMOOTH_STEPS, smooth_floor, finest_level, apply_fine)
    source_mid = restrict(residual - apply_fine(smoothed_fine), lagrange_fine, 3, 7, stay_put, stay_put)
    smoothed_mid = chebyshev(source_mid, None, SMOOTH_STEPS, smooth_floor, middle_level, apply_mid)
    source_low = restrict(source_mid - apply_mid(smoothed_mid), lagrange_mid, 1, 3, stay_put, stay_put)
    coarse_fix = chebyshev(source_low, None, COARSE_STEPS, coarse_floor, lowest_level, apply_low)
    smoothed_mid = chebyshev(source_mid, smoothed_mid + prolong(coarse_fix, lagrange_mid, 1, 3, stay_put, stay_put), SMOOTH_STEPS, smooth_floor, middle_level, apply_mid)
    return chebyshev(residual, smoothed_fine + prolong(smoothed_mid, lagrange_fine, 3, 7, stay_put, stay_put), SMOOTH_STEPS, smooth_floor, finest_level, apply_fine)
```

```python
import jax
import jax.numpy as jnp
import numpy as np
from jax import lax
from jax.experimental import pallas as pl
from jax.experimental.pallas import tpu as pltpu
from jax.sharding import PartitionSpec as P


SMOOTH_STEPS = 3
COARSE_STEPS = 12
NX, NZ, NY = 32, 16, 73
DEVICES = 256
ROWS = 80
screen_shift = 0.02
smooth_floor = 0.1
coarse_floor = 0.01
HI = lax.Precision.HIGHEST
f32 = jnp.float32


def legendre_values(points, degree):
    columns = [np.ones(points.shape), points]
    for n in range(2, degree + 1):
        columns.append(((2 * n - 1) * points * columns[-1] - (n - 1) * columns[-2]) / n)
    return np.stack(columns[: degree + 1], axis=1)


def gll_tables(degree):
    nodes = -np.cos(np.pi * np.arange(degree + 1) / degree)
    for _ in range(100):
        values = legendre_values(nodes, degree)
        nodes = nodes - (nodes * values[:, degree] - values[:, degree - 1]) / (
            (degree + 1) * values[:, degree]
        )
    leading = legendre_values(nodes, degree)[:, degree]
    weights = 2.0 / (degree * (degree + 1) * leading**2)
    differ = np.zeros((degree + 1, degree + 1))
    for i in range(degree + 1):
        for j in range(degree + 1):
            if i != j:
                differ[i, j] = leading[i] / (leading[j] * (nodes[i] - nodes[j]))
    differ[0, 0] = -degree * (degree + 1) / 4.0
    differ[degree, degree] = degree * (degree + 1) / 4.0
    return nodes, weights, differ.T @ (weights[:, None] * differ)


def interp_table(fine_degree, coarse_degree):
    fine_nodes = gll_tables(fine_degree)[0]
    coarse_nodes = gll_tables(coarse_degree)[0]
    lagrange = np.ones((fine_degree + 1, coarse_degree + 1))
    for col in range(coarse_degree + 1):
        for other in range(coarse_degree + 1):
            if other != col:
                lagrange[:, col] *= (fine_nodes - coarse_nodes[other]) / (
                    coarse_nodes[col] - coarse_nodes[other]
                )
    return lagrange


def lanes_of(values):
    n = values.shape[0]
    out = np.zeros((8, 8))
    out[:n, :n] = values
    return out.reshape(64)


def square_of(matrix, n_out, n_in):
    out = np.zeros((8, 8, 8, 8))
    out[:n_out, :n_out, :n_in, :n_in] = matrix.reshape(n_out, n_out, n_in, n_in)
    return out.reshape(64, 64)


def quad(b00, b01, b10, b11):
    return np.block([[b00, b01], [b10, b11]])


class Level:
    def __init__(self, q):
        self.q = q
        _, w, s = gll_tables(q)
        self.w, self.s = w, s
        mass = 0.5 * w[:q].copy()
        mass[0] = 0.5 * (w[0] + w[q])
        diag = 2.0 * np.diag(s)[:q].copy()
        diag[0] = 2.0 * (s[0, 0] + s[q, q])
        self.mxz = np.outer(mass, mass)
        a = np.outer(diag, mass) + np.outer(mass, diag) + screen_shift * self.mxz
        self.ratio = lanes_of(a / self.mxz)
        spread = np.abs(s).sum(axis=1)
        self.bound = max(1.0, float(np.max(spread / np.diag(s))))
        base = 2.0 * s[:q, :q].copy()
        base[0, 0] += 2.0 * s[q, q]
        e1 = np.zeros((q, q))
        e1[:, 0] = 2.0 * s[:q, q]
        even, odd = e1 + e1.T, e1 - e1.T
        dm = np.diag(mass)
        zero = np.zeros((64, 64))
        scale = np.concatenate([lanes_of(1.0 / self.mxz)] * 2)[None, :]
        sq = lambda m: square_of(m, q, q)
        fixed = sq(np.kron(base, dm) + np.kron(dm, base) + screen_shift * np.kron(dm, dm))
        tables = [quad(fixed, zero, zero, fixed)]
        for c, n in (
            (np.kron(even, dm), np.kron(odd, dm)),
            (np.kron(dm, even), np.kron(dm, odd)),
        ):
            c, n = sq(c), sq(n)
            tables.append(quad(c, zero, zero, c))
            tables.append(quad(zero, -n, n, zero))
        self.tables = [t * scale for t in tables]
        self.mass_lanes = np.concatenate([lanes_of(self.mxz)] * 2)
        self.inv_mass_lanes = np.concatenate([lanes_of(1.0 / self.mxz)] * 2)
        self.ratio_lanes = np.concatenate([self.ratio] * 2)
        self.mask_lanes = (self.mass_lanes > 0).astype(np.float64)


def transfer_tables(fine, coarse):
    j = interp_table(fine, coarse)
    ja = j[:fine, :coarse]
    jb = np.zeros((fine, coarse))
    jb[:, 0] = j[:fine, coarse]
    zero = np.zeros((64, 64))
    sq = lambda m: square_of(m, fine, coarse)
    flat = sq(np.kron(ja, ja))
    tables = [quad(flat, zero, zero, flat)]
    for b in (np.kron(jb, ja), np.kron(ja, jb), np.kron(jb, jb)):
        b = sq(b)
        tables.append(quad(b, zero, zero, b))
        tables.append(quad(zero, -b, b, zero))
    return j, tables


def mode_list():
    special = [((0, 0), (16, 0)), ((0, 8), (16, 8))]
    seen = {k for pair in special for k in pair}
    modes = list(special)
    for kx in range(NX):
        for kz in range(NZ):
            if (kx, kz) not in seen:
                seen.add((kx, kz))
                seen.add(((-kx) % NX, (-kz) % NZ))
                modes.append(((kx, kz), None))
    assert len(modes) == DEVICES
    return modes


def fourier_tables():
    x, z = np.meshgrid(np.arange(NX), np.arange(NZ), indexing="ij")
    x, z = x.reshape(-1), z.reshape(-1)
    forward = np.zeros((2 * DEVICES, NX * NZ))
    backward = np.zeros((NX * NZ, 2 * DEVICES))
    scalars = np.zeros((DEVICES, 16))
    total = NX * NZ
    for m, (first, second) in enumerate(mode_list()):
        tx = 2 * np.pi * first[0] / NX
        tz = 2 * np.pi * first[1] / NZ
        phi = tx * x + tz * z
        forward[2 * m] = np.cos(phi)
        if second is None:
            forward[2 * m + 1] = -np.sin(phi)
            backward[:, 2 * m] = 2.0 / total * np.cos(phi)
            backward[:, 2 * m + 1] = -2.0 / total * np.sin(phi)
            for n, t in enumerate((tx, tz, tx + tz)):
                scalars[m, 3 * n : 3 * n + 3] = np.cos(t), np.cos(t), np.sin(t)
        else:
            ux = 2 * np.pi * second[0] / NX
            uz = 2 * np.pi * second[1] / NZ
            psi = ux * x + uz * z
            forward[2 * m + 1] = np.cos(psi)
            backward[:, 2 * m] = 1.0 / total * np.cos(phi)
            backward[:, 2 * m + 1] = 1.0 / total * np.cos(psi)
            for n, (t, u) in enumerate(((tx, ux), (tz, uz), (tx + tz, ux + uz))):
                scalars[m, 3 * n : 3 * n + 3] = np.cos(t), np.cos(u), 0.0
    return forward, backward, scalars


FINE, MID, LOW = Level(7), Level(3), Level(1)
J7, P7_TABLES = transfer_tables(7, 3)
J3, P3_TABLES = transfer_tables(3, 1)
FORWARD, BACKWARD, SCALARS = fourier_tables()
MATRICES = np.stack(FINE.tables + MID.tables + P7_TABLES + P3_TABLES).astype(np.float32)
G7_AT, G3_AT, P7_AT, P3_AT = 0, 5, 10, 17
LANES = np.zeros((16, 128))
for n, level in enumerate((FINE, MID)):
    LANES[4 * n] = level.mass_lanes
    LANES[4 * n + 1] = level.inv_mass_lanes
    LANES[4 * n + 2] = level.ratio_lanes
    LANES[4 * n + 3] = level.mask_lanes
LANES[8] = LOW.mask_lanes
LANES = LANES.astype(np.float32)


def cheb_steps(bound, sweeps, floor):
    centre = bound * (1.0 + floor) / 2.0
    half = bound * (1.0 - floor) / 2.0
    s = centre / half
    p = 1.0 / s
    steps = []
    for _ in range(sweeps - 1):
        p_next = 1.0 / (2.0 * s - p)
        steps.append((p_next * p, 2.0 * p_next / half))
        p = p_next
    return 1.0 / centre, steps


def pack_kernel(x_ref, o_ref, m_ref):
    m_ref[...] = jnp.zeros_like(m_ref)
    for e in range(2):
        for h in range(2):
            for a in range(7):
                r = e * 128 + h * 64 + a * 8
                m_ref[r : r + 7, :] = x_ref[a, e * 7 : e * 7 + 7, h * 256 : h * 256 + 256]
    for e in range(2):
        o_ref[pl.ds(e, 256, stride=2), :] = m_ref[e * 128 : e * 128 + 128, :].T


def unpack_kernel(x_ref, o_ref):
    for e in range(2):
        m = x_ref[pl.ds(e, 256, stride=2), :].T
        for h in range(2):
            for a in range(7):
                r = h * 64 + a * 8
                o_ref[a, e * 7 : e * 7 + 7, h * 256 : h * 256 + 256] = m[r : r + 7, :]


def dft_kernel(f_ref, x_ref, o_ref):
    o_ref[...] = jnp.dot(f_ref[...], x_ref[...], precision=HI, preferred_element_type=f32)


def roll_up(v):
    return pltpu.roll(v, ROWS - 1, axis=0)


def roll_down(v):
    return pltpu.roll(v, 1, axis=0)


def wall_apply(s, q, planes, g):
    parts = [g * p for p in planes] + [g * roll_up(planes[0])]
    n = q + 1
    half = n // 2
    even = [parts[l] + parts[q - l] for l in range(half)]
    odd = [parts[l] - parts[q - l] for l in range(half)]
    out = [None] * n
    for k in range(half):
        p = m = None
        for l in range(half):
            ce = 0.5 * (s[k, l] + s[k, q - l])
            co = 0.5 * (s[k, l] - s[k, q - l])
            te, to = float(ce) * even[l], float(co) * odd[l]
            p = te if p is None else p + te
            m = to if m is None else m + to
        out[k] = p + m
        out[q - k] = p - m
    out[0] = out[0] + roll_down(out[q])
    return out[:q]


def weighted_sum(coefs, planes):
    total = None
    for c, v in zip(coefs, planes):
        c = float(c)
        if c == 0.0:
            continue
        t = v if c == 1.0 else c * v
        total = t if total is None else total + t
    return total


def restrict_wall(j, fine, coarse, planes):
    out = [weighted_sum(j[:fine, c], planes) for c in range(coarse)]
    out[0] = out[0] + roll_down(weighted_sum(j[:fine, coarse], planes))
    return out


def prolong_wall(j, fine, coarse, planes):
    closed = list(planes) + [roll_up(planes[0])]
    return [weighted_sum(j[k], closed) for k in range(fine)]


def cycle_kernel(
    idx_ref, scal_ref, h_ref, lanes_ref, mats_ref, in_ref, out_ref,
    w_ref, hrow_ref, geo_ref,
    u7, r7, x7, d7, u3, r3, x3, d3,
    g7_ref, g3_ref, p7_ref, p3_ref,
):
    base = idx_ref[0] * 16
    sc = [scal_ref[base + n] for n in range(9)]
    lane = lax.broadcasted_iota(jnp.int32, (1, 128), 1)
    first = lane < 64

    cosines = [jnp.where(first, sc[3 * n], sc[3 * n + 1]) for n in range(3)]
    sines = [sc[3 * n + 2] for n in range(3)]
    for ref, at, phases in ((g7_ref, G7_AT, 2), (g3_ref, G3_AT, 2), (p7_ref, P7_AT, 3), (p3_ref, P3_AT, 3)):
        total = mats_ref[at]
        for n in range(phases):
            total = total + cosines[n] * mats_ref[at + 1 + 2 * n]
            total = total + sines[n] * mats_ref[at + 2 + 2 * n]
        ref[...] = total

    hrow_ref[...] = jnp.zeros_like(hrow_ref)
    hrow_ref[0:1, 0:NY] = h_ref[...]
    h = jnp.broadcast_to(hrow_ref[0:1, :], (128, 128)).T[:ROWS]
    row = lax.broadcasted_iota(jnp.int32, (ROWS, 128), 0)
    g = jnp.where(row < NY, 2.0 / jnp.where(row < NY, h, 1.0), 0.0)
    h_pair = h + roll_down(h)
    g_pair = g + roll_down(g)
    geo_ref[0] = h
    geo_ref[1] = g
    geo_ref[2] = h_pair

    def wall_mass(level, k):
        if k == 0:
            return (0.5 * float(level.w[0])) * geo_ref[2]
        return (0.5 * float(level.w[k])) * geo_ref[0]

    def inverse_diag(level, ratio, mask, k):
        s = level.s
        dy = float(s[0, 0]) * g_pair if k == 0 else float(s[k, k]) * g
        d = wall_mass(level, k) * ratio + dy
        return jnp.where(d > 0.0, mask / jnp.where(d > 0.0, d, 1.0), 0.0)

    mass7, inv7, ratio7, mask7 = (lanes_ref[n : n + 1, :] for n in range(4))
    mass3, inv3, ratio3, mask3 = (lanes_ref[n : n + 1, :] for n in range(4, 8))
    mask1 = lanes_ref[8:9, :]
    for k in range(7):
        d7[k] = inverse_diag(FINE, ratio7, mask7, k)
    for k in range(3):
        d3[k] = inverse_diag(MID, ratio3, mask3, k)
    d1_mix = (
        jnp.where(first, 2.0 - 2.0 * sc[0], 2.0 - 2.0 * sc[1])
        + jnp.where(first, 2.0 - 2.0 * sc[3], 2.0 - 2.0 * sc[4])
        + screen_shift
    ) * mask1
    d1 = inverse_diag(LOW, 4.0 + screen_shift, mask1, 0)

    re = in_ref[pl.ds(0, 256, stride=2), :]
    im = in_ref[pl.ds(1, 256, stride=2), :]
    w_ref[0:256, :] = jnp.where(first, re, pltpu.roll(im, 64, axis=1)) * inv7
    w_ref[256:512, :] = jnp.where(first, pltpu.roll(re, 64, axis=1), im) * inv7
    w_ref[512:, :] = jnp.zeros((w_ref.shape[0] - 512, 128), f32)
    for k in range(7):
        r7[k] = w_ref[pl.ds(k, ROWS, stride=7), :]

    def apply(level, u, table):
        q = level.q
        flat = u[...].reshape(q * ROWS, 128)
        m = jnp.dot(flat, table[...], precision=HI, preferred_element_type=f32)
        wall = wall_apply(level.s, q, [u[k] for k in range(q)], geo_ref[1])
        return [wall_mass(level, k) * m[k * ROWS : (k + 1) * ROWS] + wall[k] for k in range(q)]

    def smooth(level, u, r, x, d, table, fresh, keep_residual):
        q = level.q
        start, steps = cheb_steps(level.bound, SMOOTH_STEPS, smooth_floor)
        for k in range(q):
            t = start * (d[k] * r[k])
            u[k] = t
            x[k] = t if fresh else x[k] + t
        for alpha, beta in steps:
            au = apply(level, u, table)
            for k in range(q):
                t = r[k] - au[k]
                r[k] = t
                t = alpha * u[k] + beta * (d[k] * t)
                u[k] = t
                x[k] = x[k] + t
        if keep_residual:
            au = apply(level, u, table)
            for k in range(q):
                r[k] = r[k] - au[k]

    def restrict_lanes(planes, table, mass):
        flat = jnp.concatenate([p * mass for p in planes], axis=0)
        m = jnp.dot(flat, table[...], precision=HI, preferred_element_type=f32)
        return [m[k * ROWS : (k + 1) * ROWS] for k in range(len(planes))]

    def prolong_lanes(planes, table):
        flat = jnp.concatenate(planes, axis=0)
        m = lax.dot_general(
            flat, table[...], (((1,), (1,)), ((), ())), precision=HI, preferred_element_type=f32
        )
        return [m[k * ROWS : (k + 1) * ROWS] for k in range(len(planes))]

    smooth(FINE, u7, r7, x7, d7, g7_ref, True, True)
    down = restrict_wall(J7, 7, 3, [r7[k] for k in range(7)])
    down = restrict_lanes(down, p7_ref, mass7)
    for k in range(3):
        r3[k] = down[k] * inv3

    smooth(MID, u3, r3, x3, d3, g3_ref, True, True)
    down = restrict_wall(J3, 3, 1, [r3[k] for k in range(3)])
    r1 = restrict_lanes(down, p3_ref, mass3)[0]

    start, steps = cheb_steps(LOW.bound, COARSE_STEPS, coarse_floor)
    my1 = wall_mass(LOW, 0) * d1_mix
    u1 = start * (d1 * r1)
    x1 = u1
    for alpha, beta in steps:
        flow = (0.5 * g) * (u1 - roll_up(u1))
        r1 = r1 - (my1 * u1 + (flow - roll_down(flow)))
        u1 = alpha * u1 + beta * (d1 * r1)
        x1 = x1 + u1

    up = prolong_wall(J3, 3, 1, prolong_lanes([x1], p3_ref))
    for k in range(3):
        u3[k] = up[k]
        x3[k] = x3[k] + up[k]
    au = apply(MID, u3, g3_ref)
    for k in range(3):
        r3[k] = r3[k] - au[k]
    smooth(MID, u3, r3, x3, d3, g3_ref, False, False)

    up = prolong_wall(J7, 7, 3, prolong_lanes([x3[k] for k in range(3)], p7_ref))
    for k in range(7):
        u7[k] = up[k]
        x7[k] = x7[k] + up[k]
    au = apply(FINE, u7, g7_ref)
    for k in range(7):
        r7[k] = r7[k] - au[k]
    smooth(FINE, u7, r7, x7, d7, g7_ref, False, False)

    for k in range(7):
        w_ref[pl.ds(k, ROWS, stride=7), :] = x7[k]
    top = w_ref[0:256, :]
    low = w_ref[256:512, :]
    out_ref[pl.ds(0, 256, stride=2), :] = jnp.where(first, top, pltpu.roll(low, 64, axis=1))
    out_ref[pl.ds(1, 256, stride=2), :] = jnp.where(first, pltpu.roll(top, 64, axis=1), low)


VMEM = pl.BlockSpec(memory_space=pltpu.VMEM)
SMEM = pl.BlockSpec(memory_space=pltpu.SMEM)
PARAMS = pltpu.CompilerParams(vmem_limit_bytes=32 * 1024 * 1024)
FLAT = jax.ShapeDtypeStruct((512, 128), f32)


def exchange(block):
    moved = lax.all_to_all(block.reshape(DEVICES, 2, 128), ("gx", "gz"), 0, 0)
    return moved.reshape(512, 128)


def transform(table, block):
    return pl.pallas_call(
        dft_kernel, out_shape=FLAT, in_specs=[VMEM, VMEM], out_specs=VMEM, compiler_params=PARAMS
    )(jnp.asarray(table, f32), block)


def body(residual, layer_heights):
    packed = pl.pallas_call(
        pack_kernel, out_shape=FLAT, in_specs=[VMEM], out_specs=VMEM,
        scratch_shapes=[pltpu.VMEM((256, 256), f32)], compiler_params=PARAMS,
    )(residual)
    modes = exchange(transform(FORWARD, exchange(packed)))
    place = lax.axis_index("gx") * 8 + lax.axis_index("gz")
    fine = pltpu.VMEM((7, ROWS, 128), f32)
    mid = pltpu.VMEM((3, ROWS, 128), f32)
    square = pltpu.VMEM((128, 128), f32)
    solved = pl.pallas_call(
        cycle_kernel, out_shape=FLAT,
        in_specs=[SMEM, SMEM, VMEM, VMEM, VMEM, VMEM], out_specs=VMEM,
        scratch_shapes=[
            pltpu.VMEM((7 * ROWS, 128), f32), pltpu.VMEM((8, 128), f32),
            pltpu.VMEM((3, ROWS, 128), f32),
            fine, fine, fine, fine, mid, mid, mid, mid,
            square, square, square, square,
        ],
        compiler_params=PARAMS,
    )(
        place.astype(jnp.int32).reshape(1),
        jnp.asarray(SCALARS.reshape(-1), f32),
        layer_heights.reshape(1, NY),
        jnp.asarray(LANES),
        jnp.asarray(MATRICES),
        modes,
    )
    spread = exchange(transform(BACKWARD, exchange(solved)))
    return pl.pallas_call(
        unpack_kernel, out_shape=jax.ShapeDtypeStruct((7, 14, 512), f32),
        in_specs=[VMEM], out_specs=VMEM, compiler_params=PARAMS,
    )(spread)


def solution(mesh):
    return jax.shard_map(
        body,
        mesh=mesh,
        in_specs=(P("gx", "gz", None), P()),
        out_specs=P("gx", "gz", None),
        check_vma=False,
    )
```

```python
import jax
import jax.numpy as jnp
import ml_dtypes
import numpy as np
from jax import lax
from jax.experimental import pallas as pl
from jax.experimental.pallas import tpu as pltpu
from jax.sharding import PartitionSpec as P


SMOOTH_STEPS = 3
COARSE_STEPS = 12
NX, NZ, NY = 32, 16, 73
DEVICES = 256
ROWS = 80
screen_shift = 0.02
smooth_floor = 0.1
coarse_floor = 0.01
f32 = jnp.float32
bf16 = jnp.bfloat16


def legendre_values(points, degree):
    columns = [np.ones(points.shape), points]
    for n in range(2, degree + 1):
        columns.append(((2 * n - 1) * points * columns[-1] - (n - 1) * columns[-2]) / n)
    return np.stack(columns[: degree + 1], axis=1)


def gll_tables(degree):
    nodes = -np.cos(np.pi * np.arange(degree + 1) / degree)
    for _ in range(100):
        values = legendre_values(nodes, degree)
        nodes = nodes - (nodes * values[:, degree] - values[:, degree - 1]) / (
            (degree + 1) * values[:, degree]
        )
    leading = legendre_values(nodes, degree)[:, degree]
    weights = 2.0 / (degree * (degree + 1) * leading**2)
    differ = np.zeros((degree + 1, degree + 1))
    for i in range(degree + 1):
        for j in range(degree + 1):
            if i != j:
                differ[i, j] = leading[i] / (leading[j] * (nodes[i] - nodes[j]))
    differ[0, 0] = -degree * (degree + 1) / 4.0
    differ[degree, degree] = degree * (degree + 1) / 4.0
    return nodes, weights, differ.T @ (weights[:, None] * differ)


def interp_table(fine_degree, coarse_degree):
    fine_nodes = gll_tables(fine_degree)[0]
    coarse_nodes = gll_tables(coarse_degree)[0]
    lagrange = np.ones((fine_degree + 1, coarse_degree + 1))
    for col in range(coarse_degree + 1):
        for other in range(coarse_degree + 1):
            if other != col:
                lagrange[:, col] *= (fine_nodes - coarse_nodes[other]) / (
                    coarse_nodes[col] - coarse_nodes[other]
                )
    return lagrange


def lanes_of(values):
    n = values.shape[0]
    out = np.zeros((8, 8))
    out[:n, :n] = values
    return out.reshape(64)


def square_of(matrix, n_out, n_in):
    out = np.zeros((8, 8, 8, 8))
    out[:n_out, :n_out, :n_in, :n_in] = matrix.reshape(n_out, n_out, n_in, n_in)
    return out.reshape(64, 64)


class Level:
    def __init__(self, q):
        self.q = q
        _, w, s = gll_tables(q)
        self.w, self.s = w, s
        mass = 0.5 * w[:q].copy()
        mass[0] = 0.5 * (w[0] + w[q])
        diag = 2.0 * np.diag(s)[:q].copy()
        diag[0] = 2.0 * (s[0, 0] + s[q, q])
        self.mxz = np.outer(mass, mass)
        a = np.outer(diag, mass) + np.outer(mass, diag) + screen_shift * self.mxz
        self.ratio = lanes_of(a / self.mxz)
        spread = np.abs(s).sum(axis=1)
        self.bound = max(1.0, float(np.max(spread / np.diag(s))))
        base = 2.0 * s[:q, :q].copy()
        base[0, 0] += 2.0 * s[q, q]
        e1 = np.zeros((q, q))
        e1[:, 0] = 2.0 * s[:q, q]
        even, odd = e1 + e1.T, e1 - e1.T
        dm = np.diag(mass)
        scale = np.concatenate([lanes_of(1.0 / self.mxz)] * 2)[None, :]
        sq = lambda m: square_of(m, q, q)
        fixed = sq(np.kron(base, dm) + np.kron(dm, base) + screen_shift * np.kron(dm, dm))
        tables = [np.hstack([fixed, 0.0 * fixed])]
        for c, n in (
            (np.kron(even, dm), np.kron(odd, dm)),
            (np.kron(dm, even), np.kron(dm, odd)),
        ):
            tables.append(np.hstack([sq(c), -sq(n)]))
        self.tables = [(t * scale)[: 64 if q > 3 else 24] for t in tables]
        self.weight = 0.5 * w
        self.stiff = s / self.weight[:, None]
        self.mass_lanes = np.concatenate([lanes_of(self.mxz)] * 2)
        self.inv_mass_lanes = np.concatenate([lanes_of(1.0 / self.mxz)] * 2)
        self.ratio_lanes = np.concatenate([self.ratio] * 2)
        self.mask_lanes = (self.mass_lanes > 0).astype(np.float64)


def transfer_tables(fine, coarse):
    j = interp_table(fine, coarse)
    ja = j[:fine, :coarse]
    jb = np.zeros((fine, coarse))
    jb[:, 0] = j[:fine, coarse]
    tables = []
    for n, b in enumerate((np.kron(ja, ja), np.kron(jb, ja), np.kron(ja, jb), np.kron(jb, jb))):
        b = square_of(b, fine, coarse).T[: 24 if coarse > 1 else 8]
        tables.append(np.hstack([b, b if n else 0.0 * b]))
    return j, tables


def flow_tables():
    x = np.arange(NX)
    forward = np.zeros((2, 2 * NX, 2 * NX))
    backward = np.zeros((2, 2 * NX, 2 * NX))
    phases = np.zeros((152, 2, 64))
    re, im = slice(0, NX), slice(NX, 2 * NX)
    for n in range(NX):
        c, s = np.cos(2 * np.pi * n * x / NX), np.sin(2 * np.pi * n * x / NX)
        forward[1, 2 * n, re], forward[1, 2 * n, im] = c, s
        forward[1, 2 * n + 1, re], forward[1, 2 * n + 1, im] = -s, c
        backward[1, re, 2 * n], backward[1, re, 2 * n + 1] = c / NX, -s / NX
        backward[1, im, 2 * n], backward[1, im, 2 * n + 1] = s / NX, c / NX
        t = 2 * np.pi * n / NX
        phases[64 + 2 * n], phases[65 + 2 * n] = np.cos(t), np.sin(t)
    for half in range(2):
        part = slice(half * NX, half * NX + NX)
        for k in range(16):
            n = 16 * half + k
            if k:
                c, s = np.cos(2 * np.pi * k * x / NX), np.sin(2 * np.pi * k * x / NX)
                forward[0, 2 * n, part], forward[0, 2 * n + 1, part] = c, -s
                backward[0, part, 2 * n] = 2 * c / NX
                backward[0, part, 2 * n + 1] = -2 * s / NX
                t = 2 * np.pi * k / NX
                phases[2 * n], phases[2 * n + 1] = np.cos(t), np.sin(t)
            else:
                one, turn = np.ones(NX), np.cos(np.pi * x)
                forward[0, 2 * n, part], forward[0, 2 * n + 1, part] = one, turn
                backward[0, part, 2 * n], backward[0, part, 2 * n + 1] = one / NX, turn / NX
                phases[2 * n, 0], phases[2 * n, 1] = 1.0, -1.0
    for b in range(9):
        t = 2 * np.pi * b / NZ
        phases[128 + 2 * b], phases[129 + 2 * b] = np.cos(t), np.sin(t) if b % 8 else 0.0
    return forward, backward, phases.reshape(152, 128)


FINE, MID, LOW = Level(7), Level(3), Level(1)
J7, P7_TABLES = transfer_tables(7, 3)
J3, P3_TABLES = transfer_tables(3, 1)
FORWARD, BACKWARD, PHASES = flow_tables()
MATRICES = np.concatenate(FINE.tables + MID.tables + P7_TABLES + P3_TABLES).astype(np.float32)
R7 = FINE.weight[:, None] * J7 / MID.weight
R3 = MID.weight[:, None] * J3 / LOW.weight
G7_AT, G3_AT, P7_AT, P3_AT = 0, 192, 264, 360


def split_terms(tables):
    high = tables.astype(np.float32).astype(ml_dtypes.bfloat16)
    low = (tables - high.astype(np.float64)).astype(ml_dtypes.bfloat16)
    rows = np.concatenate([high, high, low], axis=2).reshape(4 * NX, 6 * NX)
    return np.concatenate([rows, np.zeros((4 * NX, 2 * NX), rows.dtype)], axis=1)


LANES = np.zeros((16, 128))
for n, level in enumerate((FINE, MID)):
    LANES[4 * n] = level.mass_lanes
    LANES[4 * n + 1] = level.inv_mass_lanes
    LANES[4 * n + 2] = level.ratio_lanes
    LANES[4 * n + 3] = level.mask_lanes
LANES[8] = LOW.mask_lanes
MATRICES = np.concatenate([MATRICES, LANES, PHASES]).astype(np.float32)
LANES_AT, PHASES_AT = 392, 408


def cheb_steps(bound, sweeps, floor):
    centre = bound * (1.0 + floor) / 2.0
    half = bound * (1.0 - floor) / 2.0
    s = centre / half
    p = 1.0 / s
    steps = []
    for _ in range(sweeps - 1):
        p_next = 1.0 / (2.0 * s - p)
        steps.append((p_next * p, 2.0 * p_next / half))
        p = p_next
    return 1.0 / centre, steps


def pack_kernel(x_ref, h_ref, o_ref, rows_ref, m_ref, line_ref):
    m_ref[...] = jnp.zeros_like(m_ref)
    for e in range(2):
        for h in range(2):
            for a in range(7):
                r = e * 128 + h * 64 + a * 8
                m_ref[r : r + 7, :] = x_ref[a, e * 7 : e * 7 + 7, h * 256 : h * 256 + 256]
    for e in range(2):
        o_ref[pl.ds(e, 256, stride=2), :] = m_ref[e * 128 : e * 128 + 128, :].T
    line_ref[...] = jnp.zeros_like(line_ref)
    line_ref[0:1, 0:NY] = h_ref[...]
    rows_ref[...] = jnp.broadcast_to(line_ref[0:1, :], (128, 128)).T[:ROWS]


def unpack_kernel(x_ref, o_ref):
    for e in range(2):
        m = x_ref[pl.ds(e, 256, stride=2), :].T
        for h in range(2):
            for a in range(7):
                r = h * 64 + a * 8
                o_ref[a, e * 7 : e * 7 + 7, h * 256 : h * 256 + 256] = m[r : r + 7, :]


def halves(v):
    high = v.astype(bf16)
    return high, (v - high.astype(f32)).astype(bf16)


def dot(a, b):
    return jnp.dot(a, b, preferred_element_type=f32)


def combine(pairs):
    total = None
    for c, v in pairs:
        c = float(c)
        if abs(c) < 1e-12:
            continue
        if abs(abs(c) - 1.0) < 1e-12:
            t = v
            if total is None:
                total = v if c > 0 else -v
            else:
                total = total + v if c > 0 else total - v
            continue
        t = c * v
        total = t if total is None else total + t
    return total


def flow_product(f_ref, which, rows):
    v = jnp.concatenate(rows, axis=1)
    high, low = halves(v)
    t = f_ref[which * 64 : which * 64 + 64, :][:, :192]
    return dot(t, jnp.concatenate([high, low, high], axis=0))


def forward_kernel(f_ref, x_ref, o_ref):
    v = [x_ref[pl.ds(z, NX, stride=NZ), :] for z in range(NZ)]
    ends = (v[0] + v[8], v[0] - v[8])
    even = [None] + [v[z] + v[16 - z] for z in range(1, 8)]
    odd = [None] + [v[z] - v[16 - z] for z in range(1, 8)]
    even2 = [[None] + [even[z] + even[8 - z] for z in (1, 2, 3)], [None] + [even[z] - even[8 - z] for z in (1, 2, 3)]]
    odd2 = [[None] + [odd[z] - odd[8 - z] for z in (1, 2, 3)], [None] + [odd[z] + odd[8 - z] for z in (1, 2, 3)]]
    re, im = [], []
    for k in range(9):
        a = 2 * np.pi * k / NZ
        p = k % 2
        pairs = [(1.0, ends[p])] + [(np.cos(a * z), even2[p][z]) for z in (1, 2, 3)]
        re.append(combine(pairs + [(np.cos(4 * a), even[4])]))
        pairs = [(-np.sin(a * z), odd2[p][z]) for z in (1, 2, 3)]
        im.append(combine(pairs + [(-np.sin(4 * a), odd[4])]) if 0 < k < 8 else None)
    im[0] = re[8]
    blocks = [jnp.concatenate([re[k], im[k]], axis=0) for k in range(8)]
    o_ref[0:64, :] = flow_product(f_ref, 0, blocks[:1])
    out = flow_product(f_ref, 1, blocks[1:])
    for k in range(7):
        o_ref[64 * k + 64 : 64 * k + 128, :] = out[:, 128 * k : 128 * k + 128]


def backward_kernel(f_ref, x_ref, o_ref):
    blocks = [x_ref[64 * k : 64 * k + 64, :] for k in range(8)]
    first = flow_product(f_ref, 0, blocks[:1])
    rest = flow_product(f_ref, 1, blocks[1:])
    parts = [first] + [rest[:, 128 * k : 128 * k + 128] for k in range(7)]
    re = [v[0:NX] for v in parts] + [first[NX:]]
    im = [v[NX:] for v in parts]
    for z in range(5):
        a = 2 * np.pi * z / NZ
        e0 = combine([(1 / 16, re[0]), (np.cos(8 * a) / 16, re[8])] + [(np.cos(a * k) / 8, re[k]) for k in (2, 4, 6)])
        e1 = combine([(np.cos(a * k) / 8, re[k]) for k in (1, 3, 5, 7)])
        o0 = combine([(np.sin(a * k) / 8, im[k]) for k in (2, 4, 6)])
        o1 = combine([(np.sin(a * k) / 8, im[k]) for k in (1, 3, 5, 7)])
        plus = lambda p, q: q if p is None else p if q is None else p + q
        minus = lambda p, q: p if q is None else -q if p is None else p - q
        places = [(z, plus(e0, e1), plus(o0, o1))]
        if z < 4:
            places.append((8 - z, minus(e0, e1), minus(o1, o0)))
        for place, e, o in places:
            o_ref[pl.ds(place, NX, stride=NZ), :] = minus(e, o)
            if 0 < place < 8:
                o_ref[pl.ds(16 - place, NX, stride=NZ), :] = plus(e, o)


def table_product(v, t_ref):
    both = dot(jnp.concatenate(halves(v), axis=1), t_ref[...])
    return both[:, :128] + both[:, 128:]


def store_table(t_ref, table):
    high, low = halves(table)
    t_ref[0:128, 0:128] = high
    t_ref[128:256, 0:128] = high
    t_ref[0:128, 128:256] = low
    t_ref[128:256, 128:256] = jnp.zeros((128, 128), bf16)


def roll_up(v):
    return pltpu.roll(v, ROWS - 1, axis=0)


def roll_down(v):
    return pltpu.roll(v, 1, axis=0)


def wall_apply(s, q, planes, g):
    parts = [g * p for p in planes] + [g * roll_up(planes[0])]
    n = q + 1
    half = n // 2
    even = [parts[l] + parts[q - l] for l in range(half)]
    odd = [parts[l] - parts[q - l] for l in range(half)]
    out = [None] * n
    for k in range(half):
        p = m = None
        for l in range(half):
            ce = 0.5 * (s[k, l] + s[k, q - l])
            co = 0.5 * (s[k, l] - s[k, q - l])
            te, to = float(ce) * even[l], float(co) * odd[l]
            p = te if p is None else p + te
            m = to if m is None else m + to
        out[k] = p + m
        out[q - k] = p - m
    out[0] = out[0] + roll_down(out[q])
    return out[:q]


def weighted_sum(coefs, planes):
    total = None
    for c, v in zip(coefs, planes):
        c = float(c)
        if c == 0.0:
            continue
        t = v if c == 1.0 else c * v
        total = t if total is None else total + t
    return total


def restrict_wall(j, fine, coarse, planes):
    out = [weighted_sum(j[:fine, c], planes) for c in range(coarse)]
    out[0] = out[0] + roll_down(weighted_sum(j[:fine, coarse], planes))
    return out


def prolong_wall(j, fine, coarse, planes):
    closed = list(planes) + [roll_up(planes[0])]
    return [weighted_sum(j[k], closed) for k in range(fine)]


def cycle_kernel(
    h_ref, mats_ref, in_ref, out_ref,
    w_ref, geo_ref,
    u7, r7, x7, d7, u3, r3, x3, d3,
    square, g7_ref, g3_ref, r7_ref, p7_ref, r3_ref, p3_ref,
):
    n = lax.axis_index("gx") % 4 * 8 + lax.axis_index("gz")
    b = lax.axis_index("gx") // 4
    at_x = PHASES_AT + 2 * n + jnp.where(b > 0, 64, 0)
    at_z = PHASES_AT + 128 + 2 * jnp.where(b > 0, b, n // 16 * 8)
    cx, sx = mats_ref[pl.ds(at_x, 1), :], mats_ref[pl.ds(at_x + 1, 1), :]
    cz, sz = mats_ref[pl.ds(at_z, 1), :], mats_ref[pl.ds(at_z + 1, 1), :]
    cosines = (cx, cz, cx * cz - sx * sz)
    sines = (sx, sz, sx * cz + cx * sz)
    lane = lax.broadcasted_iota(jnp.int32, (1, 128), 1)
    first = lane < 64
    mass7, inv7, ratio7, mask7 = (mats_ref[n : n + 1, :] for n in range(LANES_AT, LANES_AT + 4))
    mass3, inv3, ratio3, mask3 = (mats_ref[n : n + 1, :] for n in range(LANES_AT + 4, LANES_AT + 8))
    mask1 = mats_ref[LANES_AT + 8 : LANES_AT + 9, :]

    upper = [jnp.where(first, c, s) for c, s in zip(cosines, sines)]
    lower = [jnp.where(first, -s, c) for c, s in zip(cosines, sines)]

    def mode_table(at, rows, phases):
        top = mats_ref[at : at + rows]
        low = pltpu.roll(top, 64, axis=1)
        for n in range(phases):
            at += rows
            t = mats_ref[at : at + rows]
            top = top + upper[n] * t
            low = low + lower[n] * pltpu.roll(t, 64, axis=1)
        if rows == 64:
            return jnp.concatenate([top, low], axis=0)
        square[...] = jnp.zeros((128, 128), f32)
        square[0:rows] = top
        square[64 : 64 + rows] = low
        return square[...]

    store_table(g7_ref, mode_table(G7_AT, 64, 2))
    store_table(g3_ref, mode_table(G3_AT, 24, 2))
    table = mode_table(P7_AT, 24, 3)
    store_table(p7_ref, table)
    store_table(r7_ref, (table * mass7).T * inv3)
    table = mode_table(P3_AT, 8, 3)
    store_table(p3_ref, table)
    store_table(r3_ref, (table * mass3).T)

    re = in_ref[pl.ds(0, 256, stride=2), :]
    im = in_ref[pl.ds(1, 256, stride=2), :]
    w_ref[0:256, :] = jnp.where(first, re, pltpu.roll(im, 64, axis=1)) * inv7
    w_ref[256:512, :] = jnp.where(first, pltpu.roll(re, 64, axis=1), im) * inv7
    w_ref[512:, :] = jnp.zeros((w_ref.shape[0] - 512, 128), f32)
    for k in range(7):
        r7[k] = float(1.0 / FINE.weight[k]) * w_ref[pl.ds(k, ROWS, stride=7), :]

    h = h_ref[...]
    row = lax.broadcasted_iota(jnp.int32, (ROWS, 128), 0)
    g = jnp.where(row < NY, 2.0 / jnp.where(row < NY, h, 1.0), 0.0)
    h_pair = h + roll_down(h)
    g_pair = g + roll_down(g)
    geo_ref[0] = h
    geo_ref[1] = g
    geo_ref[2] = h_pair

    def height(k):
        return geo_ref[0 if k else 2]

    def inverse_diag(level, ratio, mask, k):
        d = height(k) * ratio + float(level.stiff[k, k]) * (g if k else g_pair)
        return jnp.where(d > 0.0, mask / jnp.where(d > 0.0, d, 1.0), 0.0)

    for k in range(7):
        d7[k] = inverse_diag(FINE, ratio7, mask7, k)
    for k in range(3):
        d3[k] = inverse_diag(MID, ratio3, mask3, k)
    d1_mix = ((4.0 + screen_shift) - 2.0 * cx - 2.0 * cz) * mask1
    d1 = inverse_diag(LOW, 4.0 + screen_shift, mask1, 0)

    def apply(level, u, table):
        q = level.q
        m = table_product(u[...].reshape(q * ROWS, 128), table)
        wall = wall_apply(level.stiff, q, [u[k] for k in range(q)], geo_ref[1])
        return [height(k) * m[k * ROWS : (k + 1) * ROWS] + wall[k] for k in range(q)]

    def smooth(level, u, r, x, d, table, fresh, keep_residual):
        q = level.q
        start, steps = cheb_steps(level.bound, SMOOTH_STEPS, smooth_floor)
        for k in range(q):
            t = start * (d[k] * r[k])
            u[k] = t
            x[k] = t if fresh else x[k] + t
        for alpha, beta in steps:
            au = apply(level, u, table)
            for k in range(q):
                t = r[k] - au[k]
                r[k] = t
                t = alpha * u[k] + beta * (d[k] * t)
                u[k] = t
                x[k] = x[k] + t
        if keep_residual:
            au = apply(level, u, table)
            for k in range(q):
                r[k] = r[k] - au[k]

    def product(planes, table):
        m = table_product(jnp.concatenate(planes, axis=0), table)
        return [m[k * ROWS : (k + 1) * ROWS] for k in range(len(planes))]

    smooth(FINE, u7, r7, x7, d7, g7_ref, True, True)
    down = product(restrict_wall(R7, 7, 3, [r7[k] for k in range(7)]), r7_ref)
    for k in range(3):
        r3[k] = down[k]

    smooth(MID, u3, r3, x3, d3, g3_ref, True, True)
    r1 = product(restrict_wall(R3, 3, 1, [r3[k] for k in range(3)]), r3_ref)[0]

    start, steps = cheb_steps(LOW.bound, COARSE_STEPS, coarse_floor)
    my1 = height(0) * d1_mix
    u1 = start * (d1 * r1)
    x1 = u1
    for alpha, beta in steps:
        flow = g * (u1 - roll_up(u1))
        r1 = r1 - (my1 * u1 + (flow - roll_down(flow)))
        u1 = alpha * u1 + beta * (d1 * r1)
        x1 = x1 + u1

    up = prolong_wall(J3, 3, 1, product([x1], p3_ref))
    for k in range(3):
        u3[k] = up[k]
        x3[k] = x3[k] + up[k]
    au = apply(MID, u3, g3_ref)
    for k in range(3):
        r3[k] = r3[k] - au[k]
    smooth(MID, u3, r3, x3, d3, g3_ref, False, False)

    up = prolong_wall(J7, 7, 3, product([x3[k] for k in range(3)], p7_ref))
    for k in range(7):
        u7[k] = up[k]
        x7[k] = x7[k] + up[k]
    au = apply(FINE, u7, g7_ref)
    for k in range(7):
        r7[k] = r7[k] - au[k]
    smooth(FINE, u7, r7, x7, d7, g7_ref, False, False)

    for k in range(7):
        w_ref[pl.ds(k, ROWS, stride=7), :] = x7[k]
    top = w_ref[0:256, :]
    low = w_ref[256:512, :]
    out_ref[pl.ds(0, 256, stride=2), :] = jnp.where(first, top, pltpu.roll(low, 64, axis=1))
    out_ref[pl.ds(1, 256, stride=2), :] = jnp.where(first, pltpu.roll(top, 64, axis=1), low)


VMEM = pl.BlockSpec(memory_space=pltpu.VMEM)
PARAMS = pltpu.CompilerParams(vmem_limit_bytes=32 * 1024 * 1024)
FLAT = jax.ShapeDtypeStruct((512, 128), f32)


def exchange(block):
    moved = lax.all_to_all(block.reshape(DEVICES, 2, 128), ("gx", "gz"), 0, 0)
    return moved.reshape(512, 128)


def cycle_call(heights, modes):
    fine = pltpu.VMEM((7, ROWS, 128), f32)
    mid = pltpu.VMEM((3, ROWS, 128), f32)
    table = pltpu.VMEM((256, 256), bf16)
    return pl.pallas_call(
        cycle_kernel, out_shape=FLAT,
        in_specs=[VMEM, VMEM, VMEM], out_specs=VMEM,
        scratch_shapes=[
            pltpu.VMEM((7 * ROWS, 128), f32), mid,
            fine, fine, fine, fine, mid, mid, mid, mid,
            pltpu.VMEM((128, 128), f32), table, table, table, table, table, table,
        ],
        compiler_params=PARAMS,
    )(
        heights, jnp.asarray(MATRICES), modes,
    )


def transform(kernel, table, block):
    return pl.pallas_call(
        kernel, out_shape=FLAT, in_specs=[VMEM, VMEM], out_specs=VMEM, compiler_params=PARAMS
    )(jnp.asarray(split_terms(table)), block)


def body(residual, layer_heights):
    packed, heights = pl.pallas_call(
        pack_kernel, out_shape=(FLAT, jax.ShapeDtypeStruct((ROWS, 128), f32)),
        in_specs=[VMEM, VMEM], out_specs=(VMEM, VMEM),
        scratch_shapes=[pltpu.VMEM((256, 256), f32), pltpu.VMEM((8, 128), f32)],
        compiler_params=PARAMS,
    )(residual, layer_heights.reshape(1, NY))
    modes = exchange(transform(forward_kernel, FORWARD, exchange(packed)))
    solved = cycle_call(heights, modes)
    spread = exchange(transform(backward_kernel, BACKWARD, exchange(solved)))
    return pl.pallas_call(
        unpack_kernel, out_shape=jax.ShapeDtypeStruct((7, 14, 512), f32),
        in_specs=[VMEM], out_specs=VMEM, compiler_params=PARAMS,
    )(spread)


def solution(mesh):
    return jax.shard_map(
        body,
        mesh=mesh,
        in_specs=(P("gx", "gz", None), P()),
        out_specs=P("gx", "gz", None),
        check_vma=False,
    )
```

```python
import jax
import jax.numpy as jnp
import ml_dtypes
import numpy as np
from jax import lax
from jax.experimental import pallas as pl
from jax.experimental.pallas import tpu as pltpu
from jax.sharding import Mesh
from jax.sharding import PartitionSpec as P


SMOOTH_STEPS = 3
COARSE_STEPS = 12
NX, NZ, NY = 32, 16, 73
DEVICES = 256
ROWS = 80
screen_shift = 0.02
smooth_floor = 0.1
coarse_floor = 0.01
f32 = jnp.float32
bf16 = jnp.bfloat16


def legendre_values(points, degree):
    columns = [np.ones(points.shape), points]
    for n in range(2, degree + 1):
        columns.append(((2 * n - 1) * points * columns[-1] - (n - 1) * columns[-2]) / n)
    return np.stack(columns[: degree + 1], axis=1)


def gll_tables(degree):
    nodes = -np.cos(np.pi * np.arange(degree + 1) / degree)
    for _ in range(100):
        values = legendre_values(nodes, degree)
        nodes = nodes - (nodes * values[:, degree] - values[:, degree - 1]) / (
            (degree + 1) * values[:, degree]
        )
    leading = legendre_values(nodes, degree)[:, degree]
    weights = 2.0 / (degree * (degree + 1) * leading**2)
    differ = np.zeros((degree + 1, degree + 1))
    for i in range(degree + 1):
        for j in range(degree + 1):
            if i != j:
                differ[i, j] = leading[i] / (leading[j] * (nodes[i] - nodes[j]))
    differ[0, 0] = -degree * (degree + 1) / 4.0
    differ[degree, degree] = degree * (degree + 1) / 4.0
    return nodes, weights, differ.T @ (weights[:, None] * differ)


def interp_table(fine_degree, coarse_degree):
    fine_nodes = gll_tables(fine_degree)[0]
    coarse_nodes = gll_tables(coarse_degree)[0]
    lagrange = np.ones((fine_degree + 1, coarse_degree + 1))
    for col in range(coarse_degree + 1):
        for other in range(coarse_degree + 1):
            if other != col:
                lagrange[:, col] *= (fine_nodes - coarse_nodes[other]) / (
                    coarse_nodes[col] - coarse_nodes[other]
                )
    return lagrange


def lanes_of(values):
    n = values.shape[0]
    out = np.zeros((7, 7))
    out[:n, :n] = values
    return np.pad(out.reshape(49), (0, 15))


def square_of(matrix, n_out, n_in):
    out = np.zeros((7, 7, 7, 7))
    out[:n_out, :n_out, :n_in, :n_in] = matrix.reshape(n_out, n_out, n_in, n_in)
    return np.pad(out.reshape(49, 49), ((0, 15), (0, 15)))


class Level:
    def __init__(self, q):
        self.q = q
        _, w, s = gll_tables(q)
        self.w, self.s = w, s
        mass = 0.5 * w[:q].copy()
        mass[0] = 0.5 * (w[0] + w[q])
        diag = 2.0 * np.diag(s)[:q].copy()
        diag[0] = 2.0 * (s[0, 0] + s[q, q])
        self.mxz = np.outer(mass, mass)
        a = np.outer(diag, mass) + np.outer(mass, diag) + screen_shift * self.mxz
        self.ratio = lanes_of(a / self.mxz)
        spread = np.abs(s).sum(axis=1)
        self.bound = max(1.0, float(np.max(spread / np.diag(s))))
        base = 2.0 * s[:q, :q].copy()
        base[0, 0] += 2.0 * s[q, q]
        e1 = np.zeros((q, q))
        e1[:, 0] = 2.0 * s[:q, q]
        even, odd = e1 + e1.T, e1 - e1.T
        dm = np.diag(mass)
        scale = np.concatenate([lanes_of(1.0 / self.mxz)] * 2)[None, :]
        sq = lambda m: square_of(m, q, q)
        fixed = sq(np.kron(base, dm) + np.kron(dm, base) + screen_shift * np.kron(dm, dm))
        tables = [np.hstack([fixed, 0.0 * fixed])]
        for c, n in (
            (np.kron(even, dm), np.kron(odd, dm)),
            (np.kron(dm, even), np.kron(dm, odd)),
        ):
            tables.append(np.hstack([sq(c), -sq(n)]))
        self.tables = [(t * scale)[: 64 if q > 3 else 24] for t in tables]
        self.weight = 0.5 * w
        self.stiff = s / self.weight[:, None]
        self.mass_lanes = np.concatenate([lanes_of(self.mxz)] * 2)
        self.inv_mass_lanes = np.concatenate([lanes_of(1.0 / self.mxz)] * 2)
        self.ratio_lanes = np.concatenate([self.ratio] * 2)
        self.mask_lanes = (self.mass_lanes > 0).astype(np.float64)


def transfer_tables(fine, coarse):
    j = interp_table(fine, coarse)
    ja = j[:fine, :coarse]
    jb = np.zeros((fine, coarse))
    jb[:, 0] = j[:fine, coarse]
    tables = []
    for n, b in enumerate((np.kron(ja, ja), np.kron(jb, ja), np.kron(ja, jb), np.kron(jb, jb))):
        b = square_of(b, fine, coarse).T[: 24 if coarse > 1 else 8]
        tables.append(np.hstack([b, b if n else 0.0 * b]))
    return j, tables


def phase_rows():
    rows = np.zeros((152, 2, 64))
    for n in range(NX):
        t = 2 * np.pi * n / NX
        rows[64 + 2 * n], rows[65 + 2 * n] = np.cos(t), np.sin(t)
        k = n % 16
        t = 2 * np.pi * k / NX
        if k:
            rows[2 * n], rows[2 * n + 1] = np.cos(t), np.sin(t)
        else:
            rows[2 * n, 0], rows[2 * n, 1] = 1.0, -1.0
    for k in range(9):
        t = 2 * np.pi * k / NZ
        rows[128 + 2 * k], rows[129 + 2 * k] = np.cos(t), np.sin(t) if k % 8 else 0.0
    return rows.reshape(152, 128)


FINE, MID, LOW = Level(7), Level(3), Level(1)
J7, P7_TABLES = transfer_tables(7, 3)
J3, P3_TABLES = transfer_tables(3, 1)
MATRICES = np.concatenate(FINE.tables + MID.tables + P7_TABLES + P3_TABLES).astype(np.float32)
R7 = FINE.weight[:, None] * J7 / MID.weight
R3 = MID.weight[:, None] * J3 / LOW.weight
G7_AT, G3_AT, P7_AT, P3_AT = 0, 192, 264, 360


LANES = np.zeros((16, 128))
for n, level in enumerate((FINE, MID)):
    LANES[4 * n] = level.mass_lanes
    LANES[4 * n + 1] = level.inv_mass_lanes
    LANES[4 * n + 2] = level.ratio_lanes
    LANES[4 * n + 3] = level.mask_lanes
LANES[8] = LOW.mask_lanes
MATRICES = np.concatenate([MATRICES, LANES, phase_rows()]).astype(np.float32)
LANES_AT, PHASES_AT = 392, 408


def cheb_steps(bound, sweeps, floor):
    centre = bound * (1.0 + floor) / 2.0
    half = bound * (1.0 - floor) / 2.0
    s = centre / half
    p = 1.0 / s
    steps = []
    for _ in range(sweeps - 1):
        p_next = 1.0 / (2.0 * s - p)
        steps.append((p_next * p, 2.0 * p_next / half))
        p = p_next
    return 1.0 / centre, steps


SLAB = 13
FIELD = 32 * SLAB
USED = 8 * 49


def swap(v):
    return pltpu.roll(v, 64, axis=1)


def mix(first, v, w):
    return jnp.where(first, v, swap(w)), jnp.where(first, swap(v), w)


def pack_kernel(x_ref, h_ref, o_ref, rows_ref, line_ref):
    first, _ = lane_tools()
    o_ref[USED:, :] = jnp.zeros((FIELD - USED, 128), f32)
    for a in range(7):
        for t in range(4):
            part = slice(128 * t, 128 * t + 128)
            low, high = mix(first, x_ref[a, 0:7, part], x_ref[a, 7:14, part])
            r = 98 * t + 7 * a
            o_ref[r : r + 7, :] = low
            o_ref[r + 49 : r + 56, :] = high
    line_ref[...] = jnp.zeros_like(line_ref)
    line_ref[0:1, 0:NY] = h_ref[...]
    rows_ref[...] = jnp.broadcast_to(line_ref[0:1, :], (128, 128)).T[:ROWS]


def unpack_kernel(x_ref, o_ref):
    first, _ = lane_tools()
    for a in range(7):
        for t in range(4):
            part = slice(128 * t, 128 * t + 128)
            r = 98 * t + 7 * a
            low, high = mix(first, x_ref[r : r + 7, :], x_ref[r + 49 : r + 56, :])
            o_ref[a, 0:7, part] = low
            o_ref[a, 7:14, part] = high


def halves(v):
    high = v.astype(bf16)
    return high, (v - high.astype(f32)).astype(bf16)


def dot(a, b):
    return jnp.dot(a, b, preferred_element_type=f32)


HALF = float(np.sqrt(0.5))


def lane_tools():
    first = lax.broadcasted_iota(jnp.int32, (1, 128), 1) < 64
    return first, jnp.where(first, 1.0, -1.0).astype(f32)


def plane(ref, n):
    return ref[n * SLAB : n * SLAB + SLAB, :]


def put(ref, n, v):
    ref[n * SLAB : n * SLAB + SLAB, :] = v


def span_forward_kernel(x_ref, o_ref):
    first, sign = lane_tools()
    for r in range(4):
        x = [plane(x_ref, 8 * r + j) for j in range(8)]
        s = [None] + [x[j] + x[8 - j] for j in (1, 2, 3)]
        d = [None] + [x[j] - x[8 - j] for j in (1, 2, 3)]
        up, down = x[0] + x[4], x[0] - x[4]
        odd, turn = s[1] + s[3], HALF * (s[1] - s[3])
        slope = HALF * (d[1] + d[3])
        re = [up + s[2] + odd, down + turn, up - s[2], down - turn, up + s[2] - odd]
        im = [None, -slope - d[2], d[3] - d[1], d[2] - slope]
        flip = swap(re[0])
        put(o_ref, r, jnp.where(first, re[0] + flip, flip - re[0]))
        put(o_ref, 16 + r, sign * re[4])
        for f in (1, 2, 3):
            c, t = float(np.cos(np.pi * f / 8)), float(np.sin(np.pi * f / 8))
            re_swap, im_swap = swap(re[f]), swap(im[f])
            base = jnp.where(first, re[f], im_swap)
            extra = c * jnp.where(first, re_swap, im[f]) + t * jnp.where(first, im_swap, -re[f])
            put(o_ref, 4 * f + r, base + extra)
            put(o_ref, 4 * (8 - f) + r, sign * (base - extra))


def span_backward_kernel(x_ref, o_ref):
    first, sign = lane_tools()
    for r in range(4):
        v = [plane(x_ref, 4 * k + r) for k in range(8)]
        flip = swap(v[0])
        re = [jnp.where(first, v[0] + flip, flip - v[0])]
        im = [None]
        for f in (1, 2, 3):
            c, t = float(np.cos(np.pi * f / 8)), float(np.sin(np.pi * f / 8))
            total, other = v[f] + v[8 - f], swap(v[f] - v[8 - f])
            re.append(2.0 * jnp.where(first, total, c * other - t * total))
            im.append(2.0 * jnp.where(first, other, t * other + c * total))
        re.append((2.0 * sign) * v[4])
        up, down = re[0] + re[4], re[0] - re[4]
        odd, turn = re[1] + re[3], HALF * (re[1] - re[3])
        slope = HALF * (im[1] + im[3])
        c = [up + re[2] + odd, down + turn, up - re[2], down - turn, up + re[2] - odd]
        s = [None, slope + im[2], im[1] - im[3], slope - im[2]]
        put(o_ref, 8 * r, c[0])
        put(o_ref, 8 * r + 4, c[4])
        for j in (1, 2, 3):
            put(o_ref, 8 * r + j, c[j] - s[j])
            put(o_ref, 8 * r + 8 - j, c[j] + s[j])


def complex_transform(x, sign, direction):
    n = len(x)
    if n == 1:
        return x
    even = complex_transform(x[0::2], sign, direction)
    odd = complex_transform(x[1::2], sign, direction)
    low, high = [], []
    for k in range(n // 2):
        c = float(np.cos(2 * np.pi * k / n))
        s = direction * float(np.sin(2 * np.pi * k / n))
        if k == 0:
            t = odd[k]
        elif 4 * k == n:
            t = (s * sign) * swap(odd[k])
        else:
            t = c * odd[k] + (s * sign) * swap(odd[k])
        low.append(even[k] + t)
        high.append(even[k] - t)
    return low + high


def flow_forward_kernel(x_ref, o_ref):
    first, sign = lane_tools()
    for n, v in enumerate(complex_transform([plane(x_ref, n) for n in range(NX)], sign, 1.0)):
        put(o_ref, n, v)

    @pl.when(lax.axis_index("z") == 0)
    def _():
        w = [plane(o_ref, n) for n in range(NX)]
        put(o_ref, 0, jnp.where(first, w[0], swap(w[16])))
        put(o_ref, 16, jnp.where(first, swap(w[0]), w[16]))
        for n in range(1, 16):
            total, differ = w[n] + w[NX - n], w[n] - w[NX - n]
            put(o_ref, n, 0.5 * jnp.where(first, total, differ))
            put(o_ref, 16 + n, 0.5 * swap(jnp.where(first, -differ, total)))


def flow_backward_kernel(x_ref, o_ref, w_ref):
    first, sign = lane_tools()

    @pl.when(lax.axis_index("z") == 0)
    def _():
        v = [plane(x_ref, n) for n in range(NX)]
        put(w_ref, 0, jnp.where(first, v[0], swap(v[16])))
        put(w_ref, 16, jnp.where(first, swap(v[0]), v[16]))
        for n in range(1, 16):
            other = swap(v[16 + n])
            put(w_ref, n, v[n] - sign * other)
            put(w_ref, NX - n, sign * v[n] + other)

    @pl.when(lax.axis_index("z") > 0)
    def _():
        w_ref[...] = x_ref[...]

    for n, v in enumerate(complex_transform([plane(w_ref, n) for n in range(NX)], sign, -1.0)):
        put(o_ref, n, v)


def table_product(v, t_ref):
    both = dot(jnp.concatenate(halves(v), axis=1), t_ref[...])
    return both[:, :128] + both[:, 128:]


def store_table(t_ref, table):
    high, low = halves(table)
    t_ref[0:128, 0:128] = high
    t_ref[128:256, 0:128] = high
    t_ref[0:128, 128:256] = low
    t_ref[128:256, 128:256] = jnp.zeros((128, 128), bf16)


def roll_up(v):
    return pltpu.roll(v, ROWS - 1, axis=0)


def roll_down(v):
    return pltpu.roll(v, 1, axis=0)


def wall_apply(s, q, planes, g):
    parts = [g * p for p in planes] + [g * roll_up(planes[0])]
    n = q + 1
    half = n // 2
    even = [parts[l] + parts[q - l] for l in range(half)]
    odd = [parts[l] - parts[q - l] for l in range(half)]
    out = [None] * n
    for k in range(half):
        p = m = None
        for l in range(half):
            ce = 0.5 * (s[k, l] + s[k, q - l])
            co = 0.5 * (s[k, l] - s[k, q - l])
            te, to = float(ce) * even[l], float(co) * odd[l]
            p = te if p is None else p + te
            m = to if m is None else m + to
        out[k] = p + m
        out[q - k] = p - m
    out[0] = out[0] + roll_down(out[q])
    return out[:q]


def weighted_sum(coefs, planes):
    total = None
    for c, v in zip(coefs, planes):
        c = float(c)
        if c == 0.0:
            continue
        t = v if c == 1.0 else c * v
        total = t if total is None else total + t
    return total


def restrict_wall(j, fine, coarse, planes):
    out = [weighted_sum(j[:fine, c], planes) for c in range(coarse)]
    out[0] = out[0] + roll_down(weighted_sum(j[:fine, coarse], planes))
    return out


def prolong_wall(j, fine, coarse, planes):
    closed = list(planes) + [roll_up(planes[0])]
    return [weighted_sum(j[k], closed) for k in range(fine)]


def cycle_kernel(
    h_ref, mats_ref, in_ref, out_ref,
    w_ref, geo_ref,
    u7, r7, x7, d7, u3, r3, x3, d3,
    square, g7_ref, g3_ref, r7_ref, p7_ref, r3_ref, p3_ref,
):
    n = lax.axis_index("r") * 8 + lax.axis_index("gz")
    b = lax.axis_index("z")
    at_x = PHASES_AT + 2 * n + jnp.where(b > 0, 64, 0)
    at_z = PHASES_AT + 128 + 2 * jnp.where(b > 0, b, n // 16 * 8)
    cx, sx = mats_ref[pl.ds(at_x, 1), :], mats_ref[pl.ds(at_x + 1, 1), :]
    cz, sz = mats_ref[pl.ds(at_z, 1), :], mats_ref[pl.ds(at_z + 1, 1), :]
    cosines = (cx, cz, cx * cz - sx * sz)
    sines = (sx, sz, sx * cz + cx * sz)
    lane = lax.broadcasted_iota(jnp.int32, (1, 128), 1)
    first = lane < 64
    mass7, inv7, ratio7, mask7 = (mats_ref[n : n + 1, :] for n in range(LANES_AT, LANES_AT + 4))
    mass3, inv3, ratio3, mask3 = (mats_ref[n : n + 1, :] for n in range(LANES_AT + 4, LANES_AT + 8))
    mask1 = mats_ref[LANES_AT + 8 : LANES_AT + 9, :]

    upper = [jnp.where(first, c, s) for c, s in zip(cosines, sines)]
    lower = [jnp.where(first, -s, c) for c, s in zip(cosines, sines)]

    def mode_table(at, rows, phases):
        top = mats_ref[at : at + rows]
        low = pltpu.roll(top, 64, axis=1)
        for n in range(phases):
            at += rows
            t = mats_ref[at : at + rows]
            top = top + upper[n] * t
            low = low + lower[n] * pltpu.roll(t, 64, axis=1)
        if rows == 64:
            return jnp.concatenate([top, low], axis=0)
        square[...] = jnp.zeros((128, 128), f32)
        square[0:rows] = top
        square[64 : 64 + rows] = low
        return square[...]

    store_table(g7_ref, mode_table(G7_AT, 64, 2))
    store_table(g3_ref, mode_table(G3_AT, 24, 2))
    table = mode_table(P7_AT, 24, 3)
    store_table(p7_ref, table)
    store_table(r7_ref, (table * mass7).T * inv3)
    table = mode_table(P3_AT, 8, 3)
    store_table(p3_ref, table)
    store_table(r3_ref, (table * mass3).T)

    scale = inv7 * (1.0 / (NX * NZ))
    for t in range(4):
        r = 98 * t
        both = jnp.concatenate([in_ref[r : r + 64, :], in_ref[r + 49 : r + 113, :]], axis=0).T
        low, high = mix(first, both[:64], both[64:])
        w_ref[128 * t : 128 * t + 64, :] = low * scale
        w_ref[128 * t + 64 : 128 * t + 128, :] = high * scale
    w_ref[512:, :] = jnp.zeros((w_ref.shape[0] - 512, 128), f32)
    for k in range(7):
        r7[k] = float(1.0 / FINE.weight[k]) * w_ref[pl.ds(k, ROWS, stride=7), :]

    h = h_ref[...]
    row = lax.broadcasted_iota(jnp.int32, (ROWS, 128), 0)
    g = jnp.where(row < NY, 2.0 / jnp.where(row < NY, h, 1.0), 0.0)
    h_pair = h + roll_down(h)
    g_pair = g + roll_down(g)
    geo_ref[0] = h
    geo_ref[1] = g
    geo_ref[2] = h_pair

    def height(k):
        return geo_ref[0 if k else 2]

    def inverse_diag(level, ratio, mask, k):
        d = height(k) * ratio + float(level.stiff[k, k]) * (g if k else g_pair)
        return jnp.where(d > 0.0, mask / jnp.where(d > 0.0, d, 1.0), 0.0)

    for k in range(7):
        d7[k] = inverse_diag(FINE, ratio7, mask7, k)
    for k in range(3):
        d3[k] = inverse_diag(MID, ratio3, mask3, k)
    d1_mix = ((4.0 + screen_shift) - 2.0 * cx - 2.0 * cz) * mask1
    d1 = inverse_diag(LOW, 4.0 + screen_shift, mask1, 0)

    def apply(level, u, table):
        q = level.q
        m = table_product(u[...].reshape(q * ROWS, 128), table)
        wall = wall_apply(level.stiff, q, [u[k] for k in range(q)], geo_ref[1])
        return [height(k) * m[k * ROWS : (k + 1) * ROWS] + wall[k] for k in range(q)]

    def smooth(level, u, r, x, d, table, fresh, keep_residual):
        q = level.q
        start, steps = cheb_steps(level.bound, SMOOTH_STEPS, smooth_floor)
        for k in range(q):
            t = start * (d[k] * r[k])
            u[k] = t
            x[k] = t if fresh else x[k] + t
        for alpha, beta in steps:
            au = apply(level, u, table)
            for k in range(q):
                t = r[k] - au[k]
                r[k] = t
                t = alpha * u[k] + beta * (d[k] * t)
                u[k] = t
                x[k] = x[k] + t
        if keep_residual:
            au = apply(level, u, table)
            for k in range(q):
                r[k] = r[k] - au[k]

    def product(planes, table):
        m = table_product(jnp.concatenate(planes, axis=0), table)
        return [m[k * ROWS : (k + 1) * ROWS] for k in range(len(planes))]

    smooth(FINE, u7, r7, x7, d7, g7_ref, True, True)
    down = product(restrict_wall(R7, 7, 3, [r7[k] for k in range(7)]), r7_ref)
    for k in range(3):
        r3[k] = down[k]

    smooth(MID, u3, r3, x3, d3, g3_ref, True, True)
    r1 = product(restrict_wall(R3, 3, 1, [r3[k] for k in range(3)]), r3_ref)[0]

    start, steps = cheb_steps(LOW.bound, COARSE_STEPS, coarse_floor)
    my1 = height(0) * d1_mix
    u1 = start * (d1 * r1)
    x1 = u1
    for alpha, beta in steps:
        flow = g * (u1 - roll_up(u1))
        r1 = r1 - (my1 * u1 + (flow - roll_down(flow)))
        u1 = alpha * u1 + beta * (d1 * r1)
        x1 = x1 + u1

    up = prolong_wall(J3, 3, 1, product([x1], p3_ref))
    for k in range(3):
        u3[k] = up[k]
        x3[k] = x3[k] + up[k]
    au = apply(MID, u3, g3_ref)
    for k in range(3):
        r3[k] = r3[k] - au[k]
    smooth(MID, u3, r3, x3, d3, g3_ref, False, False)

    up = prolong_wall(J7, 7, 3, product([x3[k] for k in range(3)], p7_ref))
    for k in range(7):
        u7[k] = up[k]
        x7[k] = x7[k] + up[k]
    au = apply(FINE, u7, g7_ref)
    for k in range(7):
        r7[k] = r7[k] - au[k]
    smooth(FINE, u7, r7, x7, d7, g7_ref, False, False)

    for k in range(7):
        w_ref[pl.ds(k, ROWS, stride=7), :] = x7[k]
    for t in range(4):
        r = 98 * t
        both = jnp.concatenate(
            mix(first, w_ref[128 * t : 128 * t + 64, :], w_ref[128 * t + 64 : 128 * t + 128, :]), axis=0
        ).T
        out_ref[r : r + 49, :] = both[0:49]
        out_ref[r + 49 : r + 98, :] = both[64:113]
    out_ref[USED:, :] = jnp.zeros((FIELD - USED, 128), f32)


VMEM = pl.BlockSpec(memory_space=pltpu.VMEM)
PARAMS = pltpu.CompilerParams(vmem_limit_bytes=32 * 1024 * 1024)
FLAT = jax.ShapeDtypeStruct((FIELD, 128), f32)


def in_plane(block):
    block = block.reshape(32, SLAB, 1, 128)
    return lax.all_to_all(block, ("r", "gz"), 0, 0).reshape(FIELD, 128)


def along_z(block):
    block = block.reshape(8, 4 * SLAB, 1, 128)
    return lax.all_to_all(block, "z", 0, 0).reshape(FIELD, 128)


def cycle_call(heights, modes):
    fine = pltpu.VMEM((7, ROWS, 128), f32)
    mid = pltpu.VMEM((3, ROWS, 128), f32)
    table = pltpu.VMEM((256, 256), bf16)
    return pl.pallas_call(
        cycle_kernel, out_shape=FLAT,
        in_specs=[VMEM, VMEM, VMEM], out_specs=VMEM,
        scratch_shapes=[
            pltpu.VMEM((7 * ROWS, 128), f32), mid,
            fine, fine, fine, fine, mid, mid, mid, mid,
            pltpu.VMEM((128, 128), f32), table, table, table, table, table, table,
        ],
        compiler_params=PARAMS,
    )(
        heights, jnp.asarray(MATRICES), modes,
    )


def transform(kernel, block, scratch=()):
    return pl.pallas_call(
        kernel, out_shape=FLAT, in_specs=[VMEM], out_specs=VMEM,
        scratch_shapes=scratch, compiler_params=PARAMS,
    )(block)


def body(residual, layer_heights):
    packed, heights = pl.pallas_call(
        pack_kernel, out_shape=(FLAT, jax.ShapeDtypeStruct((ROWS, 128), f32)),
        in_specs=[VMEM, VMEM], out_specs=(VMEM, VMEM),
        scratch_shapes=[pltpu.VMEM((8, 128), f32)],
        compiler_params=PARAMS,
    )(residual, layer_heights.reshape(1, NY))
    spans = transform(span_forward_kernel, in_plane(packed))
    modes = in_plane(transform(flow_forward_kernel, along_z(spans)))
    solved = cycle_call(heights, modes)
    flows = transform(flow_backward_kernel, in_plane(solved), [pltpu.VMEM((FIELD, 128), f32)])
    spread = in_plane(transform(span_backward_kernel, along_z(flows)))
    return pl.pallas_call(
        unpack_kernel, out_shape=jax.ShapeDtypeStruct((7, 14, 512), f32),
        in_specs=[VMEM], out_specs=VMEM, compiler_params=PARAMS,
    )(spread)


def solution(mesh):
    split = Mesh(mesh.devices.reshape(8, 4, 8), ("z", "r", "gz"))
    spec = P(("z", "r"), "gz", None)
    return jax.shard_map(
        body, mesh=split, in_specs=(spec, P()), out_specs=spec, check_vma=False
    )
```

```python
import jax
import jax.numpy as jnp
import ml_dtypes
import numpy as np
from jax import lax
from jax.experimental import pallas as pl
from jax.experimental.pallas import tpu as pltpu
from jax.sharding import Mesh
from jax.sharding import PartitionSpec as P


SMOOTH_STEPS = 3
COARSE_STEPS = 12
NX, NZ, NY = 32, 16, 73
DEVICES = 256
ROWS = 80
screen_shift = 0.02
smooth_floor = 0.1
coarse_floor = 0.01
f32 = jnp.float32
bf16 = jnp.bfloat16


def legendre_values(points, degree):
    columns = [np.ones(points.shape), points]
    for n in range(2, degree + 1):
        columns.append(((2 * n - 1) * points * columns[-1] - (n - 1) * columns[-2]) / n)
    return np.stack(columns[: degree + 1], axis=1)


def gll_tables(degree):
    nodes = -np.cos(np.pi * np.arange(degree + 1) / degree)
    for _ in range(100):
        values = legendre_values(nodes, degree)
        nodes = nodes - (nodes * values[:, degree] - values[:, degree - 1]) / (
            (degree + 1) * values[:, degree]
        )
    leading = legendre_values(nodes, degree)[:, degree]
    weights = 2.0 / (degree * (degree + 1) * leading**2)
    differ = np.zeros((degree + 1, degree + 1))
    for i in range(degree + 1):
        for j in range(degree + 1):
            if i != j:
                differ[i, j] = leading[i] / (leading[j] * (nodes[i] - nodes[j]))
    differ[0, 0] = -degree * (degree + 1) / 4.0
    differ[degree, degree] = degree * (degree + 1) / 4.0
    return nodes, weights, differ.T @ (weights[:, None] * differ)


def interp_table(fine_degree, coarse_degree):
    fine_nodes = gll_tables(fine_degree)[0]
    coarse_nodes = gll_tables(coarse_degree)[0]
    lagrange = np.ones((fine_degree + 1, coarse_degree + 1))
    for col in range(coarse_degree + 1):
        for other in range(coarse_degree + 1):
            if other != col:
                lagrange[:, col] *= (fine_nodes - coarse_nodes[other]) / (
                    coarse_nodes[col] - coarse_nodes[other]
                )
    return lagrange


def lanes_of(values):
    n = values.shape[0]
    out = np.zeros((7, 7))
    out[:n, :n] = values
    return np.pad(out.reshape(49), (0, 15))


def square_of(matrix, n_out, n_in):
    out = np.zeros((7, 7, 7, 7))
    out[:n_out, :n_out, :n_in, :n_in] = matrix.reshape(n_out, n_out, n_in, n_in)
    return np.pad(out.reshape(49, 49), ((0, 15), (0, 15)))


class Level:
    def __init__(self, q):
        self.q = q
        _, w, s = gll_tables(q)
        self.w, self.s = w, s
        mass = 0.5 * w[:q].copy()
        mass[0] = 0.5 * (w[0] + w[q])
        diag = 2.0 * np.diag(s)[:q].copy()
        diag[0] = 2.0 * (s[0, 0] + s[q, q])
        self.mxz = np.outer(mass, mass)
        a = np.outer(diag, mass) + np.outer(mass, diag) + screen_shift * self.mxz
        self.ratio = lanes_of(a / self.mxz)
        spread = np.abs(s).sum(axis=1)
        self.bound = max(1.0, float(np.max(spread / np.diag(s))))
        base = 2.0 * s[:q, :q].copy()
        base[0, 0] += 2.0 * s[q, q]
        e1 = np.zeros((q, q))
        e1[:, 0] = 2.0 * s[:q, q]
        even, odd = e1 + e1.T, e1 - e1.T
        dm = np.diag(mass)
        scale = np.concatenate([lanes_of(1.0 / self.mxz)] * 2)[None, :]
        sq = lambda m: square_of(m, q, q)
        fixed = sq(np.kron(base, dm) + np.kron(dm, base) + screen_shift * np.kron(dm, dm))
        tables = [np.hstack([fixed, 0.0 * fixed])]
        for c, n in (
            (np.kron(even, dm), np.kron(odd, dm)),
            (np.kron(dm, even), np.kron(dm, odd)),
        ):
            tables.append(np.hstack([sq(c), -sq(n)]))
        self.tables = [(t * scale)[: 64 if q > 3 else 24] for t in tables]
        self.weight = 0.5 * w
        self.stiff = s / self.weight[:, None]
        self.mass_lanes = np.concatenate([lanes_of(self.mxz)] * 2)
        self.inv_mass_lanes = np.concatenate([lanes_of(1.0 / self.mxz)] * 2)
        self.ratio_lanes = np.concatenate([self.ratio] * 2)
        self.mask_lanes = (self.mass_lanes > 0).astype(np.float64)


def transfer_tables(fine, coarse):
    j = interp_table(fine, coarse)
    ja = j[:fine, :coarse]
    jb = np.zeros((fine, coarse))
    jb[:, 0] = j[:fine, coarse]
    tables = []
    for n, b in enumerate((np.kron(ja, ja), np.kron(jb, ja), np.kron(ja, jb), np.kron(jb, jb))):
        b = square_of(b, fine, coarse).T[: 24 if coarse > 1 else 8]
        tables.append(np.hstack([b, b if n else 0.0 * b]))
    return j, tables


def phase_rows():
    rows = np.zeros((152, 2, 64))
    for n in range(NX):
        t = 2 * np.pi * n / NX
        rows[64 + 2 * n], rows[65 + 2 * n] = np.cos(t), np.sin(t)
        k = n % 16
        t = 2 * np.pi * k / NX
        if k:
            rows[2 * n], rows[2 * n + 1] = np.cos(t), np.sin(t)
        else:
            rows[2 * n, 0], rows[2 * n, 1] = 1.0, -1.0
    for k in range(9):
        t = 2 * np.pi * k / NZ
        rows[128 + 2 * k], rows[129 + 2 * k] = np.cos(t), np.sin(t) if k % 8 else 0.0
    return rows.reshape(152, 128)


FINE, MID, LOW = Level(7), Level(3), Level(1)
J7, P7_TABLES = transfer_tables(7, 3)
J3, P3_TABLES = transfer_tables(3, 1)
MATRICES = np.concatenate(FINE.tables + MID.tables + P7_TABLES + P3_TABLES).astype(np.float32)
R7 = FINE.weight[:, None] * J7 / MID.weight
R3 = MID.weight[:, None] * J3 / LOW.weight
G7_AT, G3_AT, P7_AT, P3_AT = 0, 192, 264, 360


LANES = np.zeros((16, 128))
for n, level in enumerate((FINE, MID)):
    LANES[4 * n] = level.mass_lanes
    LANES[4 * n + 1] = level.inv_mass_lanes
    LANES[4 * n + 2] = level.ratio_lanes
    LANES[4 * n + 3] = level.mask_lanes
LANES[8] = LOW.mask_lanes
MATRICES = np.concatenate([MATRICES, LANES, phase_rows()]).astype(np.float32)
LANES_AT, PHASES_AT = 392, 408


def cheb_steps(bound, sweeps, floor):
    centre = bound * (1.0 + floor) / 2.0
    half = bound * (1.0 - floor) / 2.0
    s = centre / half
    p = 1.0 / s
    steps = []
    for _ in range(sweeps - 1):
        p_next = 1.0 / (2.0 * s - p)
        steps.append((p_next * p, 2.0 * p_next / half))
        p = p_next
    return 1.0 / centre, steps


FLOW, SPAN = ("zh", "z0", "xh", "core"), ("xl", "y")
LAST = ("xl", "y", "z0", "core")
SLAB = 13
FIELD = 32 * SLAB
USED = 8 * 49


def swap(v):
    return pltpu.roll(v, 64, axis=1)


def mix(first, v, w):
    return jnp.where(first, v, swap(w)), jnp.where(first, swap(v), w)


def pack_kernel(x_ref, h_ref, o_ref, rows_ref, line_ref):
    first, _ = lane_tools()
    o_ref[USED:, :] = jnp.zeros((FIELD - USED, 128), f32)
    for a in range(7):
        for t in range(4):
            part = slice(128 * t, 128 * t + 128)
            low, high = mix(first, x_ref[a, 0:7, part], x_ref[a, 7:14, part])
            r = 98 * t + 7 * a
            o_ref[r : r + 7, :] = low
            o_ref[r + 49 : r + 56, :] = high
    line_ref[...] = jnp.zeros_like(line_ref)
    line_ref[0:1, 0:NY] = h_ref[...]
    rows_ref[...] = jnp.broadcast_to(line_ref[0:1, :], (128, 128)).T[:ROWS]


def unpack_kernel(x_ref, o_ref):
    first, _ = lane_tools()
    for a in range(7):
        for t in range(4):
            part = slice(128 * t, 128 * t + 128)
            r = 98 * t + 7 * a
            low, high = mix(first, x_ref[r : r + 7, :], x_ref[r + 49 : r + 56, :])
            o_ref[a, 0:7, part] = low
            o_ref[a, 7:14, part] = high


def halves(v):
    high = v.astype(bf16)
    return high, (v - high.astype(f32)).astype(bf16)


def dot(a, b):
    return jnp.dot(a, b, preferred_element_type=f32)


HALF = float(np.sqrt(0.5))


def lane_tools():
    first = lax.broadcasted_iota(jnp.int32, (1, 128), 1) < 64
    return first, jnp.where(first, 1.0, -1.0).astype(f32)


def plane(ref, n):
    return ref[n * SLAB : n * SLAB + SLAB, :]


def put(ref, n, v):
    ref[n * SLAB : n * SLAB + SLAB, :] = v


def span_mode():
    return lax.axis_index("zh") * 2 + lax.axis_index("xh")


def span_forward_kernel(x_ref, o_ref):
    first, sign = lane_tools()
    for z0, core in ((0, 0), (0, 1), (1, 0), (1, 1)):
        x = [plane(x_ref, 4 * j + 2 * z0 + core) for j in range(8)]
        at = [4 * (k // 2 * 2 + z0) + 2 * (k % 2) + core for k in range(8)]
        s = [None] + [x[j] + x[8 - j] for j in (1, 2, 3)]
        d = [None] + [x[j] - x[8 - j] for j in (1, 2, 3)]
        up, down = x[0] + x[4], x[0] - x[4]
        odd, turn = s[1] + s[3], HALF * (s[1] - s[3])
        slope = HALF * (d[1] + d[3])
        re = [up + s[2] + odd, down + turn, up - s[2], down - turn, up + s[2] - odd]
        im = [None, -slope - d[2], d[3] - d[1], d[2] - slope]
        flip = swap(re[0])
        put(o_ref, at[0], jnp.where(first, re[0] + flip, flip - re[0]))
        put(o_ref, at[4], sign * re[4])
        for f in (1, 2, 3):
            c, t = float(np.cos(np.pi * f / 8)), float(np.sin(np.pi * f / 8))
            re_swap, im_swap = swap(re[f]), swap(im[f])
            base = jnp.where(first, re[f], im_swap)
            extra = c * jnp.where(first, re_swap, im[f]) + t * jnp.where(first, im_swap, -re[f])
            put(o_ref, at[f], base + extra)
            put(o_ref, at[8 - f], sign * (base - extra))


def span_backward_kernel(x_ref, o_ref):
    first, sign = lane_tools()
    for z0, core in ((0, 0), (0, 1), (1, 0), (1, 1)):
        v = [plane(x_ref, 4 * (k // 2 * 2 + z0) + 2 * (k % 2) + core) for k in range(8)]
        flip = swap(v[0])
        re = [jnp.where(first, v[0] + flip, flip - v[0])]
        im = [None]
        for f in (1, 2, 3):
            c, t = float(np.cos(np.pi * f / 8)), float(np.sin(np.pi * f / 8))
            total, other = v[f] + v[8 - f], swap(v[f] - v[8 - f])
            re.append(2.0 * jnp.where(first, total, c * other - t * total))
            im.append(2.0 * jnp.where(first, other, t * other + c * total))
        re.append((2.0 * sign) * v[4])
        up, down = re[0] + re[4], re[0] - re[4]
        odd, turn = re[1] + re[3], HALF * (re[1] - re[3])
        slope = HALF * (im[1] + im[3])
        c = [up + re[2] + odd, down + turn, up - re[2], down - turn, up + re[2] - odd]
        s = [None, slope + im[2], im[1] - im[3], slope - im[2]]
        at = [4 * j + 2 * z0 + core for j in range(8)]
        put(o_ref, at[0], c[0])
        put(o_ref, at[4], c[4])
        for j in (1, 2, 3):
            put(o_ref, at[j], c[j] - s[j])
            put(o_ref, at[8 - j], c[j] + s[j])


def complex_transform(x, sign, direction):
    n = len(x)
    if n == 1:
        return x
    even = complex_transform(x[0::2], sign, direction)
    odd = complex_transform(x[1::2], sign, direction)
    low, high = [], []
    for k in range(n // 2):
        c = float(np.cos(2 * np.pi * k / n))
        s = direction * float(np.sin(2 * np.pi * k / n))
        if k == 0:
            t = odd[k]
        elif 4 * k == n:
            t = (s * sign) * swap(odd[k])
        else:
            t = c * odd[k] + (s * sign) * swap(odd[k])
        low.append(even[k] + t)
        high.append(even[k] - t)
    return low + high


def flow_forward_kernel(x_ref, o_ref):
    first, sign = lane_tools()
    for n, v in enumerate(complex_transform([plane(x_ref, n) for n in range(NX)], sign, 1.0)):
        put(o_ref, n, v)

    @pl.when(span_mode() == 0)
    def _():
        w = [plane(o_ref, n) for n in range(NX)]
        put(o_ref, 0, jnp.where(first, w[0], swap(w[16])))
        put(o_ref, 16, jnp.where(first, swap(w[0]), w[16]))
        for n in range(1, 16):
            total, differ = w[n] + w[NX - n], w[n] - w[NX - n]
            put(o_ref, n, 0.5 * jnp.where(first, total, differ))
            put(o_ref, 16 + n, 0.5 * swap(jnp.where(first, -differ, total)))


def flow_backward_kernel(x_ref, o_ref, w_ref):
    first, sign = lane_tools()

    @pl.when(span_mode() == 0)
    def _():
        v = [plane(x_ref, n) for n in range(NX)]
        put(w_ref, 0, jnp.where(first, v[0], swap(v[16])))
        put(w_ref, 16, jnp.where(first, swap(v[0]), v[16]))
        for n in range(1, 16):
            other = swap(v[16 + n])
            put(w_ref, n, v[n] - sign * other)
            put(w_ref, NX - n, sign * v[n] + other)

    @pl.when(span_mode() > 0)
    def _():
        w_ref[...] = x_ref[...]

    for n, v in enumerate(complex_transform([plane(w_ref, n) for n in range(NX)], sign, -1.0)):
        put(o_ref, n, v)


def table_product(v, t_ref):
    both = dot(jnp.concatenate(halves(v), axis=1), t_ref[...])
    return both[:, :128] + both[:, 128:]


def store_table(t_ref, table):
    high, low = halves(table)
    t_ref[0:128, 0:128] = high
    t_ref[128:256, 0:128] = high
    t_ref[0:128, 128:256] = low
    t_ref[128:256, 128:256] = jnp.zeros((128, 128), bf16)


def roll_up(v):
    return pltpu.roll(v, ROWS - 1, axis=0)


def roll_down(v):
    return pltpu.roll(v, 1, axis=0)


def wall_apply(s, q, planes, g):
    parts = [g * p for p in planes] + [g * roll_up(planes[0])]
    n = q + 1
    half = n // 2
    even = [parts[l] + parts[q - l] for l in range(half)]
    odd = [parts[l] - parts[q - l] for l in range(half)]
    out = [None] * n
    for k in range(half):
        p = m = None
        for l in range(half):
            ce = 0.5 * (s[k, l] + s[k, q - l])
            co = 0.5 * (s[k, l] - s[k, q - l])
            te, to = float(ce) * even[l], float(co) * odd[l]
            p = te if p is None else p + te
            m = to if m is None else m + to
        out[k] = p + m
        out[q - k] = p - m
    out[0] = out[0] + roll_down(out[q])
    return out[:q]


def weighted_sum(coefs, planes):
    total = None
    for c, v in zip(coefs, planes):
        c = float(c)
        if c == 0.0:
            continue
        t = v if c == 1.0 else c * v
        total = t if total is None else total + t
    return total


def restrict_wall(j, fine, coarse, planes):
    out = [weighted_sum(j[:fine, c], planes) for c in range(coarse)]
    out[0] = out[0] + roll_down(weighted_sum(j[:fine, coarse], planes))
    return out


def prolong_wall(j, fine, coarse, planes):
    closed = list(planes) + [roll_up(planes[0])]
    return [weighted_sum(j[k], closed) for k in range(fine)]


def cycle_kernel(
    h_ref, mats_ref, in_ref, out_ref,
    w_ref, geo_ref,
    u7, r7, x7, d7, u3, r3, x3, d3,
    square, g7_ref, g3_ref, r7_ref, p7_ref, r3_ref, p3_ref,
):
    n = lax.axis_index(LAST)
    b = span_mode()
    at_x = PHASES_AT + 2 * n + jnp.where(b > 0, 64, 0)
    at_z = PHASES_AT + 128 + 2 * jnp.where(b > 0, b, n // 16 * 8)
    cx, sx = mats_ref[pl.ds(at_x, 1), :], mats_ref[pl.ds(at_x + 1, 1), :]
    cz, sz = mats_ref[pl.ds(at_z, 1), :], mats_ref[pl.ds(at_z + 1, 1), :]
    cosines = (cx, cz, cx * cz - sx * sz)
    sines = (sx, sz, sx * cz + cx * sz)
    lane = lax.broadcasted_iota(jnp.int32, (1, 128), 1)
    first = lane < 64
    mass7, inv7, ratio7, mask7 = (mats_ref[n : n + 1, :] for n in range(LANES_AT, LANES_AT + 4))
    mass3, inv3, ratio3, mask3 = (mats_ref[n : n + 1, :] for n in range(LANES_AT + 4, LANES_AT + 8))
    mask1 = mats_ref[LANES_AT + 8 : LANES_AT + 9, :]

    upper = [jnp.where(first, c, s) for c, s in zip(cosines, sines)]
    lower = [jnp.where(first, -s, c) for c, s in zip(cosines, sines)]

    def mode_table(at, rows, phases):
        top = mats_ref[at : at + rows]
        low = pltpu.roll(top, 64, axis=1)
        for n in range(phases):
            at += rows
            t = mats_ref[at : at + rows]
            top = top + upper[n] * t
            low = low + lower[n] * pltpu.roll(t, 64, axis=1)
        if rows == 64:
            return jnp.concatenate([top, low], axis=0)
        square[...] = jnp.zeros((128, 128), f32)
        square[0:rows] = top
        square[64 : 64 + rows] = low
        return square[...]

    store_table(g7_ref, mode_table(G7_AT, 64, 2))
    store_table(g3_ref, mode_table(G3_AT, 24, 2))
    table = mode_table(P7_AT, 24, 3)
    store_table(p7_ref, table)
    store_table(r7_ref, (table * mass7).T * inv3)
    table = mode_table(P3_AT, 8, 3)
    store_table(p3_ref, table)
    store_table(r3_ref, (table * mass3).T)

    scale = inv7 * (1.0 / (NX * NZ))
    for t in range(4):
        r = 98 * t
        both = jnp.concatenate([in_ref[r : r + 64, :], in_ref[r + 49 : r + 113, :]], axis=0).T
        low, high = mix(first, both[:64], both[64:])
        w_ref[128 * t : 128 * t + 64, :] = low * scale
        w_ref[128 * t + 64 : 128 * t + 128, :] = high * scale
    w_ref[512:, :] = jnp.zeros((w_ref.shape[0] - 512, 128), f32)
    for k in range(7):
        r7[k] = float(1.0 / FINE.weight[k]) * w_ref[pl.ds(k, ROWS, stride=7), :]

    h = h_ref[...]
    row = lax.broadcasted_iota(jnp.int32, (ROWS, 128), 0)
    g = jnp.where(row < NY, 2.0 / jnp.where(row < NY, h, 1.0), 0.0)
    h_pair = h + roll_down(h)
    g_pair = g + roll_down(g)
    geo_ref[0] = h
    geo_ref[1] = g
    geo_ref[2] = h_pair

    def height(k):
        return geo_ref[0 if k else 2]

    def inverse_diag(level, ratio, mask, k):
        d = height(k) * ratio + float(level.stiff[k, k]) * (g if k else g_pair)
        return jnp.where(d > 0.0, mask / jnp.where(d > 0.0, d, 1.0), 0.0)

    for k in range(7):
        d7[k] = inverse_diag(FINE, ratio7, mask7, k)
    for k in range(3):
        d3[k] = inverse_diag(MID, ratio3, mask3, k)
    d1_mix = ((4.0 + screen_shift) - 2.0 * cx - 2.0 * cz) * mask1
    d1 = inverse_diag(LOW, 4.0 + screen_shift, mask1, 0)

    def apply(level, u, table):
        q = level.q
        m = table_product(u[...].reshape(q * ROWS, 128), table)
        wall = wall_apply(level.stiff, q, [u[k] for k in range(q)], geo_ref[1])
        return [height(k) * m[k * ROWS : (k + 1) * ROWS] + wall[k] for k in range(q)]

    def smooth(level, u, r, x, d, table, fresh, keep_residual):
        q = level.q
        start, steps = cheb_steps(level.bound, SMOOTH_STEPS, smooth_floor)
        for k in range(q):
            t = start * (d[k] * r[k])
            u[k] = t
            x[k] = t if fresh else x[k] + t
        for alpha, beta in steps:
            au = apply(level, u, table)
            for k in range(q):
                t = r[k] - au[k]
                r[k] = t
                t = alpha * u[k] + beta * (d[k] * t)
                u[k] = t
                x[k] = x[k] + t
        if keep_residual:
            au = apply(level, u, table)
            for k in range(q):
                r[k] = r[k] - au[k]

    def product(planes, table):
        m = table_product(jnp.concatenate(planes, axis=0), table)
        return [m[k * ROWS : (k + 1) * ROWS] for k in range(len(planes))]

    smooth(FINE, u7, r7, x7, d7, g7_ref, True, True)
    down = product(restrict_wall(R7, 7, 3, [r7[k] for k in range(7)]), r7_ref)
    for k in range(3):
        r3[k] = down[k]

    smooth(MID, u3, r3, x3, d3, g3_ref, True, True)
    r1 = product(restrict_wall(R3, 3, 1, [r3[k] for k in range(3)]), r3_ref)[0]

    start, steps = cheb_steps(LOW.bound, COARSE_STEPS, coarse_floor)
    my1 = height(0) * d1_mix
    u1 = start * (d1 * r1)
    x1 = u1
    for alpha, beta in steps:
        flow = g * (u1 - roll_up(u1))
        r1 = r1 - (my1 * u1 + (flow - roll_down(flow)))
        u1 = alpha * u1 + beta * (d1 * r1)
        x1 = x1 + u1

    up = prolong_wall(J3, 3, 1, product([x1], p3_ref))
    for k in range(3):
        u3[k] = up[k]
        x3[k] = x3[k] + up[k]
    au = apply(MID, u3, g3_ref)
    for k in range(3):
        r3[k] = r3[k] - au[k]
    smooth(MID, u3, r3, x3, d3, g3_ref, False, False)

    up = prolong_wall(J7, 7, 3, product([x3[k] for k in range(3)], p7_ref))
    for k in range(7):
        u7[k] = up[k]
        x7[k] = x7[k] + up[k]
    au = apply(FINE, u7, g7_ref)
    for k in range(7):
        r7[k] = r7[k] - au[k]
    smooth(FINE, u7, r7, x7, d7, g7_ref, False, False)

    for k in range(7):
        w_ref[pl.ds(k, ROWS, stride=7), :] = x7[k]
    for t in range(4):
        r = 98 * t
        both = jnp.concatenate(
            mix(first, w_ref[128 * t : 128 * t + 64, :], w_ref[128 * t + 64 : 128 * t + 128, :]), axis=0
        ).T
        out_ref[r : r + 49, :] = both[0:49]
        out_ref[r + 49 : r + 98, :] = both[64:113]
    out_ref[USED:, :] = jnp.zeros((FIELD - USED, 128), f32)


VMEM = pl.BlockSpec(memory_space=pltpu.VMEM)
PARAMS = pltpu.CompilerParams(vmem_limit_bytes=32 * 1024 * 1024)
FLAT = jax.ShapeDtypeStruct((FIELD, 128), f32)


def exchange(block, axes):
    n = lax.axis_size(axes)
    block = block.reshape(n, FIELD // n, 1, 128)
    return lax.all_to_all(block, axes, 0, 0).reshape(FIELD, 128)


def cycle_call(heights, modes):
    fine = pltpu.VMEM((7, ROWS, 128), f32)
    mid = pltpu.VMEM((3, ROWS, 128), f32)
    table = pltpu.VMEM((256, 256), bf16)
    return pl.pallas_call(
        cycle_kernel, out_shape=FLAT,
        in_specs=[VMEM, VMEM, VMEM], out_specs=VMEM,
        scratch_shapes=[
            pltpu.VMEM((7 * ROWS, 128), f32), mid,
            fine, fine, fine, fine, mid, mid, mid, mid,
            pltpu.VMEM((128, 128), f32), table, table, table, table, table, table,
        ],
        compiler_params=PARAMS,
    )(
        heights, jnp.asarray(MATRICES), modes,
    )


def transform(kernel, block, scratch=()):
    return pl.pallas_call(
        kernel, out_shape=FLAT, in_specs=[VMEM], out_specs=VMEM,
        scratch_shapes=scratch, compiler_params=PARAMS,
    )(block)


def body(residual, layer_heights):
    packed, heights = pl.pallas_call(
        pack_kernel, out_shape=(FLAT, jax.ShapeDtypeStruct((ROWS, 128), f32)),
        in_specs=[VMEM, VMEM], out_specs=(VMEM, VMEM),
        scratch_shapes=[pltpu.VMEM((8, 128), f32)],
        compiler_params=PARAMS,
    )(residual, layer_heights.reshape(1, NY))
    spans = transform(span_forward_kernel, exchange(packed, SPAN))
    modes = exchange(transform(flow_forward_kernel, exchange(spans, FLOW)), LAST)
    solved = exchange(cycle_call(heights, modes), LAST)
    flows = transform(flow_backward_kernel, solved, [pltpu.VMEM((FIELD, 128), f32)])
    spread = exchange(transform(span_backward_kernel, exchange(flows, FLOW)), SPAN)
    return pl.pallas_call(
        unpack_kernel, out_shape=jax.ShapeDtypeStruct((7, 14, 512), f32),
        in_specs=[VMEM], out_specs=VMEM, compiler_params=PARAMS,
    )(spread)


def solution(mesh):
    split = Mesh(mesh.devices.reshape(4, 2, 2, 2, 2, 4), FLOW + SPAN)
    spec = P(FLOW, SPAN, None)
    return jax.shard_map(
        body, mesh=split, in_specs=(spec, P()), out_specs=spec, check_vma=False
    )
```

```python
import jax
import jax.numpy as jnp
import ml_dtypes
import numpy as np
from jax import lax
from jax.experimental import pallas as pl
from jax.experimental.pallas import tpu as pltpu
from jax.sharding import Mesh
from jax.sharding import PartitionSpec as P


SMOOTH_STEPS = 3
COARSE_STEPS = 12
NX, NZ, NY = 32, 16, 73
DEVICES = 256
ROWS = 80
screen_shift = 0.02
smooth_floor = 0.1
coarse_floor = 0.01
f32 = jnp.float32
bf16 = jnp.bfloat16


def legendre_values(points, degree):
    columns = [np.ones(points.shape), points]
    for n in range(2, degree + 1):
        columns.append(((2 * n - 1) * points * columns[-1] - (n - 1) * columns[-2]) / n)
    return np.stack(columns[: degree + 1], axis=1)


def gll_tables(degree):
    nodes = -np.cos(np.pi * np.arange(degree + 1) / degree)
    for _ in range(100):
        values = legendre_values(nodes, degree)
        nodes = nodes - (nodes * values[:, degree] - values[:, degree - 1]) / (
            (degree + 1) * values[:, degree]
        )
    leading = legendre_values(nodes, degree)[:, degree]
    weights = 2.0 / (degree * (degree + 1) * leading**2)
    differ = np.zeros((degree + 1, degree + 1))
    for i in range(degree + 1):
        for j in range(degree + 1):
            if i != j:
                differ[i, j] = leading[i] / (leading[j] * (nodes[i] - nodes[j]))
    differ[0, 0] = -degree * (degree + 1) / 4.0
    differ[degree, degree] = degree * (degree + 1) / 4.0
    return nodes, weights, differ.T @ (weights[:, None] * differ)


def interp_table(fine_degree, coarse_degree):
    fine_nodes = gll_tables(fine_degree)[0]
    coarse_nodes = gll_tables(coarse_degree)[0]
    lagrange = np.ones((fine_degree + 1, coarse_degree + 1))
    for col in range(coarse_degree + 1):
        for other in range(coarse_degree + 1):
            if other != col:
                lagrange[:, col] *= (fine_nodes - coarse_nodes[other]) / (
                    coarse_nodes[col] - coarse_nodes[other]
                )
    return lagrange


def lanes_of(values):
    n = values.shape[0]
    out = np.zeros((7, 7))
    out[:n, :n] = values
    return np.pad(out.reshape(49), (0, 15))


def square_of(matrix, n_out, n_in):
    out = np.zeros((7, 7, 7, 7))
    out[:n_out, :n_out, :n_in, :n_in] = matrix.reshape(n_out, n_out, n_in, n_in)
    return np.pad(out.reshape(49, 49), ((0, 15), (0, 15)))


class Level:
    def __init__(self, q):
        self.q = q
        _, w, s = gll_tables(q)
        self.w, self.s = w, s
        mass = 0.5 * w[:q].copy()
        mass[0] = 0.5 * (w[0] + w[q])
        diag = 2.0 * np.diag(s)[:q].copy()
        diag[0] = 2.0 * (s[0, 0] + s[q, q])
        self.mxz = np.outer(mass, mass)
        a = np.outer(diag, mass) + np.outer(mass, diag) + screen_shift * self.mxz
        self.ratio = lanes_of(a / self.mxz)
        spread = np.abs(s).sum(axis=1)
        self.bound = max(1.0, float(np.max(spread / np.diag(s))))
        base = 2.0 * s[:q, :q].copy()
        base[0, 0] += 2.0 * s[q, q]
        e1 = np.zeros((q, q))
        e1[:, 0] = 2.0 * s[:q, q]
        even, odd = e1 + e1.T, e1 - e1.T
        dm = np.diag(mass)
        scale = np.concatenate([lanes_of(1.0 / self.mxz)] * 2)[None, :]
        sq = lambda m: square_of(m, q, q)
        fixed = sq(np.kron(base, dm) + np.kron(dm, base) + screen_shift * np.kron(dm, dm))
        tables = [np.hstack([fixed, 0.0 * fixed])]
        for c, n in (
            (np.kron(even, dm), np.kron(odd, dm)),
            (np.kron(dm, even), np.kron(dm, odd)),
        ):
            tables.append(np.hstack([sq(c), -sq(n)]))
        self.tables = [(t * scale)[: 64 if q > 3 else 24] for t in tables]
        self.weight = 0.5 * w
        self.stiff = s / self.weight[:, None]
        self.mass_lanes = np.concatenate([lanes_of(self.mxz)] * 2)
        self.inv_mass_lanes = np.concatenate([lanes_of(1.0 / self.mxz)] * 2)
        self.ratio_lanes = np.concatenate([self.ratio] * 2)
        self.mask_lanes = (self.mass_lanes > 0).astype(np.float64)


def transfer_tables(fine, coarse):
    j = interp_table(fine, coarse)
    ja = j[:fine, :coarse]
    jb = np.zeros((fine, coarse))
    jb[:, 0] = j[:fine, coarse]
    tables = []
    for n, b in enumerate((np.kron(ja, ja), np.kron(jb, ja), np.kron(ja, jb), np.kron(jb, jb))):
        b = square_of(b, fine, coarse).T[: 24 if coarse > 1 else 8]
        tables.append(np.hstack([b, b if n else 0.0 * b]))
    return j, tables


def phase_rows():
    rows = np.zeros((152, 2, 64))
    for n in range(NX):
        t = 2 * np.pi * n / NX
        rows[64 + 2 * n], rows[65 + 2 * n] = np.cos(t), np.sin(t)
        k = n % 16
        t = 2 * np.pi * k / NX
        if k:
            rows[2 * n], rows[2 * n + 1] = np.cos(t), np.sin(t)
        else:
            rows[2 * n, 0], rows[2 * n, 1] = 1.0, -1.0
    for k in range(9):
        t = 2 * np.pi * k / NZ
        rows[128 + 2 * k], rows[129 + 2 * k] = np.cos(t), np.sin(t) if k % 8 else 0.0
    return rows.reshape(152, 128)


FINE, MID, LOW = Level(7), Level(3), Level(1)
J7, P7_TABLES = transfer_tables(7, 3)
J3, P3_TABLES = transfer_tables(3, 1)
MATRICES = np.concatenate(FINE.tables + MID.tables + P7_TABLES + P3_TABLES).astype(np.float32)
R7 = FINE.weight[:, None] * J7 / MID.weight
R3 = MID.weight[:, None] * J3 / LOW.weight
G7_AT, G3_AT, P7_AT, P3_AT = 0, 192, 264, 360


LANES = np.zeros((16, 128))
for n, level in enumerate((FINE, MID)):
    LANES[4 * n] = level.mass_lanes
    LANES[4 * n + 1] = level.inv_mass_lanes
    LANES[4 * n + 2] = level.ratio_lanes
    LANES[4 * n + 3] = level.mask_lanes
LANES[8] = LOW.mask_lanes
MATRICES = np.concatenate([MATRICES, LANES, phase_rows()]).astype(np.float32)
LANES_AT, PHASES_AT = 392, 408


def cheb_steps(bound, sweeps, floor):
    centre = bound * (1.0 + floor) / 2.0
    half = bound * (1.0 - floor) / 2.0
    s = centre / half
    p = 1.0 / s
    steps = []
    for _ in range(sweeps - 1):
        p_next = 1.0 / (2.0 * s - p)
        steps.append((p_next * p, 2.0 * p_next / half))
        p = p_next
    return 1.0 / centre, steps


FLOW, SPAN = ("zh", "z0", "xh", "core"), ("xl", "y")
LAST = ("xl", "y", "z0", "core")
ORDER = ("zh", "z0", "xh", "core")
SLAB = 13
FIELD = 32 * SLAB
USED = 8 * 49


def swap(v):
    return pltpu.roll(v, 64, axis=1)


def mix(first, v, w):
    return jnp.where(first, v, swap(w)), jnp.where(first, swap(v), w)


def pack_kernel(x_hbm, h_hbm, o_ref, rows_ref, x_ref, h_ref, line_ref, sems):
    line = pltpu.make_async_copy(h_hbm, h_ref, sems.at[0])
    line.start()
    field = pltpu.make_async_copy(x_hbm, x_ref, sems.at[1])
    field.start()
    first, _ = lane_tools()
    o_ref[USED:, :] = jnp.zeros((FIELD - USED, 128), f32)
    line_ref[...] = jnp.zeros_like(line_ref)
    line.wait()
    line_ref[0:1, 0:NY] = h_ref[...]
    rows_ref[...] = jnp.broadcast_to(line_ref[0:1, :], (128, 128)).T[:ROWS]
    field.wait()
    for a in range(7):
        for t in range(4):
            part = slice(128 * t, 128 * t + 128)
            low, high = mix(first, x_ref[a, 0:7, part], x_ref[a, 7:14, part])
            r = 98 * t + 7 * a
            o_ref[r : r + 7, :] = low
            o_ref[r + 49 : r + 56, :] = high


def unpack_kernel(x_ref, o_ref):
    first, _ = lane_tools()
    for a in range(7):
        for t in range(4):
            part = slice(128 * t, 128 * t + 128)
            r = 98 * t + 7 * a
            low, high = mix(first, x_ref[r : r + 7, :], x_ref[r + 49 : r + 56, :])
            o_ref[a, 0:7, part] = low
            o_ref[a, 7:14, part] = high


def halves(v):
    high = v.astype(bf16)
    return high, (v - high.astype(f32)).astype(bf16)


def dot(a, b):
    return jnp.dot(a, b, preferred_element_type=f32)


HALF = float(np.sqrt(0.5))


def lane_tools():
    first = lax.broadcasted_iota(jnp.int32, (1, 128), 1) < 64
    return first, jnp.where(first, 1.0, -1.0).astype(f32)


def plane(ref, n):
    return ref[n * SLAB : n * SLAB + SLAB, :]


def put(ref, n, v):
    ref[n * SLAB : n * SLAB + SLAB, :] = v


def flow_place(n):
    bits = {"zh": n // 8, "z0": n // 4 % 2, "xh": n // 2 % 2, "core": n % 2}
    place = 0
    for name in ORDER:
        place = place * (4 if name == "zh" else 2) + bits[name]
    return place


def span_mode():
    return lax.axis_index("zh") * 2 + lax.axis_index("xh")


def span_forward_kernel(x_ref, o_ref):
    first, sign = lane_tools()
    for z0, core in ((0, 0), (0, 1), (1, 0), (1, 1)):
        x = [plane(x_ref, 4 * j + 2 * z0 + core) for j in range(8)]
        at = [flow_place(4 * (k // 2 * 2 + z0) + 2 * (k % 2) + core) for k in range(8)]
        s = [None] + [x[j] + x[8 - j] for j in (1, 2, 3)]
        d = [None] + [x[j] - x[8 - j] for j in (1, 2, 3)]
        up, down = x[0] + x[4], x[0] - x[4]
        odd, turn = s[1] + s[3], HALF * (s[1] - s[3])
        slope = HALF * (d[1] + d[3])
        re = [up + s[2] + odd, down + turn, up - s[2], down - turn, up + s[2] - odd]
        im = [None, -slope - d[2], d[3] - d[1], d[2] - slope]
        flip = swap(re[0])
        put(o_ref, at[0], jnp.where(first, re[0] + flip, flip - re[0]))
        put(o_ref, at[4], sign * re[4])
        for f in (1, 2, 3):
            c, t = float(np.cos(np.pi * f / 8)), float(np.sin(np.pi * f / 8))
            re_swap, im_swap = swap(re[f]), swap(im[f])
            base = jnp.where(first, re[f], im_swap)
            extra = c * jnp.where(first, re_swap, im[f]) + t * jnp.where(first, im_swap, -re[f])
            put(o_ref, at[f], base + extra)
            put(o_ref, at[8 - f], sign * (base - extra))


def span_backward_kernel(x_ref, o_ref):
    first, sign = lane_tools()
    for z0, core in ((0, 0), (0, 1), (1, 0), (1, 1)):
        v = [plane(x_ref, flow_place(4 * (k // 2 * 2 + z0) + 2 * (k % 2) + core)) for k in range(8)]
        flip = swap(v[0])
        re = [jnp.where(first, v[0] + flip, flip - v[0])]
        im = [None]
        for f in (1, 2, 3):
            c, t = float(np.cos(np.pi * f / 8)), float(np.sin(np.pi * f / 8))
            total, other = v[f] + v[8 - f], swap(v[f] - v[8 - f])
            re.append(2.0 * jnp.where(first, total, c * other - t * total))
            im.append(2.0 * jnp.where(first, other, t * other + c * total))
        re.append((2.0 * sign) * v[4])
        up, down = re[0] + re[4], re[0] - re[4]
        odd, turn = re[1] + re[3], HALF * (re[1] - re[3])
        slope = HALF * (im[1] + im[3])
        c = [up + re[2] + odd, down + turn, up - re[2], down - turn, up + re[2] - odd]
        s = [None, slope + im[2], im[1] - im[3], slope - im[2]]
        at = [4 * j + 2 * z0 + core for j in range(8)]
        put(o_ref, at[0], c[0])
        put(o_ref, at[4], c[4])
        for j in (1, 2, 3):
            put(o_ref, at[j], c[j] - s[j])
            put(o_ref, at[8 - j], c[j] + s[j])


def complex_transform(x, sign, direction):
    n = len(x)
    if n == 1:
        return x
    even = complex_transform(x[0::2], sign, direction)
    odd = complex_transform(x[1::2], sign, direction)
    low, high = [], []
    for k in range(n // 2):
        c = float(np.cos(2 * np.pi * k / n))
        s = direction * float(np.sin(2 * np.pi * k / n))
        if k == 0:
            t = odd[k]
        elif 4 * k == n:
            t = (s * sign) * swap(odd[k])
        else:
            t = c * odd[k] + (s * sign) * swap(odd[k])
        low.append(even[k] + t)
        high.append(even[k] - t)
    return low + high


def flow_forward_kernel(x_ref, o_ref):
    first, sign = lane_tools()
    for n, v in enumerate(complex_transform([plane(x_ref, flow_place(n)) for n in range(NX)], sign, 1.0)):
        put(o_ref, n, v)

    @pl.when(span_mode() == 0)
    def _():
        w = [plane(o_ref, n) for n in range(NX)]
        put(o_ref, 0, jnp.where(first, w[0], swap(w[16])))
        put(o_ref, 16, jnp.where(first, swap(w[0]), w[16]))
        for n in range(1, 16):
            total, differ = w[n] + w[NX - n], w[n] - w[NX - n]
            put(o_ref, n, 0.5 * jnp.where(first, total, differ))
            put(o_ref, 16 + n, 0.5 * swap(jnp.where(first, -differ, total)))


def flow_backward_kernel(x_ref, o_ref, w_ref):
    first, sign = lane_tools()

    @pl.when(span_mode() == 0)
    def _():
        v = [plane(x_ref, n) for n in range(NX)]
        put(w_ref, 0, jnp.where(first, v[0], swap(v[16])))
        put(w_ref, 16, jnp.where(first, swap(v[0]), v[16]))
        for n in range(1, 16):
            other = swap(v[16 + n])
            put(w_ref, n, v[n] - sign * other)
            put(w_ref, NX - n, sign * v[n] + other)

    @pl.when(span_mode() > 0)
    def _():
        w_ref[...] = x_ref[...]

    for n, v in enumerate(complex_transform([plane(w_ref, n) for n in range(NX)], sign, -1.0)):
        put(o_ref, flow_place(n), v)


def table_product(v, t_ref):
    both = dot(jnp.concatenate(halves(v), axis=1), t_ref[...])
    return both[:, :128] + both[:, 128:]


def store_table(t_ref, table):
    high, low = halves(table)
    t_ref[0:128, 0:128] = high
    t_ref[128:256, 0:128] = high
    t_ref[0:128, 128:256] = low
    t_ref[128:256, 128:256] = jnp.zeros((128, 128), bf16)


def roll_up(v):
    return pltpu.roll(v, ROWS - 1, axis=0)


def roll_down(v):
    return pltpu.roll(v, 1, axis=0)


def wall_apply(s, q, planes, g):
    parts = [g * p for p in planes] + [g * roll_up(planes[0])]
    n = q + 1
    half = n // 2
    even = [parts[l] + parts[q - l] for l in range(half)]
    odd = [parts[l] - parts[q - l] for l in range(half)]
    out = [None] * n
    for k in range(half):
        p = m = None
        for l in range(half):
            ce = 0.5 * (s[k, l] + s[k, q - l])
            co = 0.5 * (s[k, l] - s[k, q - l])
            te, to = float(ce) * even[l], float(co) * odd[l]
            p = te if p is None else p + te
            m = to if m is None else m + to
        out[k] = p + m
        out[q - k] = p - m
    out[0] = out[0] + roll_down(out[q])
    return out[:q]


def weighted_sum(coefs, planes):
    total = None
    for c, v in zip(coefs, planes):
        c = float(c)
        if c == 0.0:
            continue
        t = v if c == 1.0 else c * v
        total = t if total is None else total + t
    return total


def restrict_wall(j, fine, coarse, planes):
    out = [weighted_sum(j[:fine, c], planes) for c in range(coarse)]
    out[0] = out[0] + roll_down(weighted_sum(j[:fine, coarse], planes))
    return out


def prolong_wall(j, fine, coarse, planes):
    closed = list(planes) + [roll_up(planes[0])]
    return [weighted_sum(j[k], closed) for k in range(fine)]


def cycle_kernel(
    h_ref, mats_ref, in_ref, out_ref,
    w_ref, geo_ref,
    u7, r7, x7, d7, u3, r3, x3, d3,
    square, g7_ref, g3_ref, r7_ref, p7_ref, r3_ref, p3_ref,
):
    n = lax.axis_index(LAST)
    b = span_mode()
    at_x = PHASES_AT + 2 * n + jnp.where(b > 0, 64, 0)
    at_z = PHASES_AT + 128 + 2 * jnp.where(b > 0, b, n // 16 * 8)
    cx, sx = mats_ref[pl.ds(at_x, 1), :], mats_ref[pl.ds(at_x + 1, 1), :]
    cz, sz = mats_ref[pl.ds(at_z, 1), :], mats_ref[pl.ds(at_z + 1, 1), :]
    cosines = (cx, cz, cx * cz - sx * sz)
    sines = (sx, sz, sx * cz + cx * sz)
    lane = lax.broadcasted_iota(jnp.int32, (1, 128), 1)
    first = lane < 64
    mass7, inv7, ratio7, mask7 = (mats_ref[n : n + 1, :] for n in range(LANES_AT, LANES_AT + 4))
    mass3, inv3, ratio3, mask3 = (mats_ref[n : n + 1, :] for n in range(LANES_AT + 4, LANES_AT + 8))
    mask1 = mats_ref[LANES_AT + 8 : LANES_AT + 9, :]

    upper = [jnp.where(first, c, s) for c, s in zip(cosines, sines)]
    lower = [jnp.where(first, -s, c) for c, s in zip(cosines, sines)]

    def mode_table(at, rows, phases):
        top = mats_ref[at : at + rows]
        low = pltpu.roll(top, 64, axis=1)
        for n in range(phases):
            at += rows
            t = mats_ref[at : at + rows]
            top = top + upper[n] * t
            low = low + lower[n] * pltpu.roll(t, 64, axis=1)
        if rows == 64:
            return jnp.concatenate([top, low], axis=0)
        square[...] = jnp.zeros((128, 128), f32)
        square[0:rows] = top
        square[64 : 64 + rows] = low
        return square[...]

    store_table(g7_ref, mode_table(G7_AT, 64, 2))
    store_table(g3_ref, mode_table(G3_AT, 24, 2))
    table = mode_table(P7_AT, 24, 3)
    store_table(p7_ref, table)
    store_table(r7_ref, (table * mass7).T * inv3)
    table = mode_table(P3_AT, 8, 3)
    store_table(p3_ref, table)
    store_table(r3_ref, (table * mass3).T)

    scale = inv7 * (1.0 / (NX * NZ))
    for t in range(4):
        r = 98 * t
        both = jnp.concatenate([in_ref[r : r + 64, :], in_ref[r + 49 : r + 113, :]], axis=0).T
        low, high = mix(first, both[:64], both[64:])
        w_ref[128 * t : 128 * t + 64, :] = low * scale
        w_ref[128 * t + 64 : 128 * t + 128, :] = high * scale
    w_ref[512:, :] = jnp.zeros((w_ref.shape[0] - 512, 128), f32)
    for k in range(7):
        r7[k] = float(1.0 / FINE.weight[k]) * w_ref[pl.ds(k, ROWS, stride=7), :]

    h = h_ref[...]
    row = lax.broadcasted_iota(jnp.int32, (ROWS, 128), 0)
    g = jnp.where(row < NY, 2.0 / jnp.where(row < NY, h, 1.0), 0.0)
    h_pair = h + roll_down(h)
    g_pair = g + roll_down(g)
    geo_ref[0] = h
    geo_ref[1] = g
    geo_ref[2] = h_pair

    def height(k):
        return geo_ref[0 if k else 2]

    def inverse_diag(level, ratio, mask, k):
        d = height(k) * ratio + float(level.stiff[k, k]) * (g if k else g_pair)
        return jnp.where(d > 0.0, mask / jnp.where(d > 0.0, d, 1.0), 0.0)

    for k in range(7):
        d7[k] = inverse_diag(FINE, ratio7, mask7, k)
    for k in range(3):
        d3[k] = inverse_diag(MID, ratio3, mask3, k)
    d1_mix = ((4.0 + screen_shift) - 2.0 * cx - 2.0 * cz) * mask1
    d1 = inverse_diag(LOW, 4.0 + screen_shift, mask1, 0)

    def apply(level, u, table):
        q = level.q
        m = table_product(u[...].reshape(q * ROWS, 128), table)
        wall = wall_apply(level.stiff, q, [u[k] for k in range(q)], geo_ref[1])
        return [height(k) * m[k * ROWS : (k + 1) * ROWS] + wall[k] for k in range(q)]

    def smooth(level, u, r, x, d, table, fresh, keep_residual):
        q = level.q
        start, steps = cheb_steps(level.bound, SMOOTH_STEPS, smooth_floor)
        for k in range(q):
            t = start * (d[k] * r[k])
            u[k] = t
            x[k] = t if fresh else x[k] + t
        for alpha, beta in steps:
            au = apply(level, u, table)
            for k in range(q):
                t = r[k] - au[k]
                r[k] = t
                t = alpha * u[k] + beta * (d[k] * t)
                u[k] = t
                x[k] = x[k] + t
        if keep_residual:
            au = apply(level, u, table)
            for k in range(q):
                r[k] = r[k] - au[k]

    def product(planes, table):
        m = table_product(jnp.concatenate(planes, axis=0), table)
        return [m[k * ROWS : (k + 1) * ROWS] for k in range(len(planes))]

    smooth(FINE, u7, r7, x7, d7, g7_ref, True, True)
    down = product(restrict_wall(R7, 7, 3, [r7[k] for k in range(7)]), r7_ref)
    for k in range(3):
        r3[k] = down[k]

    smooth(MID, u3, r3, x3, d3, g3_ref, True, True)
    r1 = product(restrict_wall(R3, 3, 1, [r3[k] for k in range(3)]), r3_ref)[0]

    start, steps = cheb_steps(LOW.bound, COARSE_STEPS, coarse_floor)
    my1 = height(0) * d1_mix
    u1 = start * (d1 * r1)
    x1 = u1
    for alpha, beta in steps:
        flow = g * (u1 - roll_up(u1))
        r1 = r1 - (my1 * u1 + (flow - roll_down(flow)))
        u1 = alpha * u1 + beta * (d1 * r1)
        x1 = x1 + u1

    up = prolong_wall(J3, 3, 1, product([x1], p3_ref))
    for k in range(3):
        u3[k] = up[k]
        x3[k] = x3[k] + up[k]
    au = apply(MID, u3, g3_ref)
    for k in range(3):
        r3[k] = r3[k] - au[k]
    smooth(MID, u3, r3, x3, d3, g3_ref, False, False)

    up = prolong_wall(J7, 7, 3, product([x3[k] for k in range(3)], p7_ref))
    for k in range(7):
        u7[k] = up[k]
        x7[k] = x7[k] + up[k]
    au = apply(FINE, u7, g7_ref)
    for k in range(7):
        r7[k] = r7[k] - au[k]
    smooth(FINE, u7, r7, x7, d7, g7_ref, False, False)

    for k in range(7):
        w_ref[pl.ds(k, ROWS, stride=7), :] = x7[k]
    for t in range(4):
        r = 98 * t
        both = jnp.concatenate(
            mix(first, w_ref[128 * t : 128 * t + 64, :], w_ref[128 * t + 64 : 128 * t + 128, :]), axis=0
        ).T
        out_ref[r : r + 49, :] = both[0:49]
        out_ref[r + 49 : r + 98, :] = both[64:113]
    out_ref[USED:, :] = jnp.zeros((FIELD - USED, 128), f32)


VMEM = pl.BlockSpec(memory_space=pltpu.VMEM)
HBM = pl.BlockSpec(memory_space=pltpu.HBM)
PARAMS = pltpu.CompilerParams(vmem_limit_bytes=32 * 1024 * 1024)
FLAT = jax.ShapeDtypeStruct((FIELD, 128), f32)


def exchange(block, axes):
    n = lax.axis_size(axes)
    block = block.reshape(n, FIELD // n, 1, 128)
    return lax.all_to_all(block, axes, 0, 0).reshape(FIELD, 128)


def cycle_call(heights, modes):
    fine = pltpu.VMEM((7, ROWS, 128), f32)
    mid = pltpu.VMEM((3, ROWS, 128), f32)
    table = pltpu.VMEM((256, 256), bf16)
    return pl.pallas_call(
        cycle_kernel, out_shape=FLAT,
        in_specs=[VMEM, VMEM, VMEM], out_specs=VMEM,
        scratch_shapes=[
            pltpu.VMEM((7 * ROWS, 128), f32), mid,
            fine, fine, fine, fine, mid, mid, mid, mid,
            pltpu.VMEM((128, 128), f32), table, table, table, table, table, table,
        ],
        compiler_params=PARAMS,
    )(
        heights, jnp.asarray(MATRICES), modes,
    )


def transform(kernel, block, scratch=()):
    return pl.pallas_call(
        kernel, out_shape=FLAT, in_specs=[VMEM], out_specs=VMEM,
        scratch_shapes=scratch, compiler_params=PARAMS,
    )(block)


def body(residual, layer_heights):
    stay = lambda v: pltpu.with_memory_space_constraint(v, pltpu.HBM)
    packed, heights = pl.pallas_call(
        pack_kernel, out_shape=(FLAT, jax.ShapeDtypeStruct((ROWS, 128), f32)),
        in_specs=[HBM, HBM], out_specs=(VMEM, VMEM),
        scratch_shapes=[
            pltpu.VMEM((7, 14, 512), f32), pltpu.VMEM((1, NY), f32), pltpu.VMEM((8, 128), f32),
            pltpu.SemaphoreType.DMA((2,)),
        ],
        compiler_params=PARAMS,
    )(stay(residual), stay(layer_heights.reshape(1, NY)))
    spans = transform(span_forward_kernel, exchange(packed, SPAN))
    modes = exchange(transform(flow_forward_kernel, exchange(spans, ORDER)), LAST)
    solved = exchange(cycle_call(heights, modes), LAST)
    flows = transform(flow_backward_kernel, solved, [pltpu.VMEM((FIELD, 128), f32)])
    spread = exchange(transform(span_backward_kernel, exchange(flows, ORDER)), SPAN)
    return pl.pallas_call(
        unpack_kernel, out_shape=jax.ShapeDtypeStruct((7, 14, 512), f32),
        in_specs=[VMEM], out_specs=VMEM, compiler_params=PARAMS,
    )(spread)


def solution(mesh):
    split = Mesh(mesh.devices.reshape(4, 2, 2, 2, 2, 4), FLOW + SPAN)
    spec = P(FLOW, SPAN, None)
    return jax.shard_map(
        body, mesh=split, in_specs=(spec, P()), out_specs=spec, check_vma=False
    )
```

```python
import jax
import jax.numpy as jnp
import ml_dtypes
import numpy as np
from jax import lax
from jax.experimental import pallas as pl
from jax.experimental.pallas import tpu as pltpu
from jax.sharding import Mesh
from jax.sharding import PartitionSpec as P


SMOOTH_STEPS = 3
COARSE_STEPS = 12
NX, NZ, NY = 32, 16, 73
DEVICES = 256
ROWS = 80
screen_shift = 0.02
smooth_floor = 0.1
coarse_floor = 0.01
f32 = jnp.float32
bf16 = jnp.bfloat16


def legendre_values(points, degree):
    columns = [np.ones(points.shape), points]
    for n in range(2, degree + 1):
        columns.append(((2 * n - 1) * points * columns[-1] - (n - 1) * columns[-2]) / n)
    return np.stack(columns[: degree + 1], axis=1)


def gll_tables(degree):
    nodes = -np.cos(np.pi * np.arange(degree + 1) / degree)
    for _ in range(100):
        values = legendre_values(nodes, degree)
        nodes = nodes - (nodes * values[:, degree] - values[:, degree - 1]) / (
            (degree + 1) * values[:, degree]
        )
    leading = legendre_values(nodes, degree)[:, degree]
    weights = 2.0 / (degree * (degree + 1) * leading**2)
    differ = np.zeros((degree + 1, degree + 1))
    for i in range(degree + 1):
        for j in range(degree + 1):
            if i != j:
                differ[i, j] = leading[i] / (leading[j] * (nodes[i] - nodes[j]))
    differ[0, 0] = -degree * (degree + 1) / 4.0
    differ[degree, degree] = degree * (degree + 1) / 4.0
    return nodes, weights, differ.T @ (weights[:, None] * differ)


def interp_table(fine_degree, coarse_degree):
    fine_nodes = gll_tables(fine_degree)[0]
    coarse_nodes = gll_tables(coarse_degree)[0]
    lagrange = np.ones((fine_degree + 1, coarse_degree + 1))
    for col in range(coarse_degree + 1):
        for other in range(coarse_degree + 1):
            if other != col:
                lagrange[:, col] *= (fine_nodes - coarse_nodes[other]) / (
                    coarse_nodes[col] - coarse_nodes[other]
                )
    return lagrange


def lane_at(a, b):
    n = 7 * b + a
    return n if n < 25 else n + 7


def lanes_of(values):
    n = values.shape[0]
    out = np.zeros(64)
    for a in range(n):
        for b in range(n):
            out[lane_at(a, b)] = values[a, b]
    return out


def square_of(matrix, n_out, n_in):
    rows = [lane_at(a, b) for a in range(n_out) for b in range(n_out)]
    columns = [lane_at(a, b) for a in range(n_in) for b in range(n_in)]
    out = np.zeros((64, 64))
    out[np.ix_(rows, columns)] = matrix
    return out


def line_basis(q, t):
    u = np.zeros((q, q), complex)
    u[0, 0] = 1.0
    turn = np.exp(-0.5j * t) / np.sqrt(2.0)
    for a in range(1, (q + 1) // 2):
        u[a, a] = u[a, q - a] = turn
        u[q - a, a], u[q - a, q - a] = -1j * turn, 1j * turn
    return u


def closing(q, t):
    out = np.eye(q + 1, q, dtype=complex)
    out[q, 0] = np.exp(1j * t)
    return out


def real_parts(matrix_of, count):
    angles = 0.3 + 0.7 * np.arange(8)
    terms = np.stack([np.ones(8), np.cos(angles / 2), np.sin(angles / 2), np.cos(angles)], 1)[:, :count]
    values = np.stack([matrix_of(t) for t in angles])
    flat = values.reshape(8, -1)
    parts = np.linalg.lstsq(terms, flat.real, rcond=None)[0]
    assert np.abs(terms @ parts - flat).max() < 1e-11 * np.abs(flat).max()
    return parts.reshape((count,) + values.shape[1:])


class Level:
    def __init__(self, q):
        self.q = q
        _, w, s = gll_tables(q)
        self.w, self.s = w, s
        mass = 0.5 * w[:q].copy()
        mass[0] = 0.5 * (w[0] + w[q])
        diag = 2.0 * np.diag(s)[:q].copy()
        diag[0] = 2.0 * (s[0, 0] + s[q, q])
        self.mxz = np.outer(mass, mass)
        a = np.outer(diag, mass) + np.outer(mass, diag) + screen_shift * self.mxz
        self.ratio = lanes_of(a / self.mxz)
        spread = np.abs(s).sum(axis=1)
        self.bound = max(1.0, float(np.max(spread / np.diag(s))))
        base = 2.0 * s[:q, :q].copy()
        base[0, 0] += 2.0 * s[q, q]
        e1 = np.zeros((q, q))
        e1[:, 0] = 2.0 * s[:q, q]
        even, odd = e1 + e1.T, e1 - e1.T
        dm = np.diag(mass)
        scale = np.concatenate([lanes_of(1.0 / self.mxz)] * 2)[None, :]
        sq = lambda m: square_of(m, q, q)
        span = real_parts(
            lambda t: line_basis(q, t) @ closing(q, t).conj().T @ (2.0 * s) @ closing(q, t) @ line_basis(q, t).conj().T, 4
        )
        fixed = sq(np.kron(base, dm) + np.kron(dm, span[0]) + screen_shift * np.kron(dm, dm))
        tables = [np.hstack([fixed, 0.0 * fixed])]
        tables.append(np.hstack([sq(np.kron(even, dm)), -sq(np.kron(odd, dm))]))
        for part in span[1:]:
            part = sq(np.kron(dm, part))
            tables.append(np.hstack([part, 0.0 * part]))
        self.tables = [(t * scale)[: 64 if q > 3 else 24] for t in tables]
        self.weight = 0.5 * w
        self.stiff = s / self.weight[:, None]
        self.mass_lanes = np.concatenate([lanes_of(self.mxz)] * 2)
        self.inv_mass_lanes = np.concatenate([lanes_of(1.0 / self.mxz)] * 2)
        self.ratio_lanes = np.concatenate([self.ratio] * 2)
        self.mask_lanes = (self.mass_lanes > 0).astype(np.float64)


def transfer_tables(fine, coarse):
    j = interp_table(fine, coarse)
    ja = j[:fine, :coarse]
    jb = np.zeros((fine, coarse))
    jb[:, 0] = j[:fine, coarse]
    span = real_parts(
        lambda t: line_basis(fine, t) @ j[:fine] @ closing(coarse, t) @ line_basis(coarse, t).conj().T, 3
    )
    tables = []
    for part in span:
        for flow in (ja, jb):
            b = square_of(np.kron(flow, part), fine, coarse).T[: 24 if coarse > 1 else 8]
            tables.append(np.hstack([b, b if flow is jb else 0.0 * b]))
    return j, tables


def phase_rows():
    rows = np.zeros((80, 2, 64))
    for n in range(16):
        t = 2 * np.pi * n / NX
        if n:
            rows[2 * n], rows[2 * n + 1] = np.cos(t), np.sin(t)
        else:
            rows[0, 0], rows[0, 1] = 1.0, -1.0
    for k in range(8):
        for part in range(2):
            t = 2 * np.pi * k / NZ if k else np.pi * part
            at = 32 + 3 * (2 * k + part)
            rows[at], rows[at + 1], rows[at + 2] = np.cos(t / 2), np.sin(t / 2), np.cos(t)
    return rows.reshape(80, 128)


FINE, MID, LOW = Level(7), Level(3), Level(1)
J7, P7_TABLES = transfer_tables(7, 3)
J3, P3_TABLES = transfer_tables(3, 1)
MATRICES = np.concatenate(FINE.tables + MID.tables + P7_TABLES + P3_TABLES).astype(np.float32)
R7 = FINE.weight[:, None] * J7 / MID.weight
R3 = MID.weight[:, None] * J3 / LOW.weight
G7_AT, G3_AT, P7_AT, P3_AT = 0, 320, 440, 584


LANES = np.zeros((16, 128))
for n, level in enumerate((FINE, MID)):
    LANES[4 * n] = level.mass_lanes
    LANES[4 * n + 1] = level.inv_mass_lanes
    LANES[4 * n + 2] = level.ratio_lanes
    LANES[4 * n + 3] = level.mask_lanes
LANES[8] = LOW.mask_lanes
MATRICES = np.concatenate([MATRICES, LANES, phase_rows()]).astype(np.float32)
LANES_AT, PHASES_AT = 632, 648


def cheb_steps(bound, sweeps, floor):
    centre = bound * (1.0 + floor) / 2.0
    half = bound * (1.0 - floor) / 2.0
    s = centre / half
    p = 1.0 / s
    steps = []
    for _ in range(sweeps - 1):
        p_next = 1.0 / (2.0 * s - p)
        steps.append((p_next * p, 2.0 * p_next / half))
        p = p_next
    return 1.0 / centre, steps


FLOW, SPAN = ("zh", "z0", "xh", "core"), ("xl", "y")
LAST = ("xl", "y", "core")
USED = 8 * 49
SLAB = 13
FIELD = 32 * SLAB


def swap(v):
    return pltpu.roll(v, 64, axis=1)


def mix(first, v, w):
    return jnp.where(first, v, swap(w)), jnp.where(first, swap(v), w)


def pack_kernel(x_hbm, h_hbm, o_ref, rows_ref, x_ref, h_ref, line_ref, sems):
    line = pltpu.make_async_copy(h_hbm, h_ref, sems.at[0])
    line.start()
    field = pltpu.make_async_copy(x_hbm, x_ref, sems.at[1])
    field.start()
    first, _ = lane_tools()
    line_ref[...] = jnp.zeros_like(line_ref)
    line.wait()
    line_ref[0:1, 0:NY] = h_ref[...]
    rows_ref[...] = jnp.broadcast_to(line_ref[0:1, :], (128, 128)).T[:ROWS]
    field.wait()
    for a in range(7):
        for t in range(4):
            part = slice(128 * t, 128 * t + 128)
            low, high = mix(first, x_ref[a, 0:7, part], x_ref[a, 7:14, part])
            o_ref[pl.ds(98 * t + a, 7, stride=7), :] = low
            o_ref[pl.ds(98 * t + 49 + a, 7, stride=7), :] = high


def unpack_kernel(x_ref, o_ref):
    first, _ = lane_tools()
    for a in range(7):
        for t in range(4):
            part = slice(128 * t, 128 * t + 128)
            low, high = mix(
                first,
                x_ref[pl.ds(98 * t + a, 7, stride=7), :],
                x_ref[pl.ds(98 * t + 49 + a, 7, stride=7), :],
            )
            o_ref[a, 0:7, part] = low
            o_ref[a, 7:14, part] = high


def halves(v):
    high = v.astype(bf16)
    return high, (v - high.astype(f32)).astype(bf16)


def dot(a, b):
    return jnp.dot(a, b, preferred_element_type=f32)


HALF = float(np.sqrt(0.5))


def lane_tools():
    first = lax.broadcasted_iota(jnp.int32, (1, 128), 1) < 64
    return first, jnp.where(first, 1.0, -1.0).astype(f32)


def turned(v, sign, angle, size):
    c, s = float(size * np.cos(angle)), float(size * np.sin(angle))
    return c * v + (s * sign) * swap(v)


def span_modes(x, first, sign):
    s = [None] + [x[j] + x[8 - j] for j in (1, 2, 3)]
    d = [None] + [x[j] - x[8 - j] for j in (1, 2, 3)]
    up, down = x[0] + x[4], x[0] - x[4]
    odd, turn = s[1] + s[3], HALF * (s[1] - s[3])
    slope = HALF * (d[1] + d[3])
    re = [up + s[2] + odd, down + turn, up - s[2], down - turn, up + s[2] - odd]
    im = [None, -slope - d[2], d[3] - d[1], d[2] - slope]
    flip = swap(re[0])
    out = [None] * 8
    out[0] = jnp.where(first, re[0] + flip, flip - re[0])
    out[4] = sign * re[4]
    for f in (1, 2, 3):
        c, t = float(np.cos(np.pi * f / 8)), float(np.sin(np.pi * f / 8))
        re_swap, im_swap = swap(re[f]), swap(im[f])
        base = jnp.where(first, re[f], im_swap)
        extra = c * jnp.where(first, re_swap, im[f]) + t * jnp.where(first, im_swap, -re[f])
        out[f] = base + extra
        out[8 - f] = sign * (base - extra)
    return out


def span_elements(v, first, sign):
    flip = swap(v[0])
    re = [jnp.where(first, v[0] + flip, flip - v[0])]
    im = [None]
    for f in (1, 2, 3):
        c, t = float(np.cos(np.pi * f / 8)), float(np.sin(np.pi * f / 8))
        total, other = v[f] + v[8 - f], swap(v[f] - v[8 - f])
        re.append(2.0 * jnp.where(first, total, c * other - t * total))
        im.append(2.0 * jnp.where(first, other, t * other + c * total))
    re.append((2.0 * sign) * v[4])
    up, down = re[0] + re[4], re[0] - re[4]
    odd, turn = re[1] + re[3], HALF * (re[1] - re[3])
    slope = HALF * (im[1] + im[3])
    c = [up + re[2] + odd, down + turn, up - re[2], down - turn, up + re[2] - odd]
    s = [None, slope + im[2], im[1] - im[3], slope - im[2]]
    return [c[0]] + [c[j] - s[j] for j in (1, 2, 3)] + [c[4]] + [c[j] + s[j] for j in (3, 2, 1)]


def mode_rows(k, part):
    return 26 * (4 * (k // 2) + 2 * part + k % 2)


def span_forward_kernel(x_ref, o_ref, v_ref):
    first, sign = lane_tools()
    for k in range(8):
        v_ref[k, 48:56] = jnp.zeros((8, 128), f32)
    nodes = lambda b: [x_ref[49 * j + 7 * b : 49 * j + 7 * b + 7, :] for j in range(8)]
    for k, v in enumerate(span_modes(nodes(0), first, sign)):
        v_ref[k, 0:7] = v
    for b in (1, 2, 3):
        near, far = nodes(b), nodes(7 - b)
        total = span_modes([p + q for p, q in zip(near, far)], first, sign)
        differ = span_modes([p - q for p, q in zip(near, far)], first, sign)
        for k in range(8):
            t = np.pi * k / NZ
            at, end = 7 * b, 7 * (7 - b)
            v_ref[k, at : at + 7] = turned(total[k], sign, t, HALF) if k else HALF * total[k]
            v_ref[k, end : end + 7] = turned(differ[k], sign, t + np.pi / 2, HALF) if k else -HALF * differ[k]
    for k in range(8):
        re, im = mix(first, v_ref[k, 0:26], v_ref[k, 25:51])
        o_ref[mode_rows(k, 0) : mode_rows(k, 0) + 26, :] = re
        o_ref[mode_rows(k, 1) : mode_rows(k, 1) + 26, :] = im


def span_backward_kernel(x_ref, o_ref, v_ref):
    first, sign = lane_tools()
    for k in range(8):
        near, far = mix(
            first,
            x_ref[mode_rows(k, 0) : mode_rows(k, 0) + 26, :],
            x_ref[mode_rows(k, 1) : mode_rows(k, 1) + 26, :],
        )
        v_ref[k, 0:25] = near[0:25]
        v_ref[k, 25:49] = far[0:24]

    def store(b, planes):
        for j, v in enumerate(planes):
            o_ref[49 * j + 7 * b : 49 * j + 7 * b + 7, :] = v

    store(0, span_elements([v_ref[k, 0:7] for k in range(8)], first, sign))
    for b in (1, 2, 3):
        total, differ = [], []
        for k in range(8):
            t = np.pi * k / NZ
            at, end = 7 * b, 7 * (7 - b)
            v, w = v_ref[k, at : at + 7], v_ref[k, end : end + 7]
            total.append(turned(v, sign, -t, HALF) if k else HALF * v)
            differ.append(turned(w, sign, -t - np.pi / 2, HALF) if k else -HALF * w)
        total, differ = span_elements(total, first, sign), span_elements(differ, first, sign)
        store(b, [p + q for p, q in zip(total, differ)])
        store(7 - b, [p - q for p, q in zip(total, differ)])


def line_modes(x):
    n = len(x)
    if n == 1:
        return [(x[0], None)]
    even, odd = line_modes(x[0::2]), line_modes(x[1::2])
    out = [None] * (n // 2 + 1)
    out[0], out[n // 2] = (even[0][0] + odd[0][0], None), (even[0][0] - odd[0][0], None)
    for k in range(1, n // 4 + 1):
        (p, q), (v, w) = even[k], odd[k]
        if 4 * k == n:
            out[k] = (p, -v)
            continue
        c, s = float(np.cos(2 * np.pi * k / n)), float(np.sin(2 * np.pi * k / n))
        re, im = c * v + s * w, c * w - s * v
        out[k], out[n // 2 - k] = (p + re, q + im), (p - re, im - q)
    return out


def line_elements(modes, n):
    if n == 1:
        return [modes[0][0]]
    even, odd = [None] * (n // 4 + 1), [None] * (n // 4 + 1)
    low, high = modes[0][0], modes[n // 2][0]
    even[0], odd[0] = (low + high, None), (low - high, None)
    for k in range(1, n // 4 + 1):
        (p, q), (v, w) = modes[k], modes[n // 2 - k]
        if 4 * k == n:
            even[k], odd[k] = (2.0 * p, None), (-2.0 * q, None)
            continue
        c, s = float(np.cos(2 * np.pi * k / n)), float(np.sin(2 * np.pi * k / n))
        re, im = p - v, q + w
        even[k], odd[k] = (p + v, q - w), (c * re - s * im, c * im + s * re)
    x, y = line_elements(even, n // 2), line_elements(odd, n // 2)
    return [v for pair in zip(x, y) for v in pair]


def slab(ref, n):
    return ref[n * SLAB : n * SLAB + SLAB, :]


def flow_forward_kernel(x_ref, o_ref):
    modes = line_modes([slab(x_ref, n) for n in range(NX)])
    for n in range(16):
        re, im = modes[n][0], modes[n][1] if n else modes[16][0]
        o_ref[26 * n : 26 * n + 13, :] = re
        o_ref[26 * n + 13 : 26 * n + 26, :] = im


def flow_backward_kernel(x_ref, o_ref):
    modes = [(slab(x_ref, 2 * n), slab(x_ref, 2 * n + 1)) for n in range(16)]
    modes = [(modes[0][0], None)] + modes[1:] + [(modes[0][1], None)]
    for n, v in enumerate(line_elements(modes, NX)):
        o_ref[n * SLAB : n * SLAB + SLAB, :] = v


def table_product(v, t_ref):
    both = dot(jnp.concatenate(halves(v), axis=1), t_ref[...])
    return both[:, :128] + both[:, 128:]


def store_table(t_ref, table):
    high, low = halves(table)
    t_ref[0:128, 0:128] = high
    t_ref[128:256, 0:128] = high
    t_ref[0:128, 128:256] = low
    t_ref[128:256, 128:256] = jnp.zeros((128, 128), bf16)


def roll_up(v):
    return pltpu.roll(v, ROWS - 1, axis=0)


def roll_down(v):
    return pltpu.roll(v, 1, axis=0)


def wall_apply(s, q, planes, g):
    parts = [g * p for p in planes] + [g * roll_up(planes[0])]
    n = q + 1
    half = n // 2
    even = [parts[l] + parts[q - l] for l in range(half)]
    odd = [parts[l] - parts[q - l] for l in range(half)]
    out = [None] * n
    for k in range(half):
        p = m = None
        for l in range(half):
            ce = 0.5 * (s[k, l] + s[k, q - l])
            co = 0.5 * (s[k, l] - s[k, q - l])
            te, to = float(ce) * even[l], float(co) * odd[l]
            p = te if p is None else p + te
            m = to if m is None else m + to
        out[k] = p + m
        out[q - k] = p - m
    out[0] = out[0] + roll_down(out[q])
    return out[:q]


def weighted_sum(coefs, planes):
    total = None
    for c, v in zip(coefs, planes):
        c = float(c)
        if c == 0.0:
            continue
        t = v if c == 1.0 else c * v
        total = t if total is None else total + t
    return total


def restrict_wall(j, fine, coarse, planes):
    out = [weighted_sum(j[:fine, c], planes) for c in range(coarse)]
    out[0] = out[0] + roll_down(weighted_sum(j[:fine, coarse], planes))
    return out


def prolong_wall(j, fine, coarse, planes):
    closed = list(planes) + [roll_up(planes[0])]
    return [weighted_sum(j[k], closed) for k in range(fine)]


PIECES = [(y, half, part) for y in range(2) for half in range(2) for part in range(2)]


def cycle_kernel(
    h_ref, mats_ref, in_ref, out_ref,
    w_ref, geo_ref,
    u7, r7, x7, d7, u3, r3, x3, d3,
    square, g7_ref, g3_ref, r7_ref, p7_ref, r3_ref, p3_ref,
):
    at_x = PHASES_AT + 2 * lax.axis_index(LAST)
    at_z = PHASES_AT + 32 + 3 * lax.axis_index(("zh", "xh", "z0"))
    cx, sx = mats_ref[pl.ds(at_x, 1), :], mats_ref[pl.ds(at_x + 1, 1), :]
    ch, sh, cz = (mats_ref[pl.ds(at_z + n, 1), :] for n in range(3))
    lane = lax.broadcasted_iota(jnp.int32, (1, 128), 1)
    first = lane < 64
    mass7, inv7, ratio7, mask7 = (mats_ref[n : n + 1, :] for n in range(LANES_AT, LANES_AT + 4))
    mass3, inv3, ratio3, mask3 = (mats_ref[n : n + 1, :] for n in range(LANES_AT + 4, LANES_AT + 8))
    mask1 = mats_ref[LANES_AT + 8 : LANES_AT + 9, :]

    both = (cx, sx)
    alone = lambda c: (c, jnp.zeros_like(c))
    operator = [both, alone(ch), alone(sh), alone(cz)]
    transfer = [both, alone(ch), (cx * ch, sx * ch), alone(sh), (cx * sh, sx * sh)]

    def mode_table(at, rows, phases):
        top = mats_ref[at : at + rows]
        low = pltpu.roll(top, 64, axis=1)
        for c, s in phases:
            at += rows
            t = mats_ref[at : at + rows]
            top = top + jnp.where(first, c, s) * t
            low = low + jnp.where(first, -s, c) * pltpu.roll(t, 64, axis=1)
        if rows == 64:
            return jnp.concatenate([top, low], axis=0)
        square[...] = jnp.zeros((128, 128), f32)
        square[0:rows] = top
        square[64 : 64 + rows] = low
        return square[...]

    store_table(g7_ref, mode_table(G7_AT, 64, operator))
    store_table(g3_ref, mode_table(G3_AT, 24, operator))
    table = mode_table(P7_AT, 24, transfer)
    store_table(p7_ref, table)
    store_table(r7_ref, (table * mass7).T * inv3)
    table = mode_table(P3_AT, 8, transfer)
    store_table(p3_ref, table)
    store_table(r3_ref, (table * mass3).T)

    scale = inv7 * (1.0 / (NX * NZ))
    outer = lane % 64 < 32
    square[...] = jnp.zeros((128, 128), f32)
    for t in range(4):
        for y, half, part in PIECES:
            r, v = 64 * part + 32 * y + 13 * half, 52 * (2 * t + y) + 26 * half + 13 * part
            square[r : r + 13, :] = in_ref[v : v + 13, :]
        both = square[...].T
        low, high = both[:64], both[64:]
        w_ref[128 * t : 128 * t + 64, :] = jnp.where(outer, low, pltpu.roll(high, 32, axis=1)) * scale
        w_ref[128 * t + 64 : 128 * t + 128, :] = jnp.where(outer, pltpu.roll(low, 96, axis=1), high) * scale
    w_ref[512:, :] = jnp.zeros((w_ref.shape[0] - 512, 128), f32)
    for k in range(7):
        r7[k] = float(1.0 / FINE.weight[k]) * w_ref[pl.ds(k, ROWS, stride=7), :]

    h = h_ref[...]
    row = lax.broadcasted_iota(jnp.int32, (ROWS, 128), 0)
    g = jnp.where(row < NY, 2.0 / jnp.where(row < NY, h, 1.0), 0.0)
    h_pair = h + roll_down(h)
    g_pair = g + roll_down(g)
    geo_ref[0] = h
    geo_ref[1] = g
    geo_ref[2] = h_pair

    def height(k):
        return geo_ref[0 if k else 2]

    def inverse_diag(level, ratio, mask, k):
        d = height(k) * ratio + float(level.stiff[k, k]) * (g if k else g_pair)
        return jnp.where(d > 0.0, mask / jnp.where(d > 0.0, d, 1.0), 0.0)

    for k in range(7):
        d7[k] = inverse_diag(FINE, ratio7, mask7, k)
    for k in range(3):
        d3[k] = inverse_diag(MID, ratio3, mask3, k)
    d1_mix = ((4.0 + screen_shift) - 2.0 * cx - 2.0 * cz) * mask1
    d1 = inverse_diag(LOW, 4.0 + screen_shift, mask1, 0)

    def apply(level, u, table):
        q = level.q
        m = table_product(u[...].reshape(q * ROWS, 128), table)
        wall = wall_apply(level.stiff, q, [u[k] for k in range(q)], geo_ref[1])
        return [height(k) * m[k * ROWS : (k + 1) * ROWS] + wall[k] for k in range(q)]

    def smooth(level, u, r, x, d, table, fresh, keep_residual):
        q = level.q
        start, steps = cheb_steps(level.bound, SMOOTH_STEPS, smooth_floor)
        for k in range(q):
            t = start * (d[k] * r[k])
            u[k] = t
            x[k] = t if fresh else x[k] + t
        for alpha, beta in steps:
            au = apply(level, u, table)
            for k in range(q):
                t = r[k] - au[k]
                r[k] = t
                t = alpha * u[k] + beta * (d[k] * t)
                u[k] = t
                x[k] = x[k] + t
        if keep_residual:
            au = apply(level, u, table)
            for k in range(q):
                r[k] = r[k] - au[k]

    def product(planes, table):
        m = table_product(jnp.concatenate(planes, axis=0), table)
        return [m[k * ROWS : (k + 1) * ROWS] for k in range(len(planes))]

    smooth(FINE, u7, r7, x7, d7, g7_ref, True, True)
    down = product(restrict_wall(R7, 7, 3, [r7[k] for k in range(7)]), r7_ref)
    for k in range(3):
        r3[k] = down[k]

    smooth(MID, u3, r3, x3, d3, g3_ref, True, True)
    r1 = product(restrict_wall(R3, 3, 1, [r3[k] for k in range(3)]), r3_ref)[0]

    start, steps = cheb_steps(LOW.bound, COARSE_STEPS, coarse_floor)
    my1 = height(0) * d1_mix
    u1 = start * (d1 * r1)
    x1 = u1
    for alpha, beta in steps:
        flow = g * (u1 - roll_up(u1))
        r1 = r1 - (my1 * u1 + (flow - roll_down(flow)))
        u1 = alpha * u1 + beta * (d1 * r1)
        x1 = x1 + u1

    up = prolong_wall(J3, 3, 1, product([x1], p3_ref))
    for k in range(3):
        u3[k] = up[k]
        x3[k] = x3[k] + up[k]
    au = apply(MID, u3, g3_ref)
    for k in range(3):
        r3[k] = r3[k] - au[k]
    smooth(MID, u3, r3, x3, d3, g3_ref, False, False)

    up = prolong_wall(J7, 7, 3, product([x3[k] for k in range(3)], p7_ref))
    for k in range(7):
        u7[k] = up[k]
        x7[k] = x7[k] + up[k]
    au = apply(FINE, u7, g7_ref)
    for k in range(7):
        r7[k] = r7[k] - au[k]
    smooth(FINE, u7, r7, x7, d7, g7_ref, False, False)

    for k in range(7):
        w_ref[pl.ds(k, ROWS, stride=7), :] = x7[k]
    for t in range(4):
        low, high = w_ref[128 * t : 128 * t + 64, :], w_ref[128 * t + 64 : 128 * t + 128, :]
        square[...] = jnp.concatenate(
            [
                jnp.where(outer, low, pltpu.roll(high, 32, axis=1)),
                jnp.where(outer, pltpu.roll(low, 96, axis=1), high),
            ],
            axis=0,
        ).T
        for y, half, part in PIECES:
            r, v = 64 * part + 32 * y + 13 * half, 52 * (2 * t + y) + 26 * half + 13 * part
            out_ref[v : v + 13, :] = square[r : r + 13, :]


VMEM = pl.BlockSpec(memory_space=pltpu.VMEM)
HBM = pl.BlockSpec(memory_space=pltpu.HBM)
PARAMS = pltpu.CompilerParams(vmem_limit_bytes=32 * 1024 * 1024)
FLAT = jax.ShapeDtypeStruct((FIELD, 128), f32)
TIGHT = jax.ShapeDtypeStruct((USED, 128), f32)
LINES = [pltpu.VMEM((8, 56, 128), f32)]


def exchange(block, axes):
    n, rows = lax.axis_size(axes), block.shape[0]
    block = block.reshape(n, rows // n, 1, 128)
    return lax.all_to_all(block, axes, 0, 0).reshape(rows, 128)


def cycle_call(heights, modes):
    fine = pltpu.VMEM((7, ROWS, 128), f32)
    mid = pltpu.VMEM((3, ROWS, 128), f32)
    table = pltpu.VMEM((256, 256), bf16)
    return pl.pallas_call(
        cycle_kernel, out_shape=FLAT,
        in_specs=[VMEM, VMEM, VMEM], out_specs=VMEM,
        scratch_shapes=[
            pltpu.VMEM((7 * ROWS, 128), f32), mid,
            fine, fine, fine, fine, mid, mid, mid, mid,
            pltpu.VMEM((128, 128), f32), table, table, table, table, table, table,
        ],
        compiler_params=PARAMS,
    )(
        heights, jnp.asarray(MATRICES), modes,
    )


def transform(kernel, block, out_shape=FLAT, scratch=()):
    return pl.pallas_call(
        kernel, out_shape=out_shape, in_specs=[VMEM], out_specs=VMEM,
        scratch_shapes=scratch, compiler_params=PARAMS,
    )(block)


def body(residual, layer_heights):
    stay = lambda v: pltpu.with_memory_space_constraint(v, pltpu.HBM)
    packed, heights = pl.pallas_call(
        pack_kernel, out_shape=(TIGHT, jax.ShapeDtypeStruct((ROWS, 128), f32)),
        in_specs=[HBM, HBM], out_specs=(VMEM, VMEM),
        scratch_shapes=[
            pltpu.VMEM((7, 14, 512), f32), pltpu.VMEM((1, NY), f32), pltpu.VMEM((8, 128), f32),
            pltpu.SemaphoreType.DMA((2,)),
        ],
        compiler_params=PARAMS,
    )(stay(residual), stay(layer_heights.reshape(1, NY)))
    spans = transform(span_forward_kernel, exchange(packed, SPAN), scratch=LINES)
    modes = exchange(transform(flow_forward_kernel, exchange(spans, FLOW)), LAST)
    solved = exchange(cycle_call(heights, modes), LAST)
    flows = exchange(transform(flow_backward_kernel, solved), FLOW)
    spread = exchange(transform(span_backward_kernel, flows, TIGHT, LINES), SPAN)
    return pl.pallas_call(
        unpack_kernel, out_shape=jax.ShapeDtypeStruct((7, 14, 512), f32),
        in_specs=[VMEM], out_specs=VMEM, compiler_params=PARAMS,
    )(spread)


def solution(mesh):
    split = Mesh(mesh.devices.reshape(4, 2, 2, 2, 2, 4), FLOW + SPAN)
    spec = P(FLOW, SPAN, None)
    return jax.shard_map(
        body, mesh=split, in_specs=(spec, P()), out_specs=spec, check_vma=False
    )
```

```python
import jax
import jax.numpy as jnp
import ml_dtypes
import numpy as np
from jax import lax
from jax.experimental import pallas as pl
from jax.experimental.pallas import tpu as pltpu
from jax.sharding import Mesh
from jax.sharding import PartitionSpec as P


SMOOTH_STEPS = 3
COARSE_STEPS = 12
NX, NZ, NY = 32, 16, 73
DEVICES = 256
ROWS = 80
screen_shift = 0.02
smooth_floor = 0.1
coarse_floor = 0.01
f32 = jnp.float32
bf16 = jnp.bfloat16


def legendre_values(points, degree):
    columns = [np.ones(points.shape), points]
    for n in range(2, degree + 1):
        columns.append(((2 * n - 1) * points * columns[-1] - (n - 1) * columns[-2]) / n)
    return np.stack(columns[: degree + 1], axis=1)


def gll_tables(degree):
    nodes = -np.cos(np.pi * np.arange(degree + 1) / degree)
    for _ in range(100):
        values = legendre_values(nodes, degree)
        nodes = nodes - (nodes * values[:, degree] - values[:, degree - 1]) / (
            (degree + 1) * values[:, degree]
        )
    leading = legendre_values(nodes, degree)[:, degree]
    weights = 2.0 / (degree * (degree + 1) * leading**2)
    differ = np.zeros((degree + 1, degree + 1))
    for i in range(degree + 1):
        for j in range(degree + 1):
            if i != j:
                differ[i, j] = leading[i] / (leading[j] * (nodes[i] - nodes[j]))
    differ[0, 0] = -degree * (degree + 1) / 4.0
    differ[degree, degree] = degree * (degree + 1) / 4.0
    return nodes, weights, differ.T @ (weights[:, None] * differ)


def interp_table(fine_degree, coarse_degree):
    fine_nodes = gll_tables(fine_degree)[0]
    coarse_nodes = gll_tables(coarse_degree)[0]
    lagrange = np.ones((fine_degree + 1, coarse_degree + 1))
    for col in range(coarse_degree + 1):
        for other in range(coarse_degree + 1):
            if other != col:
                lagrange[:, col] *= (fine_nodes - coarse_nodes[other]) / (
                    coarse_nodes[col] - coarse_nodes[other]
                )
    return lagrange


def lane_at(a, b):
    n = 7 * b + a
    return n if n < 25 else n + 7


def lanes_of(values):
    n = values.shape[0]
    out = np.zeros(64)
    for a in range(n):
        for b in range(n):
            out[lane_at(a, b)] = values[a, b]
    return out


def square_of(matrix, n_out, n_in):
    rows = [lane_at(a, b) for a in range(n_out) for b in range(n_out)]
    columns = [lane_at(a, b) for a in range(n_in) for b in range(n_in)]
    out = np.zeros((64, 64))
    out[np.ix_(rows, columns)] = matrix
    return out


def line_basis(q, t):
    u = np.zeros((q, q), complex)
    u[0, 0] = 1.0
    turn = np.exp(-0.5j * t) / np.sqrt(2.0)
    for a in range(1, (q + 1) // 2):
        u[a, a] = u[a, q - a] = turn
        u[q - a, a], u[q - a, q - a] = -1j * turn, 1j * turn
    return u


def closing(q, t):
    out = np.eye(q + 1, q, dtype=complex)
    out[q, 0] = np.exp(1j * t)
    return out


def real_parts(matrix_of, count):
    angles = 0.3 + 0.7 * np.arange(8)
    terms = np.stack([np.ones(8), np.cos(angles / 2), np.sin(angles / 2), np.cos(angles)], 1)[:, :count]
    values = np.stack([matrix_of(t) for t in angles])
    flat = values.reshape(8, -1)
    parts = np.linalg.lstsq(terms, flat.real, rcond=None)[0]
    assert np.abs(terms @ parts - flat).max() < 1e-11 * np.abs(flat).max()
    return parts.reshape((count,) + values.shape[1:])


class Level:
    def __init__(self, q):
        self.q = q
        _, w, s = gll_tables(q)
        self.w, self.s = w, s
        mass = 0.5 * w[:q].copy()
        mass[0] = 0.5 * (w[0] + w[q])
        diag = 2.0 * np.diag(s)[:q].copy()
        diag[0] = 2.0 * (s[0, 0] + s[q, q])
        self.mxz = np.outer(mass, mass)
        a = np.outer(diag, mass) + np.outer(mass, diag) + screen_shift * self.mxz
        self.ratio = lanes_of(a / self.mxz)
        spread = np.abs(s).sum(axis=1)
        self.bound = max(1.0, float(np.max(spread / np.diag(s))))
        base = 2.0 * s[:q, :q].copy()
        base[0, 0] += 2.0 * s[q, q]
        e1 = np.zeros((q, q))
        e1[:, 0] = 2.0 * s[:q, q]
        even, odd = e1 + e1.T, e1 - e1.T
        dm = np.diag(mass)
        scale = np.concatenate([lanes_of(1.0 / self.mxz)] * 2)[None, :]
        sq = lambda m: square_of(m, q, q)
        span = real_parts(
            lambda t: line_basis(q, t) @ closing(q, t).conj().T @ (2.0 * s) @ closing(q, t) @ line_basis(q, t).conj().T, 4
        )
        fixed = sq(np.kron(base, dm) + np.kron(dm, span[0]) + screen_shift * np.kron(dm, dm))
        tables = [np.hstack([fixed, 0.0 * fixed])]
        tables.append(np.hstack([sq(np.kron(even, dm)), -sq(np.kron(odd, dm))]))
        for part in span[1:]:
            part = sq(np.kron(dm, part))
            tables.append(np.hstack([part, 0.0 * part]))
        self.tables = [(t * scale)[: 64 if q > 3 else 24] for t in tables]
        self.weight = 0.5 * w
        self.stiff = s / self.weight[:, None]
        self.mass_lanes = np.concatenate([lanes_of(self.mxz)] * 2)
        self.inv_mass_lanes = np.concatenate([lanes_of(1.0 / self.mxz)] * 2)
        self.ratio_lanes = np.concatenate([self.ratio] * 2)
        self.mask_lanes = (self.mass_lanes > 0).astype(np.float64)


def transfer_tables(fine, coarse):
    j = interp_table(fine, coarse)
    ja = j[:fine, :coarse]
    jb = np.zeros((fine, coarse))
    jb[:, 0] = j[:fine, coarse]
    span = real_parts(
        lambda t: line_basis(fine, t) @ j[:fine] @ closing(coarse, t) @ line_basis(coarse, t).conj().T, 3
    )
    tables = []
    for part in span:
        for flow in (ja, jb):
            b = square_of(np.kron(flow, part), fine, coarse).T[: 24 if coarse > 1 else 8]
            tables.append(np.hstack([b, b if flow is jb else 0.0 * b]))
    return j, tables


def phase_rows():
    rows = np.zeros((80, 2, 64))
    for n in range(16):
        t = 2 * np.pi * n / NX
        if n:
            rows[2 * n], rows[2 * n + 1] = np.cos(t), np.sin(t)
        else:
            rows[0, 0], rows[0, 1] = 1.0, -1.0
    for k in range(8):
        for part in range(2):
            t = 2 * np.pi * k / NZ if k else np.pi * part
            at = 32 + 3 * (2 * k + part)
            rows[at], rows[at + 1], rows[at + 2] = np.cos(t / 2), np.sin(t / 2), np.cos(t)
    return rows.reshape(80, 128)


FINE, MID, LOW = Level(7), Level(3), Level(1)
J7, P7_TABLES = transfer_tables(7, 3)
J3, P3_TABLES = transfer_tables(3, 1)
MATRICES = np.concatenate(FINE.tables + MID.tables + P7_TABLES + P3_TABLES).astype(np.float32)
R7 = FINE.weight[:, None] * J7 / MID.weight
R3 = MID.weight[:, None] * J3 / LOW.weight
G7_AT, G3_AT, P7_AT, P3_AT = 0, 320, 440, 584


LANES = np.zeros((16, 128))
for n, level in enumerate((FINE, MID)):
    LANES[4 * n] = level.mass_lanes
    LANES[4 * n + 1] = level.inv_mass_lanes
    LANES[4 * n + 2] = level.ratio_lanes
    LANES[4 * n + 3] = level.mask_lanes
LANES[8] = LOW.mask_lanes
MATRICES = np.concatenate([MATRICES, LANES, phase_rows()]).astype(np.float32)
LANES_AT, PHASES_AT = 632, 648


def cheb_steps(bound, sweeps, floor):
    centre = bound * (1.0 + floor) / 2.0
    half = bound * (1.0 - floor) / 2.0
    s = centre / half
    p = 1.0 / s
    steps = []
    for _ in range(sweeps - 1):
        p_next = 1.0 / (2.0 * s - p)
        steps.append((p_next * p, 2.0 * p_next / half))
        p = p_next
    return 1.0 / centre, steps


FLOW, SPAN = ("zh", "z0", "xh", "core"), ("xl", "y")
LAST = ("xl", "y", "core")
USED = 8 * 49
SLAB = 13
FIELD = 32 * SLAB


def swap(v):
    return pltpu.roll(v, 64, axis=1)


def mix(first, v, w):
    return jnp.where(first, v, swap(w)), jnp.where(first, swap(v), w)


def pack_kernel(x_hbm, h_hbm, o_ref, rows_ref, x_ref, h_ref, line_ref, sems):
    line = pltpu.make_async_copy(h_hbm, h_ref, sems.at[0])
    line.start()
    field = pltpu.make_async_copy(x_hbm, x_ref, sems.at[1])
    field.start()
    first, _ = lane_tools()
    line_ref[...] = jnp.zeros_like(line_ref)
    line.wait()
    line_ref[0:1, 0:NY] = h_ref[...]
    rows_ref[...] = jnp.broadcast_to(line_ref[0:1, :], (128, 128)).T[:ROWS]
    field.wait()
    for a in range(7):
        for t in range(4):
            part = slice(128 * t, 128 * t + 128)
            low, high = mix(first, x_ref[a, 0:7, part], x_ref[a, 7:14, part])
            o_ref[pl.ds(98 * t + a, 7, stride=7), :] = low
            o_ref[pl.ds(98 * t + 49 + a, 7, stride=7), :] = high


def unpack_kernel(x_ref, o_ref):
    first, _ = lane_tools()
    for a in range(7):
        for t in range(4):
            part = slice(128 * t, 128 * t + 128)
            low, high = mix(
                first,
                x_ref[pl.ds(98 * t + a, 7, stride=7), :],
                x_ref[pl.ds(98 * t + 49 + a, 7, stride=7), :],
            )
            o_ref[a, 0:7, part] = low
            o_ref[a, 7:14, part] = high


def halves(v):
    high = v.astype(bf16)
    return high, (v - high.astype(f32)).astype(bf16)


def dot(a, b):
    return jnp.dot(a, b, preferred_element_type=f32)


HALF = float(np.sqrt(0.5))


def lane_tools():
    first = lax.broadcasted_iota(jnp.int32, (1, 128), 1) < 64
    return first, jnp.where(first, 1.0, -1.0).astype(f32)


def span_modes(x, first, sign, offset, size):
    s = [None] + [x[j] + x[8 - j] for j in (1, 2, 3)]
    d = [None] + [x[j] - x[8 - j] for j in (1, 2, 3)]
    up, down = x[0] + x[4], x[0] - x[4]
    odd, turn = s[1] + s[3], HALF * (s[1] - s[3])
    slope = HALF * (d[1] + d[3])
    re = [up + s[2] + odd, down + turn, up - s[2], down - turn, up + s[2] - odd]
    im = [None, -slope - d[2], d[3] - d[1], d[2] - slope]

    def phases(k):
        t = np.pi * k / 8
        p = 0.0 if offset is None else t / 2 + offset
        return [float(size * v) for v in (np.cos(p), np.sin(p), np.cos(p + t), np.sin(p + t))]

    flip = swap(re[0])
    out = [None] * 8
    out[0] = jnp.where(first, re[0] + flip, flip - re[0])
    c, s, v, w = phases(4)
    out[4] = jnp.where(first, c, -w) * re[4] + jnp.where(first, v, -s) * swap(re[4])
    for f in (1, 2, 3):
        re_swap, im_swap = swap(re[f]), swap(im[f])
        a = jnp.where(first, re[f], im_swap)
        b = jnp.where(first, im[f], -re_swap)
        p = jnp.where(first, re_swap, im[f])
        q = jnp.where(first, im_swap, -re[f])
        c, s, v, w = phases(f)
        out[f] = (c * a + v * p) + (s * b + w * q)
        c, s, v, w = phases(8 - f)
        out[8 - f] = sign * ((c * a + v * p) - (s * b + w * q))
    return out


def span_elements(x, first, sign, offset, size):
    def phases(k):
        t = np.pi * k / 8
        p = 0.0 if offset is None else t / 2 + offset
        return [float(size * v) for v in (np.cos(p), np.sin(p), np.cos(p + t), np.sin(p + t))]

    pick = lambda p, q: jnp.where(first, p, q)
    flip = swap(x[0])
    re = [jnp.where(first, x[0] + flip, flip - x[0])]
    im = [None]
    for f in (1, 2, 3):
        c, s, v, w = [2.0 * n for n in phases(f)]
        near, near_swap = x[f], swap(x[f])
        one = pick(c, -w) * near + pick(-s, v) * near_swap
        two = pick(s, v) * near + pick(c, w) * near_swap
        c, s, v, w = [2.0 * n for n in phases(8 - f)]
        far, far_swap = x[8 - f], swap(x[8 - f])
        re.append(one + (pick(c, -w) * far + pick(-s, v) * far_swap))
        im.append(two - (pick(s, v) * far + pick(c, w) * far_swap))
    c, s, v, w = [2.0 * n for n in phases(4)]
    re.append(pick(c, -w) * x[4] + pick(-s, v) * swap(x[4]))
    up, down = re[0] + re[4], re[0] - re[4]
    odd, turn = re[1] + re[3], HALF * (re[1] - re[3])
    slope = HALF * (im[1] + im[3])
    c = [up + re[2] + odd, down + turn, up - re[2], down - turn, up + re[2] - odd]
    s = [None, slope + im[2], im[1] - im[3], slope - im[2]]
    return [c[0]] + [c[j] - s[j] for j in (1, 2, 3)] + [c[4]] + [c[j] + s[j] for j in (3, 2, 1)]


def mode_rows(k, part):
    return 26 * (4 * (k // 2) + 2 * part + k % 2)


def span_forward_kernel(x_ref, o_ref, v_ref):
    first, sign = lane_tools()
    for k in range(8):
        v_ref[k, 48:56] = jnp.zeros((8, 128), f32)
    nodes = lambda b: [x_ref[49 * j + 7 * b : 49 * j + 7 * b + 7, :] for j in range(8)]
    for k, v in enumerate(span_modes(nodes(0), first, sign, None, 1.0)):
        v_ref[k, 0:7] = v
    for b in (1, 2, 3):
        near, far = nodes(b), nodes(7 - b)
        total = span_modes([p + q for p, q in zip(near, far)], first, sign, 0.0, HALF)
        differ = span_modes([p - q for p, q in zip(near, far)], first, sign, np.pi / 2, HALF)
        total[0], differ[0] = HALF * total[0], -HALF * differ[0]
        for k in range(8):
            v_ref[k, 7 * b : 7 * b + 7] = total[k]
            v_ref[k, 7 * (7 - b) : 7 * (7 - b) + 7] = differ[k]
    for k in range(8):
        re, im = mix(first, v_ref[k, 0:26], v_ref[k, 25:51])
        o_ref[mode_rows(k, 0) : mode_rows(k, 0) + 26, :] = re
        o_ref[mode_rows(k, 1) : mode_rows(k, 1) + 26, :] = im


def span_backward_kernel(x_ref, o_ref, v_ref):
    first, sign = lane_tools()
    for k in range(8):
        near, far = mix(
            first,
            x_ref[mode_rows(k, 0) : mode_rows(k, 0) + 26, :],
            x_ref[mode_rows(k, 1) : mode_rows(k, 1) + 26, :],
        )
        v_ref[k, 0:25] = near[0:25]
        v_ref[k, 25:49] = far[0:24]

    def store(b, planes):
        for j, v in enumerate(planes):
            o_ref[49 * j + 7 * b : 49 * j + 7 * b + 7, :] = v

    store(0, span_elements([v_ref[k, 0:7] for k in range(8)], first, sign, None, 1.0))
    for b in (1, 2, 3):
        total = [v_ref[k, 7 * b : 7 * b + 7] for k in range(8)]
        differ = [v_ref[k, 7 * (7 - b) : 7 * (7 - b) + 7] for k in range(8)]
        total[0], differ[0] = HALF * total[0], -HALF * differ[0]
        total = span_elements(total, first, sign, 0.0, HALF)
        differ = span_elements(differ, first, sign, np.pi / 2, HALF)
        store(b, [p + q for p, q in zip(total, differ)])
        store(7 - b, [p - q for p, q in zip(total, differ)])


def line_modes(x):
    n = len(x)
    if n == 1:
        return [(x[0], None)]
    even, odd = line_modes(x[0::2]), line_modes(x[1::2])
    out = [None] * (n // 2 + 1)
    out[0], out[n // 2] = (even[0][0] + odd[0][0], None), (even[0][0] - odd[0][0], None)
    for k in range(1, n // 4 + 1):
        (p, q), (v, w) = even[k], odd[k]
        if 4 * k == n:
            out[k] = (p, -v)
            continue
        c, s = float(np.cos(2 * np.pi * k / n)), float(np.sin(2 * np.pi * k / n))
        re, im = c * v + s * w, c * w - s * v
        out[k], out[n // 2 - k] = (p + re, q + im), (p - re, im - q)
    return out


def line_elements(modes, n):
    if n == 1:
        return [modes[0][0]]
    even, odd = [None] * (n // 4 + 1), [None] * (n // 4 + 1)
    low, high = modes[0][0], modes[n // 2][0]
    even[0], odd[0] = (low + high, None), (low - high, None)
    for k in range(1, n // 4 + 1):
        (p, q), (v, w) = modes[k], modes[n // 2 - k]
        if 4 * k == n:
            even[k], odd[k] = (2.0 * p, None), (-2.0 * q, None)
            continue
        c, s = float(np.cos(2 * np.pi * k / n)), float(np.sin(2 * np.pi * k / n))
        re, im = p - v, q + w
        even[k], odd[k] = (p + v, q - w), (c * re - s * im, c * im + s * re)
    x, y = line_elements(even, n // 2), line_elements(odd, n // 2)
    return [v for pair in zip(x, y) for v in pair]


def slab(ref, n):
    return ref[n * SLAB : n * SLAB + SLAB, :]


def flow_forward_kernel(x_ref, o_ref):
    modes = line_modes([slab(x_ref, n) for n in range(NX)])
    for n in range(16):
        re, im = modes[n][0], modes[n][1] if n else modes[16][0]
        o_ref[26 * n : 26 * n + 13, :] = re
        o_ref[26 * n + 13 : 26 * n + 26, :] = im


def flow_backward_kernel(x_ref, o_ref):
    modes = [(slab(x_ref, 2 * n), slab(x_ref, 2 * n + 1)) for n in range(16)]
    modes = [(modes[0][0], None)] + modes[1:] + [(modes[0][1], None)]
    for n, v in enumerate(line_elements(modes, NX)):
        o_ref[n * SLAB : n * SLAB + SLAB, :] = v


def table_product(v, t_ref):
    both = dot(jnp.concatenate(halves(v), axis=1), t_ref[...])
    return both[:, :128] + both[:, 128:]


def store_table(t_ref, table):
    high, low = halves(table)
    t_ref[0:128, 0:128] = high
    t_ref[128:256, 0:128] = high
    t_ref[0:128, 128:256] = low
    t_ref[128:256, 128:256] = jnp.zeros((128, 128), bf16)


def roll_up(v):
    return pltpu.roll(v, ROWS - 1, axis=0)


def roll_down(v):
    return pltpu.roll(v, 1, axis=0)


def wall_apply(s, q, planes, g):
    parts = [g * p for p in planes] + [g * roll_up(planes[0])]
    n = q + 1
    half = n // 2
    even = [parts[l] + parts[q - l] for l in range(half)]
    odd = [parts[l] - parts[q - l] for l in range(half)]
    out = [None] * n
    for k in range(half):
        p = m = None
        for l in range(half):
            ce = 0.5 * (s[k, l] + s[k, q - l])
            co = 0.5 * (s[k, l] - s[k, q - l])
            te, to = float(ce) * even[l], float(co) * odd[l]
            p = te if p is None else p + te
            m = to if m is None else m + to
        out[k] = p + m
        out[q - k] = p - m
    out[0] = out[0] + roll_down(out[q])
    return out[:q]


def weighted_sum(coefs, planes):
    total = None
    for c, v in zip(coefs, planes):
        c = float(c)
        if c == 0.0:
            continue
        t = v if c == 1.0 else c * v
        total = t if total is None else total + t
    return total


def restrict_wall(j, fine, coarse, planes):
    out = [weighted_sum(j[:fine, c], planes) for c in range(coarse)]
    out[0] = out[0] + roll_down(weighted_sum(j[:fine, coarse], planes))
    return out


def prolong_wall(j, fine, coarse, planes):
    closed = list(planes) + [roll_up(planes[0])]
    return [weighted_sum(j[k], closed) for k in range(fine)]


PIECES = [(y, half, part) for y in range(2) for half in range(2) for part in range(2)]


def cycle_kernel(
    h_ref, mats_ref, in_ref, out_ref,
    w_ref, geo_ref,
    u7, r7, x7, d7, u3, r3, x3, d3,
    square, g7_ref, g3_ref, r7_ref, p7_ref, r3_ref, p3_ref,
):
    at_x = PHASES_AT + 2 * lax.axis_index(LAST)
    at_z = PHASES_AT + 32 + 3 * lax.axis_index(("zh", "xh", "z0"))
    cx, sx = mats_ref[pl.ds(at_x, 1), :], mats_ref[pl.ds(at_x + 1, 1), :]
    ch, sh, cz = (mats_ref[pl.ds(at_z + n, 1), :] for n in range(3))
    lane = lax.broadcasted_iota(jnp.int32, (1, 128), 1)
    first = lane < 64
    mass7, inv7, ratio7, mask7 = (mats_ref[n : n + 1, :] for n in range(LANES_AT, LANES_AT + 4))
    mass3, inv3, ratio3, mask3 = (mats_ref[n : n + 1, :] for n in range(LANES_AT + 4, LANES_AT + 8))
    mask1 = mats_ref[LANES_AT + 8 : LANES_AT + 9, :]

    both = (cx, sx)
    alone = lambda c: (c, jnp.zeros_like(c))
    operator = [both, alone(ch), alone(sh), alone(cz)]
    transfer = [both, alone(ch), (cx * ch, sx * ch), alone(sh), (cx * sh, sx * sh)]

    def mode_table(at, rows, phases):
        top = mats_ref[at : at + rows]
        low = pltpu.roll(top, 64, axis=1)
        for c, s in phases:
            at += rows
            t = mats_ref[at : at + rows]
            top = top + jnp.where(first, c, s) * t
            low = low + jnp.where(first, -s, c) * pltpu.roll(t, 64, axis=1)
        if rows == 64:
            return jnp.concatenate([top, low], axis=0)
        square[...] = jnp.zeros((128, 128), f32)
        square[0:rows] = top
        square[64 : 64 + rows] = low
        return square[...]

    store_table(g7_ref, mode_table(G7_AT, 64, operator))
    store_table(g3_ref, mode_table(G3_AT, 24, operator))
    table = mode_table(P7_AT, 24, transfer)
    store_table(p7_ref, table)
    store_table(r7_ref, (table * mass7).T * inv3)
    table = mode_table(P3_AT, 8, transfer)
    store_table(p3_ref, table)
    store_table(r3_ref, (table * mass3).T)

    scale = inv7 * (1.0 / (NX * NZ))
    outer = lane % 64 < 32
    square[...] = jnp.zeros((128, 128), f32)
    for t in range(4):
        for y, half, part in PIECES:
            r, v = 64 * part + 32 * y + 13 * half, 52 * (2 * t + y) + 26 * half + 13 * part
            square[r : r + 13, :] = in_ref[v : v + 13, :]
        both = square[...].T
        low, high = both[:64], both[64:]
        w_ref[128 * t : 128 * t + 64, :] = jnp.where(outer, low, pltpu.roll(high, 32, axis=1)) * scale
        w_ref[128 * t + 64 : 128 * t + 128, :] = jnp.where(outer, pltpu.roll(low, 96, axis=1), high) * scale
    w_ref[512:, :] = jnp.zeros((w_ref.shape[0] - 512, 128), f32)
    for k in range(7):
        r7[k] = float(1.0 / FINE.weight[k]) * w_ref[pl.ds(k, ROWS, stride=7), :]

    h = h_ref[...]
    row = lax.broadcasted_iota(jnp.int32, (ROWS, 128), 0)
    g = jnp.where(row < NY, 2.0 / jnp.where(row < NY, h, 1.0), 0.0)
    h_pair = h + roll_down(h)
    g_pair = g + roll_down(g)
    geo_ref[0] = h
    geo_ref[1] = g
    geo_ref[2] = h_pair

    def height(k):
        return geo_ref[0 if k else 2]

    def inverse_diag(level, ratio, mask, k):
        d = height(k) * ratio + float(level.stiff[k, k]) * (g if k else g_pair)
        return jnp.where(d > 0.0, mask / jnp.where(d > 0.0, d, 1.0), 0.0)

    for k in range(7):
        d7[k] = inverse_diag(FINE, ratio7, mask7, k)
    for k in range(3):
        d3[k] = inverse_diag(MID, ratio3, mask3, k)
    d1_mix = ((4.0 + screen_shift) - 2.0 * cx - 2.0 * cz) * mask1
    d1 = inverse_diag(LOW, 4.0 + screen_shift, mask1, 0)

    def apply(level, u, table):
        q = level.q
        m = table_product(u[...].reshape(q * ROWS, 128), table)
        wall = wall_apply(level.stiff, q, [u[k] for k in range(q)], geo_ref[1])
        return [height(k) * m[k * ROWS : (k + 1) * ROWS] + wall[k] for k in range(q)]

    def smooth(level, u, r, x, d, table, fresh, keep_residual):
        q = level.q
        start, steps = cheb_steps(level.bound, SMOOTH_STEPS, smooth_floor)
        for k in range(q):
            t = start * (d[k] * r[k])
            u[k] = t
            x[k] = t if fresh else x[k] + t
        for alpha, beta in steps:
            au = apply(level, u, table)
            for k in range(q):
                t = r[k] - au[k]
                r[k] = t
                t = alpha * u[k] + beta * (d[k] * t)
                u[k] = t
                x[k] = x[k] + t
        if keep_residual:
            au = apply(level, u, table)
            for k in range(q):
                r[k] = r[k] - au[k]

    def product(planes, table):
        m = table_product(jnp.concatenate(planes, axis=0), table)
        return [m[k * ROWS : (k + 1) * ROWS] for k in range(len(planes))]

    smooth(FINE, u7, r7, x7, d7, g7_ref, True, True)
    down = product(restrict_wall(R7, 7, 3, [r7[k] for k in range(7)]), r7_ref)
    for k in range(3):
        r3[k] = down[k]

    smooth(MID, u3, r3, x3, d3, g3_ref, True, True)
    r1 = product(restrict_wall(R3, 3, 1, [r3[k] for k in range(3)]), r3_ref)[0]

    start, steps = cheb_steps(LOW.bound, COARSE_STEPS, coarse_floor)
    middle = d1 * (height(0) * d1_mix + g_pair)
    after, before = d1 * g, d1 * roll_down(g)
    r1 = d1 * r1
    u1 = start * r1
    x1 = u1
    for alpha, beta in steps:
        r1 = (r1 - middle * u1) + (after * roll_up(u1) + before * roll_down(u1))
        u1 = alpha * u1 + beta * r1
        x1 = x1 + u1

    up = prolong_wall(J3, 3, 1, product([x1], p3_ref))
    for k in range(3):
        u3[k] = up[k]
        x3[k] = x3[k] + up[k]
    au = apply(MID, u3, g3_ref)
    for k in range(3):
        r3[k] = r3[k] - au[k]
    smooth(MID, u3, r3, x3, d3, g3_ref, False, False)

    up = prolong_wall(J7, 7, 3, product([x3[k] for k in range(3)], p7_ref))
    for k in range(7):
        u7[k] = up[k]
        x7[k] = x7[k] + up[k]
    au = apply(FINE, u7, g7_ref)
    for k in range(7):
        r7[k] = r7[k] - au[k]
    smooth(FINE, u7, r7, x7, d7, g7_ref, False, False)

    for k in range(7):
        w_ref[pl.ds(k, ROWS, stride=7), :] = x7[k]
    for t in range(4):
        low, high = w_ref[128 * t : 128 * t + 64, :], w_ref[128 * t + 64 : 128 * t + 128, :]
        square[...] = jnp.concatenate(
            [
                jnp.where(outer, low, pltpu.roll(high, 32, axis=1)),
                jnp.where(outer, pltpu.roll(low, 96, axis=1), high),
            ],
            axis=0,
        ).T
        for y, half, part in PIECES:
            r, v = 64 * part + 32 * y + 13 * half, 52 * (2 * t + y) + 26 * half + 13 * part
            out_ref[v : v + 13, :] = square[r : r + 13, :]


VMEM = pl.BlockSpec(memory_space=pltpu.VMEM)
HBM = pl.BlockSpec(memory_space=pltpu.HBM)
PARAMS = pltpu.CompilerParams(vmem_limit_bytes=32 * 1024 * 1024)
FLAT = jax.ShapeDtypeStruct((FIELD, 128), f32)
TIGHT = jax.ShapeDtypeStruct((USED, 128), f32)
LINES = [pltpu.VMEM((8, 56, 128), f32)]


def exchange(block, axes):
    n, rows = lax.axis_size(axes), block.shape[0]
    block = block.reshape(n, rows // n, 1, 128)
    return lax.all_to_all(block, axes, 0, 0).reshape(rows, 128)


def cycle_call(heights, modes):
    fine = pltpu.VMEM((7, ROWS, 128), f32)
    mid = pltpu.VMEM((3, ROWS, 128), f32)
    table = pltpu.VMEM((256, 256), bf16)
    return pl.pallas_call(
        cycle_kernel, out_shape=FLAT,
        in_specs=[VMEM, VMEM, VMEM], out_specs=VMEM,
        scratch_shapes=[
            pltpu.VMEM((7 * ROWS, 128), f32), mid,
            fine, fine, fine, fine, mid, mid, mid, mid,
            pltpu.VMEM((128, 128), f32), table, table, table, table, table, table,
        ],
        compiler_params=PARAMS,
    )(
        heights, jnp.asarray(MATRICES), modes,
    )


def transform(kernel, block, out_shape=FLAT, scratch=()):
    return pl.pallas_call(
        kernel, out_shape=out_shape, in_specs=[VMEM], out_specs=VMEM,
        scratch_shapes=scratch, compiler_params=PARAMS,
    )(block)


def body(residual, layer_heights):
    stay = lambda v: pltpu.with_memory_space_constraint(v, pltpu.HBM)
    packed, heights = pl.pallas_call(
        pack_kernel, out_shape=(TIGHT, jax.ShapeDtypeStruct((ROWS, 128), f32)),
        in_specs=[HBM, HBM], out_specs=(VMEM, VMEM),
        scratch_shapes=[
            pltpu.VMEM((7, 14, 512), f32), pltpu.VMEM((1, NY), f32), pltpu.VMEM((8, 128), f32),
            pltpu.SemaphoreType.DMA((2,)),
        ],
        compiler_params=PARAMS,
    )(stay(residual), stay(layer_heights.reshape(1, NY)))
    spans = transform(span_forward_kernel, exchange(packed, SPAN), scratch=LINES)
    modes = exchange(transform(flow_forward_kernel, exchange(spans, FLOW)), LAST)
    solved = exchange(cycle_call(heights, modes), LAST)
    flows = exchange(transform(flow_backward_kernel, solved), FLOW)
    spread = exchange(transform(span_backward_kernel, flows, TIGHT, LINES), SPAN)
    return pl.pallas_call(
        unpack_kernel, out_shape=jax.ShapeDtypeStruct((7, 14, 512), f32),
        in_specs=[VMEM], out_specs=VMEM, compiler_params=PARAMS,
    )(spread)


def solution(mesh):
    split = Mesh(mesh.devices.reshape(4, 2, 2, 2, 2, 4), FLOW + SPAN)
    spec = P(FLOW, SPAN, None)
    return jax.shard_map(
        body, mesh=split, in_specs=(spec, P()), out_specs=spec, check_vma=False
    )
```

```python
import jax
import jax.numpy as jnp
import ml_dtypes
import numpy as np
from jax import lax
from jax.experimental import pallas as pl
from jax.experimental.pallas import tpu as pltpu
from jax.sharding import Mesh
from jax.sharding import PartitionSpec as P


SMOOTH_STEPS = 3
COARSE_STEPS = 12
NX, NZ, NY = 32, 16, 73
DEVICES = 256
ROWS = 80
screen_shift = 0.02
smooth_floor = 0.1
coarse_floor = 0.01
f32 = jnp.float32
bf16 = jnp.bfloat16


def legendre_values(points, degree):
    columns = [np.ones(points.shape), points]
    for n in range(2, degree + 1):
        columns.append(((2 * n - 1) * points * columns[-1] - (n - 1) * columns[-2]) / n)
    return np.stack(columns[: degree + 1], axis=1)


def gll_tables(degree):
    nodes = -np.cos(np.pi * np.arange(degree + 1) / degree)
    for _ in range(100):
        values = legendre_values(nodes, degree)
        nodes = nodes - (nodes * values[:, degree] - values[:, degree - 1]) / (
            (degree + 1) * values[:, degree]
        )
    leading = legendre_values(nodes, degree)[:, degree]
    weights = 2.0 / (degree * (degree + 1) * leading**2)
    differ = np.zeros((degree + 1, degree + 1))
    for i in range(degree + 1):
        for j in range(degree + 1):
            if i != j:
                differ[i, j] = leading[i] / (leading[j] * (nodes[i] - nodes[j]))
    differ[0, 0] = -degree * (degree + 1) / 4.0
    differ[degree, degree] = degree * (degree + 1) / 4.0
    return nodes, weights, differ.T @ (weights[:, None] * differ)


def interp_table(fine_degree, coarse_degree):
    fine_nodes = gll_tables(fine_degree)[0]
    coarse_nodes = gll_tables(coarse_degree)[0]
    lagrange = np.ones((fine_degree + 1, coarse_degree + 1))
    for col in range(coarse_degree + 1):
        for other in range(coarse_degree + 1):
            if other != col:
                lagrange[:, col] *= (fine_nodes - coarse_nodes[other]) / (
                    coarse_nodes[col] - coarse_nodes[other]
                )
    return lagrange


def lane_at(a, b):
    n = 7 * b + a
    return n if n < 25 else n + 7


def lanes_of(values):
    n = values.shape[0]
    out = np.zeros(64)
    for a in range(n):
        for b in range(n):
            out[lane_at(a, b)] = values[a, b]
    return out


def square_of(matrix, n_out, n_in):
    rows = [lane_at(a, b) for a in range(n_out) for b in range(n_out)]
    columns = [lane_at(a, b) for a in range(n_in) for b in range(n_in)]
    out = np.zeros((64, 64))
    out[np.ix_(rows, columns)] = matrix
    return out


def line_basis(q, t):
    u = np.zeros((q, q), complex)
    u[0, 0] = 1.0
    turn = np.exp(-0.5j * t) / np.sqrt(2.0)
    for a in range(1, (q + 1) // 2):
        u[a, a] = u[a, q - a] = turn
        u[q - a, a], u[q - a, q - a] = -1j * turn, 1j * turn
    return u


def closing(q, t):
    out = np.eye(q + 1, q, dtype=complex)
    out[q, 0] = np.exp(1j * t)
    return out


def real_parts(matrix_of, count):
    angles = 0.3 + 0.7 * np.arange(8)
    terms = np.stack([np.ones(8), np.cos(angles / 2), np.sin(angles / 2), np.cos(angles)], 1)[:, :count]
    values = np.stack([matrix_of(t) for t in angles])
    flat = values.reshape(8, -1)
    parts = np.linalg.lstsq(terms, flat.real, rcond=None)[0]
    assert np.abs(terms @ parts - flat).max() < 1e-11 * np.abs(flat).max()
    return parts.reshape((count,) + values.shape[1:])


class Level:
    def __init__(self, q):
        self.q = q
        _, w, s = gll_tables(q)
        self.w, self.s = w, s
        mass = 0.5 * w[:q].copy()
        mass[0] = 0.5 * (w[0] + w[q])
        diag = 2.0 * np.diag(s)[:q].copy()
        diag[0] = 2.0 * (s[0, 0] + s[q, q])
        self.mxz = np.outer(mass, mass)
        a = np.outer(diag, mass) + np.outer(mass, diag) + screen_shift * self.mxz
        self.ratio = lanes_of(a / self.mxz)
        spread = np.abs(s).sum(axis=1)
        self.bound = max(1.0, float(np.max(spread / np.diag(s))))
        base = 2.0 * s[:q, :q].copy()
        base[0, 0] += 2.0 * s[q, q]
        e1 = np.zeros((q, q))
        e1[:, 0] = 2.0 * s[:q, q]
        even, odd = e1 + e1.T, e1 - e1.T
        dm = np.diag(mass)
        scale = np.concatenate([lanes_of(1.0 / self.mxz)] * 2)[None, :]
        sq = lambda m: square_of(m, q, q)
        span = real_parts(
            lambda t: line_basis(q, t) @ closing(q, t).conj().T @ (2.0 * s) @ closing(q, t) @ line_basis(q, t).conj().T, 4
        )
        fixed = sq(np.kron(base, dm) + np.kron(dm, span[0]) + screen_shift * np.kron(dm, dm))
        tables = [np.hstack([fixed, 0.0 * fixed])]
        tables.append(np.hstack([sq(np.kron(even, dm)), -sq(np.kron(odd, dm))]))
        for part in span[1:]:
            part = sq(np.kron(dm, part))
            tables.append(np.hstack([part, 0.0 * part]))
        self.tables = [(t * scale)[: 64 if q > 3 else 24] for t in tables]
        self.weight = 0.5 * w
        self.stiff = s / self.weight[:, None]
        self.mass_lanes = np.concatenate([lanes_of(self.mxz)] * 2)
        self.inv_mass_lanes = np.concatenate([lanes_of(1.0 / self.mxz)] * 2)
        self.ratio_lanes = np.concatenate([self.ratio] * 2)
        self.mask_lanes = (self.mass_lanes > 0).astype(np.float64)


def transfer_tables(fine, coarse):
    j = interp_table(fine, coarse)
    ja = j[:fine, :coarse]
    jb = np.zeros((fine, coarse))
    jb[:, 0] = j[:fine, coarse]
    span = real_parts(
        lambda t: line_basis(fine, t) @ j[:fine] @ closing(coarse, t) @ line_basis(coarse, t).conj().T, 3
    )
    tables = []
    for part in span:
        for flow in (ja, jb):
            b = square_of(np.kron(flow, part), fine, coarse).T[: 24 if coarse > 1 else 8]
            tables.append(np.hstack([b, b if flow is jb else 0.0 * b]))
    return j, tables


def phase_rows():
    rows = np.zeros((80, 2, 64))
    for n in range(16):
        t = 2 * np.pi * n / NX
        if n:
            rows[2 * n], rows[2 * n + 1] = np.cos(t), np.sin(t)
        else:
            rows[0, 0], rows[0, 1] = 1.0, -1.0
    for k in range(8):
        for part in range(2):
            t = 2 * np.pi * k / NZ if k else np.pi * part
            at = 32 + 3 * (2 * k + part)
            rows[at], rows[at + 1], rows[at + 2] = np.cos(t / 2), np.sin(t / 2), np.cos(t)
    return rows.reshape(80, 128)


FINE, MID, LOW = Level(7), Level(3), Level(1)
J7, P7_TABLES = transfer_tables(7, 3)
J3, P3_TABLES = transfer_tables(3, 1)
MATRICES = np.concatenate(FINE.tables + MID.tables + P7_TABLES + P3_TABLES).astype(np.float32)
R7 = FINE.weight[:, None] * J7 / MID.weight
R3 = MID.weight[:, None] * J3 / LOW.weight
G7_AT, G3_AT, P7_AT, P3_AT = 0, 320, 440, 584


LANES = np.zeros((16, 128))
for n, level in enumerate((FINE, MID)):
    LANES[4 * n] = level.mass_lanes
    LANES[4 * n + 1] = level.inv_mass_lanes
    LANES[4 * n + 2] = level.ratio_lanes
    LANES[4 * n + 3] = level.mask_lanes
LANES[8] = LOW.mask_lanes
MATRICES = np.concatenate([MATRICES, LANES, phase_rows()]).astype(np.float32)
LANES_AT, PHASES_AT = 632, 648


def cheb_steps(bound, sweeps, floor):
    centre = bound * (1.0 + floor) / 2.0
    half = bound * (1.0 - floor) / 2.0
    s = centre / half
    p = 1.0 / s
    steps = []
    for _ in range(sweeps - 1):
        p_next = 1.0 / (2.0 * s - p)
        steps.append((p_next * p, 2.0 * p_next / half))
        p = p_next
    return 1.0 / centre, steps


FLOW, SPAN = ("zh", "z0", "xh", "core"), ("xl", "y")
LAST = ("core", "xl", "y")
USED = 8 * 49
SLAB = 13
FIELD = 32 * SLAB


def swap(v):
    return pltpu.roll(v, 64, axis=1)


def mix(first, v, w):
    return jnp.where(first, v, swap(w)), jnp.where(first, swap(v), w)


def pack_kernel(x_hbm, h_hbm, o_ref, rows_ref, x_ref, h_ref, line_ref, sems):
    line = pltpu.make_async_copy(h_hbm, h_ref, sems.at[0])
    line.start()
    field = pltpu.make_async_copy(x_hbm, x_ref, sems.at[1])
    field.start()
    first, _ = lane_tools()
    line_ref[...] = jnp.zeros_like(line_ref)
    line.wait()
    line_ref[0:1, 0:NY] = h_ref[...]
    rows_ref[...] = jnp.broadcast_to(line_ref[0:1, :], (128, 128)).T[:ROWS]
    field.wait()
    for a in range(7):
        for t in range(4):
            part = slice(128 * t, 128 * t + 128)
            low, high = mix(first, x_ref[a, 0:7, part], x_ref[a, 7:14, part])
            o_ref[pl.ds(98 * t + a, 7, stride=7), :] = low
            o_ref[pl.ds(98 * t + 49 + a, 7, stride=7), :] = high


def unpack_kernel(x_ref, o_ref):
    first, _ = lane_tools()
    for a in range(7):
        for t in range(4):
            part = slice(128 * t, 128 * t + 128)
            low, high = mix(
                first,
                x_ref[pl.ds(98 * t + a, 7, stride=7), :],
                x_ref[pl.ds(98 * t + 49 + a, 7, stride=7), :],
            )
            o_ref[a, 0:7, part] = low
            o_ref[a, 7:14, part] = high


def halves(v):
    high = v.astype(bf16)
    return high, (v - high.astype(f32)).astype(bf16)


def dot(a, b):
    return jnp.dot(a, b, preferred_element_type=f32)


HALF = float(np.sqrt(0.5))


def lane_tools():
    first = lax.broadcasted_iota(jnp.int32, (1, 128), 1) < 64
    return first, jnp.where(first, 1.0, -1.0).astype(f32)


def span_modes(x, first, sign, offset, size):
    s = [None] + [x[j] + x[8 - j] for j in (1, 2, 3)]
    d = [None] + [x[j] - x[8 - j] for j in (1, 2, 3)]
    up, down = x[0] + x[4], x[0] - x[4]
    odd, turn = s[1] + s[3], HALF * (s[1] - s[3])
    slope = HALF * (d[1] + d[3])
    re = [up + s[2] + odd, down + turn, up - s[2], down - turn, up + s[2] - odd]
    im = [None, -slope - d[2], d[3] - d[1], d[2] - slope]

    def phases(k):
        t = np.pi * k / 8
        p = 0.0 if offset is None else t / 2 + offset
        return [float(size * v) for v in (np.cos(p), np.sin(p), np.cos(p + t), np.sin(p + t))]

    flip = swap(re[0])
    out = [None] * 8
    out[0] = jnp.where(first, re[0] + flip, flip - re[0])
    c, s, v, w = phases(4)
    out[4] = jnp.where(first, c, -w) * re[4] + jnp.where(first, v, -s) * swap(re[4])
    for f in (1, 2, 3):
        re_swap, im_swap = swap(re[f]), swap(im[f])
        a = jnp.where(first, re[f], im_swap)
        b = jnp.where(first, im[f], -re_swap)
        p = jnp.where(first, re_swap, im[f])
        q = jnp.where(first, im_swap, -re[f])
        c, s, v, w = phases(f)
        out[f] = (c * a + v * p) + (s * b + w * q)
        c, s, v, w = phases(8 - f)
        out[8 - f] = sign * ((c * a + v * p) - (s * b + w * q))
    return out


def span_elements(x, first, sign, offset, size):
    def phases(k):
        t = np.pi * k / 8
        p = 0.0 if offset is None else t / 2 + offset
        return [float(size * v) for v in (np.cos(p), np.sin(p), np.cos(p + t), np.sin(p + t))]

    pick = lambda p, q: jnp.where(first, p, q)
    flip = swap(x[0])
    re = [jnp.where(first, x[0] + flip, flip - x[0])]
    im = [None]
    for f in (1, 2, 3):
        c, s, v, w = [2.0 * n for n in phases(f)]
        near, near_swap = x[f], swap(x[f])
        one = pick(c, -w) * near + pick(-s, v) * near_swap
        two = pick(s, v) * near + pick(c, w) * near_swap
        c, s, v, w = [2.0 * n for n in phases(8 - f)]
        far, far_swap = x[8 - f], swap(x[8 - f])
        re.append(one + (pick(c, -w) * far + pick(-s, v) * far_swap))
        im.append(two - (pick(s, v) * far + pick(c, w) * far_swap))
    c, s, v, w = [2.0 * n for n in phases(4)]
    re.append(pick(c, -w) * x[4] + pick(-s, v) * swap(x[4]))
    up, down = re[0] + re[4], re[0] - re[4]
    odd, turn = re[1] + re[3], HALF * (re[1] - re[3])
    slope = HALF * (im[1] + im[3])
    c = [up + re[2] + odd, down + turn, up - re[2], down - turn, up + re[2] - odd]
    s = [None, slope + im[2], im[1] - im[3], slope - im[2]]
    return [c[0]] + [c[j] - s[j] for j in (1, 2, 3)] + [c[4]] + [c[j] + s[j] for j in (3, 2, 1)]


def mode_rows(k, part):
    return 26 * (4 * (k // 2) + 2 * part + k % 2)


def span_forward_kernel(x_ref, o_ref, v_ref):
    first, sign = lane_tools()
    for k in range(8):
        v_ref[k, 48:56] = jnp.zeros((8, 128), f32)
    nodes = lambda b: [x_ref[49 * j + 7 * b : 49 * j + 7 * b + 7, :] for j in range(8)]
    for k, v in enumerate(span_modes(nodes(0), first, sign, None, 1.0)):
        v_ref[k, 0:7] = v
    for b in (1, 2, 3):
        near, far = nodes(b), nodes(7 - b)
        total = span_modes([p + q for p, q in zip(near, far)], first, sign, 0.0, HALF)
        differ = span_modes([p - q for p, q in zip(near, far)], first, sign, np.pi / 2, HALF)
        total[0], differ[0] = HALF * total[0], -HALF * differ[0]
        for k in range(8):
            v_ref[k, 7 * b : 7 * b + 7] = total[k]
            v_ref[k, 7 * (7 - b) : 7 * (7 - b) + 7] = differ[k]
    for k in range(8):
        re, im = mix(first, v_ref[k, 0:26], v_ref[k, 25:51])
        o_ref[mode_rows(k, 0) : mode_rows(k, 0) + 26, :] = re
        o_ref[mode_rows(k, 1) : mode_rows(k, 1) + 26, :] = im


def span_backward_kernel(x_ref, o_ref, v_ref):
    first, sign = lane_tools()
    for k in range(8):
        near, far = mix(
            first,
            x_ref[mode_rows(k, 0) : mode_rows(k, 0) + 26, :],
            x_ref[mode_rows(k, 1) : mode_rows(k, 1) + 26, :],
        )
        v_ref[k, 0:25] = near[0:25]
        v_ref[k, 25:49] = far[0:24]

    def store(b, planes):
        for j, v in enumerate(planes):
            o_ref[49 * j + 7 * b : 49 * j + 7 * b + 7, :] = v

    store(0, span_elements([v_ref[k, 0:7] for k in range(8)], first, sign, None, 1.0))
    for b in (1, 2, 3):
        total = [v_ref[k, 7 * b : 7 * b + 7] for k in range(8)]
        differ = [v_ref[k, 7 * (7 - b) : 7 * (7 - b) + 7] for k in range(8)]
        total[0], differ[0] = HALF * total[0], -HALF * differ[0]
        total = span_elements(total, first, sign, 0.0, HALF)
        differ = span_elements(differ, first, sign, np.pi / 2, HALF)
        store(b, [p + q for p, q in zip(total, differ)])
        store(7 - b, [p - q for p, q in zip(total, differ)])


def line_modes(x):
    n = len(x)
    if n == 1:
        return [(x[0], None)]
    even, odd = line_modes(x[0::2]), line_modes(x[1::2])
    out = [None] * (n // 2 + 1)
    out[0], out[n // 2] = (even[0][0] + odd[0][0], None), (even[0][0] - odd[0][0], None)
    for k in range(1, n // 4 + 1):
        (p, q), (v, w) = even[k], odd[k]
        if 4 * k == n:
            out[k] = (p, -v)
            continue
        c, s = float(np.cos(2 * np.pi * k / n)), float(np.sin(2 * np.pi * k / n))
        re, im = c * v + s * w, c * w - s * v
        out[k], out[n // 2 - k] = (p + re, q + im), (p - re, im - q)
    return out


def line_elements(modes, n):
    if n == 1:
        return [modes[0][0]]
    even, odd = [None] * (n // 4 + 1), [None] * (n // 4 + 1)
    low, high = modes[0][0], modes[n // 2][0]
    even[0], odd[0] = (low + high, None), (low - high, None)
    for k in range(1, n // 4 + 1):
        (p, q), (v, w) = modes[k], modes[n // 2 - k]
        if 4 * k == n:
            even[k], odd[k] = (2.0 * p, None), (-2.0 * q, None)
            continue
        c, s = float(np.cos(2 * np.pi * k / n)), float(np.sin(2 * np.pi * k / n))
        re, im = p - v, q + w
        even[k], odd[k] = (p + v, q - w), (c * re - s * im, c * im + s * re)
    x, y = line_elements(even, n // 2), line_elements(odd, n // 2)
    return [v for pair in zip(x, y) for v in pair]


def slab(ref, n):
    return ref[n * SLAB : n * SLAB + SLAB, :]


def flow_forward_kernel(x_ref, o_ref):
    modes = line_modes([slab(x_ref, n) for n in range(NX)])
    for n in range(16):
        re, im = modes[n][0], modes[n][1] if n else modes[16][0]
        o_ref[26 * n : 26 * n + 13, :] = re
        o_ref[26 * n + 13 : 26 * n + 26, :] = im


def flow_backward_kernel(x_ref, o_ref):
    modes = [(slab(x_ref, 2 * n), slab(x_ref, 2 * n + 1)) for n in range(16)]
    modes = [(modes[0][0], None)] + modes[1:] + [(modes[0][1], None)]
    for n, v in enumerate(line_elements(modes, NX)):
        o_ref[n * SLAB : n * SLAB + SLAB, :] = v


def table_product(v, t_ref):
    both = dot(jnp.concatenate(halves(v), axis=1), t_ref[...])
    return both[:, :128] + both[:, 128:]


def store_table(t_ref, table):
    high, low = halves(table)
    t_ref[0:128, 0:128] = high
    t_ref[128:256, 0:128] = high
    t_ref[0:128, 128:256] = low
    t_ref[128:256, 128:256] = jnp.zeros((128, 128), bf16)


def roll_up(v):
    return pltpu.roll(v, ROWS - 1, axis=0)


def roll_down(v):
    return pltpu.roll(v, 1, axis=0)


def wall_apply(s, q, planes, g):
    parts = [g * p for p in planes] + [g * roll_up(planes[0])]
    n = q + 1
    half = n // 2
    even = [parts[l] + parts[q - l] for l in range(half)]
    odd = [parts[l] - parts[q - l] for l in range(half)]
    out = [None] * n
    for k in range(half):
        p = m = None
        for l in range(half):
            ce = 0.5 * (s[k, l] + s[k, q - l])
            co = 0.5 * (s[k, l] - s[k, q - l])
            te, to = float(ce) * even[l], float(co) * odd[l]
            p = te if p is None else p + te
            m = to if m is None else m + to
        out[k] = p + m
        out[q - k] = p - m
    out[0] = out[0] + roll_down(out[q])
    return out[:q]


def weighted_sum(coefs, planes):
    total = None
    for c, v in zip(coefs, planes):
        c = float(c)
        if c == 0.0:
            continue
        t = v if c == 1.0 else c * v
        total = t if total is None else total + t
    return total


def restrict_wall(j, fine, coarse, planes):
    out = [weighted_sum(j[:fine, c], planes) for c in range(coarse)]
    out[0] = out[0] + roll_down(weighted_sum(j[:fine, coarse], planes))
    return out


def prolong_wall(j, fine, coarse, planes):
    closed = list(planes) + [roll_up(planes[0])]
    return [weighted_sum(j[k], closed) for k in range(fine)]


PIECES = [(y, half, part) for y in range(2) for half in range(2) for part in range(2)]


def cycle_kernel(
    h_ref, mats_ref, in_ref, out_ref,
    w_ref, geo_ref,
    u7, r7, x7, d7, u3, r3, x3, d3,
    square, g7_ref, g3_ref, r7_ref, p7_ref, r3_ref, p3_ref,
):
    at_x = PHASES_AT + 2 * lax.axis_index(LAST)
    at_z = PHASES_AT + 32 + 3 * lax.axis_index(("zh", "xh", "z0"))
    cx, sx = mats_ref[pl.ds(at_x, 1), :], mats_ref[pl.ds(at_x + 1, 1), :]
    ch, sh, cz = (mats_ref[pl.ds(at_z + n, 1), :] for n in range(3))
    lane = lax.broadcasted_iota(jnp.int32, (1, 128), 1)
    first = lane < 64
    mass7, inv7, ratio7, mask7 = (mats_ref[n : n + 1, :] for n in range(LANES_AT, LANES_AT + 4))
    mass3, inv3, ratio3, mask3 = (mats_ref[n : n + 1, :] for n in range(LANES_AT + 4, LANES_AT + 8))
    mask1 = mats_ref[LANES_AT + 8 : LANES_AT + 9, :]

    both = (cx, sx)
    alone = lambda c: (c, jnp.zeros_like(c))
    operator = [both, alone(ch), alone(sh), alone(cz)]
    transfer = [both, alone(ch), (cx * ch, sx * ch), alone(sh), (cx * sh, sx * sh)]

    def mode_table(at, rows, phases):
        top = mats_ref[at : at + rows]
        low = pltpu.roll(top, 64, axis=1)
        for c, s in phases:
            at += rows
            t = mats_ref[at : at + rows]
            top = top + jnp.where(first, c, s) * t
            low = low + jnp.where(first, -s, c) * pltpu.roll(t, 64, axis=1)
        if rows == 64:
            return jnp.concatenate([top, low], axis=0)
        square[...] = jnp.zeros((128, 128), f32)
        square[0:rows] = top
        square[64 : 64 + rows] = low
        return square[...]

    store_table(g7_ref, mode_table(G7_AT, 64, operator))
    store_table(g3_ref, mode_table(G3_AT, 24, operator))
    table = mode_table(P7_AT, 24, transfer)
    store_table(p7_ref, table)
    store_table(r7_ref, (table * mass7).T * inv3)
    table = mode_table(P3_AT, 8, transfer)
    store_table(p3_ref, table)
    store_table(r3_ref, (table * mass3).T)

    scale = inv7 * (1.0 / (NX * NZ))
    outer = lane % 64 < 32
    square[...] = jnp.zeros((128, 128), f32)
    for t in range(4):
        for y, half, part in PIECES:
            r, v = 64 * part + 32 * y + 13 * half, 208 * half + 26 * (2 * t + y) + 13 * part
            square[r : r + 13, :] = in_ref[v : v + 13, :]
        both = square[...].T
        low, high = both[:64], both[64:]
        w_ref[128 * t : 128 * t + 64, :] = jnp.where(outer, low, pltpu.roll(high, 32, axis=1)) * scale
        w_ref[128 * t + 64 : 128 * t + 128, :] = jnp.where(outer, pltpu.roll(low, 96, axis=1), high) * scale
    w_ref[512:, :] = jnp.zeros((w_ref.shape[0] - 512, 128), f32)
    for k in range(7):
        r7[k] = float(1.0 / FINE.weight[k]) * w_ref[pl.ds(k, ROWS, stride=7), :]

    h = h_ref[...]
    row = lax.broadcasted_iota(jnp.int32, (ROWS, 128), 0)
    g = jnp.where(row < NY, 2.0 / jnp.where(row < NY, h, 1.0), 0.0)
    h_pair = h + roll_down(h)
    g_pair = g + roll_down(g)
    geo_ref[0] = h
    geo_ref[1] = g
    geo_ref[2] = h_pair

    def height(k):
        return geo_ref[0 if k else 2]

    def inverse_diag(level, ratio, mask, k):
        d = height(k) * ratio + float(level.stiff[k, k]) * (g if k else g_pair)
        return jnp.where(d > 0.0, mask / jnp.where(d > 0.0, d, 1.0), 0.0)

    for k in range(7):
        d7[k] = inverse_diag(FINE, ratio7, mask7, k)
    for k in range(3):
        d3[k] = inverse_diag(MID, ratio3, mask3, k)
    d1_mix = ((4.0 + screen_shift) - 2.0 * cx - 2.0 * cz) * mask1
    d1 = inverse_diag(LOW, 4.0 + screen_shift, mask1, 0)

    def apply(level, u, table):
        q = level.q
        m = table_product(u[...].reshape(q * ROWS, 128), table)
        wall = wall_apply(level.stiff, q, [u[k] for k in range(q)], geo_ref[1])
        return [height(k) * m[k * ROWS : (k + 1) * ROWS] + wall[k] for k in range(q)]

    def smooth(level, u, r, x, d, table, fresh, keep_residual):
        q = level.q
        start, steps = cheb_steps(level.bound, SMOOTH_STEPS, smooth_floor)
        for k in range(q):
            t = start * (d[k] * r[k])
            u[k] = t
            x[k] = t if fresh else x[k] + t
        for alpha, beta in steps:
            au = apply(level, u, table)
            for k in range(q):
                t = r[k] - au[k]
                r[k] = t
                t = alpha * u[k] + beta * (d[k] * t)
                u[k] = t
                x[k] = x[k] + t
        if keep_residual:
            au = apply(level, u, table)
            for k in range(q):
                r[k] = r[k] - au[k]

    def product(planes, table):
        m = table_product(jnp.concatenate(planes, axis=0), table)
        return [m[k * ROWS : (k + 1) * ROWS] for k in range(len(planes))]

    smooth(FINE, u7, r7, x7, d7, g7_ref, True, True)
    down = product(restrict_wall(R7, 7, 3, [r7[k] for k in range(7)]), r7_ref)
    for k in range(3):
        r3[k] = down[k]

    smooth(MID, u3, r3, x3, d3, g3_ref, True, True)
    r1 = product(restrict_wall(R3, 3, 1, [r3[k] for k in range(3)]), r3_ref)[0]

    start, steps = cheb_steps(LOW.bound, COARSE_STEPS, coarse_floor)
    middle = d1 * (height(0) * d1_mix + g_pair)
    after, before = d1 * g, d1 * roll_down(g)
    r1 = d1 * r1
    u1 = start * r1
    x1 = u1
    for alpha, beta in steps:
        r1 = (r1 - middle * u1) + (after * roll_up(u1) + before * roll_down(u1))
        u1 = alpha * u1 + beta * r1
        x1 = x1 + u1

    up = prolong_wall(J3, 3, 1, product([x1], p3_ref))
    for k in range(3):
        u3[k] = up[k]
        x3[k] = x3[k] + up[k]
    au = apply(MID, u3, g3_ref)
    for k in range(3):
        r3[k] = r3[k] - au[k]
    smooth(MID, u3, r3, x3, d3, g3_ref, False, False)

    up = prolong_wall(J7, 7, 3, product([x3[k] for k in range(3)], p7_ref))
    for k in range(7):
        u7[k] = up[k]
        x7[k] = x7[k] + up[k]
    au = apply(FINE, u7, g7_ref)
    for k in range(7):
        r7[k] = r7[k] - au[k]
    smooth(FINE, u7, r7, x7, d7, g7_ref, False, False)

    for k in range(7):
        w_ref[pl.ds(k, ROWS, stride=7), :] = x7[k]
    for t in range(4):
        low, high = w_ref[128 * t : 128 * t + 64, :], w_ref[128 * t + 64 : 128 * t + 128, :]
        square[...] = jnp.concatenate(
            [
                jnp.where(outer, low, pltpu.roll(high, 32, axis=1)),
                jnp.where(outer, pltpu.roll(low, 96, axis=1), high),
            ],
            axis=0,
        ).T
        for y, half, part in PIECES:
            r, v = 64 * part + 32 * y + 13 * half, 208 * half + 26 * (2 * t + y) + 13 * part
            out_ref[v : v + 13, :] = square[r : r + 13, :]


VMEM = pl.BlockSpec(memory_space=pltpu.VMEM)
HBM = pl.BlockSpec(memory_space=pltpu.HBM)
PARAMS = pltpu.CompilerParams(vmem_limit_bytes=32 * 1024 * 1024)
FLAT = jax.ShapeDtypeStruct((FIELD, 128), f32)
TIGHT = jax.ShapeDtypeStruct((USED, 128), f32)
LINES = [pltpu.VMEM((8, 56, 128), f32)]


def exchange(block, axes):
    n, rows = lax.axis_size(axes), block.shape[0]
    block = block.reshape(n, rows // n, 1, 128)
    return lax.all_to_all(block, axes, 0, 0).reshape(rows, 128)


def cycle_call(heights, modes):
    fine = pltpu.VMEM((7, ROWS, 128), f32)
    mid = pltpu.VMEM((3, ROWS, 128), f32)
    table = pltpu.VMEM((256, 256), bf16)
    return pl.pallas_call(
        cycle_kernel, out_shape=FLAT,
        in_specs=[VMEM, VMEM, VMEM], out_specs=VMEM,
        scratch_shapes=[
            pltpu.VMEM((7 * ROWS, 128), f32), mid,
            fine, fine, fine, fine, mid, mid, mid, mid,
            pltpu.VMEM((128, 128), f32), table, table, table, table, table, table,
        ],
        compiler_params=PARAMS,
    )(
        heights, jnp.asarray(MATRICES), modes,
    )


def transform(kernel, block, out_shape=FLAT, scratch=()):
    return pl.pallas_call(
        kernel, out_shape=out_shape, in_specs=[VMEM], out_specs=VMEM,
        scratch_shapes=scratch, compiler_params=PARAMS,
    )(block)


def body(residual, layer_heights):
    stay = lambda v: pltpu.with_memory_space_constraint(v, pltpu.HBM)
    packed, heights = pl.pallas_call(
        pack_kernel, out_shape=(TIGHT, jax.ShapeDtypeStruct((ROWS, 128), f32)),
        in_specs=[HBM, HBM], out_specs=(VMEM, VMEM),
        scratch_shapes=[
            pltpu.VMEM((7, 14, 512), f32), pltpu.VMEM((1, NY), f32), pltpu.VMEM((8, 128), f32),
            pltpu.SemaphoreType.DMA((2,)),
        ],
        compiler_params=PARAMS,
    )(stay(residual), stay(layer_heights.reshape(1, NY)))
    spans = transform(span_forward_kernel, exchange(packed, SPAN), scratch=LINES)
    modes = exchange(transform(flow_forward_kernel, exchange(spans, FLOW)), LAST)
    solved = exchange(cycle_call(heights, modes), LAST)
    flows = exchange(transform(flow_backward_kernel, solved), FLOW)
    spread = exchange(transform(span_backward_kernel, flows, TIGHT, LINES), SPAN)
    return pl.pallas_call(
        unpack_kernel, out_shape=jax.ShapeDtypeStruct((7, 14, 512), f32),
        in_specs=[VMEM], out_specs=VMEM, compiler_params=PARAMS,
    )(spread)


def solution(mesh):
    split = Mesh(mesh.devices.reshape(4, 2, 2, 2, 2, 4), FLOW + SPAN)
    spec = P(FLOW, SPAN, None)
    return jax.shard_map(
        body, mesh=split, in_specs=(spec, P()), out_specs=spec, check_vma=False
    )
```

```python
import jax
import jax.numpy as jnp
import ml_dtypes
import numpy as np
from jax import lax
from jax.experimental import pallas as pl
from jax.experimental.pallas import tpu as pltpu
from jax.sharding import Mesh
from jax.sharding import PartitionSpec as P


SMOOTH_STEPS = 3
COARSE_STEPS = 12
NX, NZ, NY = 32, 16, 73
DEVICES = 256
ROWS = 80
screen_shift = 0.02
smooth_floor = 0.1
coarse_floor = 0.01
f32 = jnp.float32
bf16 = jnp.bfloat16


def legendre_values(points, degree):
    columns = [np.ones(points.shape), points]
    for n in range(2, degree + 1):
        columns.append(((2 * n - 1) * points * columns[-1] - (n - 1) * columns[-2]) / n)
    return np.stack(columns[: degree + 1], axis=1)


def gll_tables(degree):
    nodes = -np.cos(np.pi * np.arange(degree + 1) / degree)
    for _ in range(100):
        values = legendre_values(nodes, degree)
        nodes = nodes - (nodes * values[:, degree] - values[:, degree - 1]) / (
            (degree + 1) * values[:, degree]
        )
    leading = legendre_values(nodes, degree)[:, degree]
    weights = 2.0 / (degree * (degree + 1) * leading**2)
    differ = np.zeros((degree + 1, degree + 1))
    for i in range(degree + 1):
        for j in range(degree + 1):
            if i != j:
                differ[i, j] = leading[i] / (leading[j] * (nodes[i] - nodes[j]))
    differ[0, 0] = -degree * (degree + 1) / 4.0
    differ[degree, degree] = degree * (degree + 1) / 4.0
    return nodes, weights, differ.T @ (weights[:, None] * differ)


def interp_table(fine_degree, coarse_degree):
    fine_nodes = gll_tables(fine_degree)[0]
    coarse_nodes = gll_tables(coarse_degree)[0]
    lagrange = np.ones((fine_degree + 1, coarse_degree + 1))
    for col in range(coarse_degree + 1):
        for other in range(coarse_degree + 1):
            if other != col:
                lagrange[:, col] *= (fine_nodes - coarse_nodes[other]) / (
                    coarse_nodes[col] - coarse_nodes[other]
                )
    return lagrange


def lane_at(a, b):
    n = 7 * b + a
    return n if n < 25 else n + 7


def lanes_of(values):
    n = values.shape[0]
    out = np.zeros(64)
    for a in range(n):
        for b in range(n):
            out[lane_at(a, b)] = values[a, b]
    return out


def square_of(matrix, n_out, n_in):
    rows = [lane_at(a, b) for a in range(n_out) for b in range(n_out)]
    columns = [lane_at(a, b) for a in range(n_in) for b in range(n_in)]
    out = np.zeros((64, 64))
    out[np.ix_(rows, columns)] = matrix
    return out


def line_basis(q, t):
    u = np.zeros((q, q), complex)
    u[0, 0] = 1.0
    turn = np.exp(-0.5j * t) / np.sqrt(2.0)
    for a in range(1, (q + 1) // 2):
        u[a, a] = u[a, q - a] = turn
        u[q - a, a], u[q - a, q - a] = -1j * turn, 1j * turn
    return u


def closing(q, t):
    out = np.eye(q + 1, q, dtype=complex)
    out[q, 0] = np.exp(1j * t)
    return out


def real_parts(matrix_of, count):
    angles = 0.3 + 0.7 * np.arange(8)
    terms = np.stack([np.ones(8), np.cos(angles / 2), np.sin(angles / 2), np.cos(angles)], 1)[:, :count]
    values = np.stack([matrix_of(t) for t in angles])
    flat = values.reshape(8, -1)
    parts = np.linalg.lstsq(terms, flat.real, rcond=None)[0]
    assert np.abs(terms @ parts - flat).max() < 1e-11 * np.abs(flat).max()
    return parts.reshape((count,) + values.shape[1:])


class Level:
    def __init__(self, q):
        self.q = q
        _, w, s = gll_tables(q)
        self.w, self.s = w, s
        mass = 0.5 * w[:q].copy()
        mass[0] = 0.5 * (w[0] + w[q])
        diag = 2.0 * np.diag(s)[:q].copy()
        diag[0] = 2.0 * (s[0, 0] + s[q, q])
        self.mxz = np.outer(mass, mass)
        a = np.outer(diag, mass) + np.outer(mass, diag) + screen_shift * self.mxz
        self.ratio = lanes_of(a / self.mxz)
        spread = np.abs(s).sum(axis=1)
        self.bound = max(1.0, float(np.max(spread / np.diag(s))))
        base = 2.0 * s[:q, :q].copy()
        base[0, 0] += 2.0 * s[q, q]
        e1 = np.zeros((q, q))
        e1[:, 0] = 2.0 * s[:q, q]
        even, odd = e1 + e1.T, e1 - e1.T
        dm = np.diag(mass)
        scale = np.concatenate([lanes_of(1.0 / self.mxz)] * 2)[None, :]
        sq = lambda m: square_of(m, q, q)
        span = real_parts(
            lambda t: line_basis(q, t) @ closing(q, t).conj().T @ (2.0 * s) @ closing(q, t) @ line_basis(q, t).conj().T, 4
        )
        fixed = sq(np.kron(base, dm) + np.kron(dm, span[0]) + screen_shift * np.kron(dm, dm))
        tables = [np.hstack([fixed, 0.0 * fixed])]
        tables.append(np.hstack([sq(np.kron(even, dm)), -sq(np.kron(odd, dm))]))
        for part in span[1:]:
            part = sq(np.kron(dm, part))
            tables.append(np.hstack([part, 0.0 * part]))
        self.tables = [(t * scale)[: 64 if q > 3 else 24] for t in tables]
        self.weight = 0.5 * w
        self.stiff = s / self.weight[:, None]
        self.mass_lanes = np.concatenate([lanes_of(self.mxz)] * 2)
        self.inv_mass_lanes = np.concatenate([lanes_of(1.0 / self.mxz)] * 2)
        self.ratio_lanes = np.concatenate([self.ratio] * 2)
        self.mask_lanes = (self.mass_lanes > 0).astype(np.float64)


def transfer_tables(fine, coarse):
    j = interp_table(fine, coarse)
    ja = j[:fine, :coarse]
    jb = np.zeros((fine, coarse))
    jb[:, 0] = j[:fine, coarse]
    span = real_parts(
        lambda t: line_basis(fine, t) @ j[:fine] @ closing(coarse, t) @ line_basis(coarse, t).conj().T, 3
    )
    tables = []
    for part in span:
        for flow in (ja, jb):
            b = square_of(np.kron(flow, part), fine, coarse).T[: 24 if coarse > 1 else 8]
            tables.append(np.hstack([b, b if flow is jb else 0.0 * b]))
    return j, tables


def phase_rows():
    rows = np.zeros((80, 2, 64))
    for n in range(16):
        t = 2 * np.pi * n / NX
        if n:
            rows[2 * n], rows[2 * n + 1] = np.cos(t), np.sin(t)
        else:
            rows[0, 0], rows[0, 1] = 1.0, -1.0
    for k in range(8):
        for part in range(2):
            t = 2 * np.pi * k / NZ if k else np.pi * part
            at = 32 + 3 * (2 * k + part)
            rows[at], rows[at + 1], rows[at + 2] = np.cos(t / 2), np.sin(t / 2), np.cos(t)
    return rows.reshape(80, 128)


FINE, MID, LOW = Level(7), Level(3), Level(1)
J7, P7_TABLES = transfer_tables(7, 3)
J3, P3_TABLES = transfer_tables(3, 1)
MATRICES = np.concatenate(FINE.tables + MID.tables + P7_TABLES + P3_TABLES).astype(np.float32)
R7 = FINE.weight[:, None] * J7 / MID.weight
R3 = MID.weight[:, None] * J3 / LOW.weight
G7_AT, G3_AT, P7_AT, P3_AT = 0, 320, 440, 584


LANES = np.zeros((16, 128))
for n, level in enumerate((FINE, MID)):
    LANES[4 * n] = level.mass_lanes
    LANES[4 * n + 1] = level.inv_mass_lanes
    LANES[4 * n + 2] = level.ratio_lanes
    LANES[4 * n + 3] = level.mask_lanes
LANES[8] = LOW.mask_lanes
MATRICES = np.concatenate([MATRICES, LANES, phase_rows()]).astype(np.float32)
LANES_AT, PHASES_AT = 632, 648


def cheb_steps(bound, sweeps, floor):
    centre = bound * (1.0 + floor) / 2.0
    half = bound * (1.0 - floor) / 2.0
    s = centre / half
    p = 1.0 / s
    steps = []
    for _ in range(sweeps - 1):
        p_next = 1.0 / (2.0 * s - p)
        steps.append((p_next * p, 2.0 * p_next / half))
        p = p_next
    return 1.0 / centre, steps


FLOW, SPAN = ("zh", "z0", "xh", "core"), ("xl", "y")
LAST = ("xl", "y", "core")
USED = 8 * 49
SLAB = 13
FIELD = 32 * SLAB


def swap(v):
    return pltpu.roll(v, 64, axis=1)


def mix(first, v, w):
    return jnp.where(first, v, swap(w)), jnp.where(first, swap(v), w)


def pack_kernel(x_hbm, h_hbm, o_ref, rows_ref, x_ref, h_ref, line_ref, sems):
    line = pltpu.make_async_copy(h_hbm, h_ref, sems.at[0])
    line.start()
    field = pltpu.make_async_copy(x_hbm, x_ref, sems.at[1])
    field.start()
    first, _ = lane_tools()
    line_ref[...] = jnp.zeros_like(line_ref)
    line.wait()
    line_ref[0:1, 0:NY] = h_ref[...]
    rows_ref[...] = jnp.broadcast_to(line_ref[0:1, :], (128, 128)).T[:ROWS]
    field.wait()
    for a in range(7):
        for t in range(4):
            part = slice(128 * t, 128 * t + 128)
            low, high = mix(first, x_ref[a, 0:7, part], x_ref[a, 7:14, part])
            o_ref[pl.ds(98 * t + a, 7, stride=7), :] = low
            o_ref[pl.ds(98 * t + 49 + a, 7, stride=7), :] = high


def unpack_kernel(x_ref, o_ref):
    first, _ = lane_tools()
    for a in range(7):
        for t in range(4):
            part = slice(128 * t, 128 * t + 128)
            low, high = mix(
                first,
                x_ref[pl.ds(98 * t + a, 7, stride=7), :],
                x_ref[pl.ds(98 * t + 49 + a, 7, stride=7), :],
            )
            o_ref[a, 0:7, part] = low
            o_ref[a, 7:14, part] = high


def halves(v):
    high = v.astype(bf16)
    return high, (v - high.astype(f32)).astype(bf16)


def dot(a, b):
    return jnp.dot(a, b, preferred_element_type=f32)


HALF = float(np.sqrt(0.5))


def lane_tools():
    first = lax.broadcasted_iota(jnp.int32, (1, 128), 1) < 64
    return first, jnp.where(first, 1.0, -1.0).astype(f32)


def span_modes(x, first, sign, offset, size):
    s = [None] + [x[j] + x[8 - j] for j in (1, 2, 3)]
    d = [None] + [x[j] - x[8 - j] for j in (1, 2, 3)]
    up, down = x[0] + x[4], x[0] - x[4]
    odd, turn = s[1] + s[3], HALF * (s[1] - s[3])
    slope = HALF * (d[1] + d[3])
    re = [up + s[2] + odd, down + turn, up - s[2], down - turn, up + s[2] - odd]
    im = [None, -slope - d[2], d[3] - d[1], d[2] - slope]

    def phases(k):
        t = np.pi * k / 8
        p = 0.0 if offset is None else t / 2 + offset
        return [float(size * v) for v in (np.cos(p), np.sin(p), np.cos(p + t), np.sin(p + t))]

    flip = swap(re[0])
    out = [None] * 8
    out[0] = jnp.where(first, re[0] + flip, flip - re[0])
    c, s, v, w = phases(4)
    out[4] = jnp.where(first, c, -w) * re[4] + jnp.where(first, v, -s) * swap(re[4])
    for f in (1, 2, 3):
        re_swap, im_swap = swap(re[f]), swap(im[f])
        a = jnp.where(first, re[f], im_swap)
        b = jnp.where(first, im[f], -re_swap)
        p = jnp.where(first, re_swap, im[f])
        q = jnp.where(first, im_swap, -re[f])
        c, s, v, w = phases(f)
        out[f] = (c * a + v * p) + (s * b + w * q)
        c, s, v, w = phases(8 - f)
        out[8 - f] = sign * ((c * a + v * p) - (s * b + w * q))
    return out


def span_elements(x, first, sign, offset, size):
    def phases(k):
        t = np.pi * k / 8
        p = 0.0 if offset is None else t / 2 + offset
        return [float(size * v) for v in (np.cos(p), np.sin(p), np.cos(p + t), np.sin(p + t))]

    pick = lambda p, q: jnp.where(first, p, q)
    flip = swap(x[0])
    re = [jnp.where(first, x[0] + flip, flip - x[0])]
    im = [None]
    for f in (1, 2, 3):
        c, s, v, w = [2.0 * n for n in phases(f)]
        near, near_swap = x[f], swap(x[f])
        one = pick(c, -w) * near + pick(-s, v) * near_swap
        two = pick(s, v) * near + pick(c, w) * near_swap
        c, s, v, w = [2.0 * n for n in phases(8 - f)]
        far, far_swap = x[8 - f], swap(x[8 - f])
        re.append(one + (pick(c, -w) * far + pick(-s, v) * far_swap))
        im.append(two - (pick(s, v) * far + pick(c, w) * far_swap))
    c, s, v, w = [2.0 * n for n in phases(4)]
    re.append(pick(c, -w) * x[4] + pick(-s, v) * swap(x[4]))
    up, down = re[0] + re[4], re[0] - re[4]
    odd, turn = re[1] + re[3], HALF * (re[1] - re[3])
    slope = HALF * (im[1] + im[3])
    c = [up + re[2] + odd, down + turn, up - re[2], down - turn, up + re[2] - odd]
    s = [None, slope + im[2], im[1] - im[3], slope - im[2]]
    return [c[0]] + [c[j] - s[j] for j in (1, 2, 3)] + [c[4]] + [c[j] + s[j] for j in (3, 2, 1)]


def mode_rows(k, part):
    return 26 * (4 * (k // 2) + 2 * part + k % 2)


def span_forward_kernel(x_ref, o_ref, v_ref):
    first, sign = lane_tools()
    for k in range(8):
        v_ref[k, 48:56] = jnp.zeros((8, 128), f32)
    nodes = lambda b: [x_ref[49 * j + 7 * b : 49 * j + 7 * b + 7, :] for j in range(8)]
    for k, v in enumerate(span_modes(nodes(0), first, sign, None, 1.0)):
        v_ref[k, 0:7] = v
    for b in (1, 2, 3):
        near, far = nodes(b), nodes(7 - b)
        total = span_modes([p + q for p, q in zip(near, far)], first, sign, 0.0, HALF)
        differ = span_modes([p - q for p, q in zip(near, far)], first, sign, np.pi / 2, HALF)
        total[0], differ[0] = HALF * total[0], -HALF * differ[0]
        for k in range(8):
            v_ref[k, 7 * b : 7 * b + 7] = total[k]
            v_ref[k, 7 * (7 - b) : 7 * (7 - b) + 7] = differ[k]
    for k in range(8):
        re, im = mix(first, v_ref[k, 0:26], v_ref[k, 25:51])
        o_ref[mode_rows(k, 0) : mode_rows(k, 0) + 26, :] = re
        o_ref[mode_rows(k, 1) : mode_rows(k, 1) + 26, :] = im


def span_backward_kernel(x_ref, o_ref, v_ref):
    first, sign = lane_tools()
    for k in range(8):
        near, far = mix(
            first,
            x_ref[mode_rows(k, 0) : mode_rows(k, 0) + 26, :],
            x_ref[mode_rows(k, 1) : mode_rows(k, 1) + 26, :],
        )
        v_ref[k, 0:25] = near[0:25]
        v_ref[k, 25:49] = far[0:24]

    def store(b, planes):
        for j, v in enumerate(planes):
            o_ref[49 * j + 7 * b : 49 * j + 7 * b + 7, :] = v

    store(0, span_elements([v_ref[k, 0:7] for k in range(8)], first, sign, None, 1.0))
    for b in (1, 2, 3):
        total = [v_ref[k, 7 * b : 7 * b + 7] for k in range(8)]
        differ = [v_ref[k, 7 * (7 - b) : 7 * (7 - b) + 7] for k in range(8)]
        total[0], differ[0] = HALF * total[0], -HALF * differ[0]
        total = span_elements(total, first, sign, 0.0, HALF)
        differ = span_elements(differ, first, sign, np.pi / 2, HALF)
        store(b, [p + q for p, q in zip(total, differ)])
        store(7 - b, [p - q for p, q in zip(total, differ)])


def line_modes(x):
    n = len(x)
    if n == 1:
        return [(x[0], None)]
    even, odd = line_modes(x[0::2]), line_modes(x[1::2])
    out = [None] * (n // 2 + 1)
    out[0], out[n // 2] = (even[0][0] + odd[0][0], None), (even[0][0] - odd[0][0], None)
    for k in range(1, n // 4 + 1):
        (p, q), (v, w) = even[k], odd[k]
        if 4 * k == n:
            out[k] = (p, -v)
            continue
        c, s = float(np.cos(2 * np.pi * k / n)), float(np.sin(2 * np.pi * k / n))
        re, im = c * v + s * w, c * w - s * v
        out[k], out[n // 2 - k] = (p + re, q + im), (p - re, im - q)
    return out


def line_elements(modes, n):
    if n == 1:
        return [modes[0][0]]
    even, odd = [None] * (n // 4 + 1), [None] * (n // 4 + 1)
    low, high = modes[0][0], modes[n // 2][0]
    even[0], odd[0] = (low + high, None), (low - high, None)
    for k in range(1, n // 4 + 1):
        (p, q), (v, w) = modes[k], modes[n // 2 - k]
        if 4 * k == n:
            even[k], odd[k] = (2.0 * p, None), (-2.0 * q, None)
            continue
        c, s = float(np.cos(2 * np.pi * k / n)), float(np.sin(2 * np.pi * k / n))
        re, im = p - v, q + w
        even[k], odd[k] = (p + v, q - w), (c * re - s * im, c * im + s * re)
    x, y = line_elements(even, n // 2), line_elements(odd, n // 2)
    return [v for pair in zip(x, y) for v in pair]


def slab(ref, n):
    return ref[n * SLAB : n * SLAB + SLAB, :]


def flow_forward_kernel(x_ref, o_ref):
    modes = line_modes([slab(x_ref, n) for n in range(NX)])
    for n in range(16):
        re, im = modes[n][0], modes[n][1] if n else modes[16][0]
        o_ref[26 * n : 26 * n + 13, :] = re
        o_ref[26 * n + 13 : 26 * n + 26, :] = im


def flow_backward_kernel(x_ref, o_ref):
    modes = [(slab(x_ref, 2 * n), slab(x_ref, 2 * n + 1)) for n in range(16)]
    modes = [(modes[0][0], None)] + modes[1:] + [(modes[0][1], None)]
    for n, v in enumerate(line_elements(modes, NX)):
        o_ref[n * SLAB : n * SLAB + SLAB, :] = v


def table_product(v, t_ref):
    both = dot(jnp.concatenate(halves(v), axis=1), t_ref[...])
    return both[:, :128] + both[:, 128:]


def store_table(t_ref, table):
    high, low = halves(table)
    t_ref[0:128, 0:128] = high
    t_ref[128:256, 0:128] = high
    t_ref[0:128, 128:256] = low
    t_ref[128:256, 128:256] = jnp.zeros((128, 128), bf16)


def roll_up(v):
    return pltpu.roll(v, ROWS - 1, axis=0)


def roll_down(v):
    return pltpu.roll(v, 1, axis=0)


def element_products(s, q, planes):
    parts = list(planes) + [roll_up(planes[0])]
    n = q + 1
    half = n // 2
    even = [parts[l] + parts[q - l] for l in range(half)]
    odd = [parts[l] - parts[q - l] for l in range(half)]
    out = [None] * n
    for k in range(half):
        p = m = None
        for l in range(half):
            ce = 0.5 * (s[k, l] + s[k, q - l])
            co = 0.5 * (s[k, l] - s[k, q - l])
            te, to = float(ce) * even[l], float(co) * odd[l]
            p = te if p is None else p + te
            m = to if m is None else m + to
        out[k] = p + m
        out[q - k] = p - m
    return out


def weighted_sum(coefs, planes):
    total = None
    for c, v in zip(coefs, planes):
        c = float(c)
        if c == 0.0:
            continue
        t = v if c == 1.0 else c * v
        total = t if total is None else total + t
    return total


def restrict_wall(j, fine, coarse, planes, h, inv_pair):
    out = [weighted_sum(j[1:fine, c], planes[1:]) for c in range(coarse)]
    shared = h * out[0] + roll_down(h * weighted_sum(j[1:fine, coarse], planes[1:]))
    out[0] = float(j[0, 0]) * planes[0] + inv_pair * shared
    return out


def prolong_wall(j, fine, coarse, planes):
    closed = list(planes) + [roll_up(planes[0])]
    return [weighted_sum(j[k], closed) for k in range(fine)]


PIECES = [(y, half, part) for y in range(2) for half in range(2) for part in range(2)]


def cycle_kernel(
    h_ref, mats_ref, in_ref, out_ref,
    w_ref, geo_ref,
    u7, r7, x7, d7, u3, r3, x3, d3,
    square, g7_ref, g3_ref, r7_ref, p7_ref, r3_ref, p3_ref,
):
    at_x = PHASES_AT + 2 * lax.axis_index(LAST)
    at_z = PHASES_AT + 32 + 3 * lax.axis_index(("zh", "xh", "z0"))
    cx, sx = mats_ref[pl.ds(at_x, 1), :], mats_ref[pl.ds(at_x + 1, 1), :]
    ch, sh, cz = (mats_ref[pl.ds(at_z + n, 1), :] for n in range(3))
    lane = lax.broadcasted_iota(jnp.int32, (1, 128), 1)
    first = lane < 64
    mass7, inv7, ratio7, mask7 = (mats_ref[n : n + 1, :] for n in range(LANES_AT, LANES_AT + 4))
    mass3, inv3, ratio3, mask3 = (mats_ref[n : n + 1, :] for n in range(LANES_AT + 4, LANES_AT + 8))
    mask1 = mats_ref[LANES_AT + 8 : LANES_AT + 9, :]

    both = (cx, sx)
    alone = lambda c: (c, jnp.zeros_like(c))
    operator = [both, alone(ch), alone(sh), alone(cz)]
    transfer = [both, alone(ch), (cx * ch, sx * ch), alone(sh), (cx * sh, sx * sh)]

    def mode_table(at, rows, phases):
        top = mats_ref[at : at + rows]
        low = pltpu.roll(top, 64, axis=1)
        for c, s in phases:
            at += rows
            t = mats_ref[at : at + rows]
            top = top + jnp.where(first, c, s) * t
            low = low + jnp.where(first, -s, c) * pltpu.roll(t, 64, axis=1)
        if rows == 64:
            return jnp.concatenate([top, low], axis=0)
        square[...] = jnp.zeros((128, 128), f32)
        square[0:rows] = top
        square[64 : 64 + rows] = low
        return square[...]

    store_table(g7_ref, mode_table(G7_AT, 64, operator))
    store_table(g3_ref, mode_table(G3_AT, 24, operator))
    table = mode_table(P7_AT, 24, transfer)
    store_table(p7_ref, table)
    store_table(r7_ref, (table * mass7).T * inv3)
    table = mode_table(P3_AT, 8, transfer)
    store_table(p3_ref, table)
    store_table(r3_ref, (table * mass3).T)

    scale = inv7 * (1.0 / (NX * NZ))
    outer = lane % 64 < 32
    square[...] = jnp.zeros((128, 128), f32)
    for t in range(4):
        for y, half, part in PIECES:
            r, v = 64 * part + 32 * y + 13 * half, 52 * (2 * t + y) + 26 * half + 13 * part
            square[r : r + 13, :] = in_ref[v : v + 13, :]
        both = square[...].T
        low, high = both[:64], both[64:]
        w_ref[128 * t : 128 * t + 64, :] = jnp.where(outer, low, pltpu.roll(high, 32, axis=1)) * scale
        w_ref[128 * t + 64 : 128 * t + 128, :] = jnp.where(outer, pltpu.roll(low, 96, axis=1), high) * scale
    w_ref[512:, :] = jnp.zeros((w_ref.shape[0] - 512, 128), f32)
    h = h_ref[...]
    row = lax.broadcasted_iota(jnp.int32, (ROWS, 128), 0)
    inv = jnp.where(row < NY, 1.0 / jnp.where(row < NY, h, 1.0), 0.0)
    g = 2.0 * inv
    h_pair = h + roll_down(h)
    g_pair = g + roll_down(g)
    inv_pair = jnp.where(row <= NY, 1.0 / jnp.where(row <= NY, h_pair, 1.0), 0.0)
    geo_ref[0] = h
    geo_ref[1] = g
    geo_ref[2] = inv_pair
    geo_ref[3] = g * inv

    def inverse_diags(d, level, ratio, mask):
        start, steps = cheb_steps(level.bound, SMOOTH_STEPS, smooth_floor)
        for k in range(level.q):
            wall = geo_ref[3] if k else g_pair * inv_pair
            total = ratio + float(level.stiff[k, k]) * wall
            used = (row < NY if k else row <= NY) & (mask > 0.0)
            total = jnp.where(used, 1.0 / jnp.where(used, total, 1.0), 0.0)
            for n, factor in enumerate([start] + [beta for _, beta in steps]):
                d[n, k] = factor * total

    inverse_diags(d7, FINE, ratio7, mask7)
    inverse_diags(d3, MID, ratio3, mask3)
    d1_mix = (4.0 + screen_shift) - 2.0 * cx - 2.0 * cz
    d1 = h_pair * (4.0 + screen_shift) + g_pair
    used = (row <= NY) & (mask1 > 0.0)
    d1 = jnp.where(used, 1.0 / jnp.where(used, d1, 1.0), 0.0)

    for k in range(7):
        factor = float(1.0 / FINE.weight[k]) * (inv if k else inv_pair)
        r7[k] = factor * w_ref[pl.ds(k, ROWS, stride=7), :]

    def apply(level, u, table):
        q = level.q
        m = table_product(u[...].reshape(q * ROWS, 128), table)
        wall = element_products(level.stiff, q, [u[k] for k in range(q)])
        shared = geo_ref[1] * wall[0] + roll_down(geo_ref[1] * wall[q])
        out = [m[:ROWS] + geo_ref[2] * shared]
        return out + [m[k * ROWS : (k + 1) * ROWS] + geo_ref[3] * wall[k] for k in range(1, q)]

    def smooth(level, u, r, x, d, table, fresh, keep_residual):
        q = level.q
        steps = cheb_steps(level.bound, SMOOTH_STEPS, smooth_floor)[1]
        for k in range(q):
            t = d[0, k] * r[k]
            u[k] = t
            x[k] = t if fresh else x[k] + t
        for n, (alpha, _) in enumerate(steps):
            au = apply(level, u, table)
            for k in range(q):
                t = r[k] - au[k]
                r[k] = t
                t = alpha * u[k] + d[n + 1, k] * t
                u[k] = t
                x[k] = x[k] + t
        if keep_residual:
            au = apply(level, u, table)
            for k in range(q):
                r[k] = r[k] - au[k]

    def product(planes, table):
        m = table_product(jnp.concatenate(planes, axis=0), table)
        return [m[k * ROWS : (k + 1) * ROWS] for k in range(len(planes))]

    smooth(FINE, u7, r7, x7, d7, g7_ref, True, True)
    down = product(restrict_wall(R7, 7, 3, [r7[k] for k in range(7)], geo_ref[0], geo_ref[2]), r7_ref)
    for k in range(3):
        r3[k] = down[k]

    smooth(MID, u3, r3, x3, d3, g3_ref, True, True)
    r1 = product(restrict_wall(R3, 3, 1, [r3[k] for k in range(3)], geo_ref[0], geo_ref[2]), r3_ref)[0]

    start, steps = cheb_steps(LOW.bound, COARSE_STEPS, coarse_floor)
    middle = d1 * (h_pair * d1_mix + g_pair)
    after, before = d1 * g, d1 * roll_down(g)
    r1 = (d1 * h_pair) * r1
    u1 = start * r1
    x1 = u1
    for alpha, beta in steps:
        r1 = (r1 - middle * u1) + (after * roll_up(u1) + before * roll_down(u1))
        u1 = alpha * u1 + beta * r1
        x1 = x1 + u1

    up = prolong_wall(J3, 3, 1, product([x1], p3_ref))
    for k in range(3):
        u3[k] = up[k]
        x3[k] = x3[k] + up[k]
    au = apply(MID, u3, g3_ref)
    for k in range(3):
        r3[k] = r3[k] - au[k]
    smooth(MID, u3, r3, x3, d3, g3_ref, False, False)

    up = prolong_wall(J7, 7, 3, product([x3[k] for k in range(3)], p7_ref))
    for k in range(7):
        u7[k] = up[k]
        x7[k] = x7[k] + up[k]
    au = apply(FINE, u7, g7_ref)
    for k in range(7):
        r7[k] = r7[k] - au[k]
    smooth(FINE, u7, r7, x7, d7, g7_ref, False, False)

    for k in range(7):
        w_ref[pl.ds(k, ROWS, stride=7), :] = x7[k]
    for t in range(4):
        low, high = w_ref[128 * t : 128 * t + 64, :], w_ref[128 * t + 64 : 128 * t + 128, :]
        square[...] = jnp.concatenate(
            [
                jnp.where(outer, low, pltpu.roll(high, 32, axis=1)),
                jnp.where(outer, pltpu.roll(low, 96, axis=1), high),
            ],
            axis=0,
        ).T
        for y, half, part in PIECES:
            r, v = 64 * part + 32 * y + 13 * half, 52 * (2 * t + y) + 26 * half + 13 * part
            out_ref[v : v + 13, :] = square[r : r + 13, :]


VMEM = pl.BlockSpec(memory_space=pltpu.VMEM)
HBM = pl.BlockSpec(memory_space=pltpu.HBM)
PARAMS = pltpu.CompilerParams(vmem_limit_bytes=32 * 1024 * 1024)
FLAT = jax.ShapeDtypeStruct((FIELD, 128), f32)
TIGHT = jax.ShapeDtypeStruct((USED, 128), f32)
LINES = [pltpu.VMEM((8, 56, 128), f32)]


def exchange(block, axes):
    n, rows = lax.axis_size(axes), block.shape[0]
    block = block.reshape(n, rows // n, 1, 128)
    return lax.all_to_all(block, axes, 0, 0).reshape(rows, 128)


def cycle_call(heights, modes):
    fine = pltpu.VMEM((7, ROWS, 128), f32)
    mid = pltpu.VMEM((3, ROWS, 128), f32)
    table = pltpu.VMEM((256, 256), bf16)
    return pl.pallas_call(
        cycle_kernel, out_shape=FLAT,
        in_specs=[VMEM, VMEM, VMEM], out_specs=VMEM,
        scratch_shapes=[
            pltpu.VMEM((7 * ROWS, 128), f32), pltpu.VMEM((4, ROWS, 128), f32),
            fine, fine, fine, pltpu.VMEM((SMOOTH_STEPS, 7, ROWS, 128), f32),
            mid, mid, mid, pltpu.VMEM((SMOOTH_STEPS, 3, ROWS, 128), f32),
            pltpu.VMEM((128, 128), f32), table, table, table, table, table, table,
        ],
        compiler_params=PARAMS,
    )(
        heights, jnp.asarray(MATRICES), modes,
    )


def transform(kernel, block, out_shape=FLAT, scratch=()):
    return pl.pallas_call(
        kernel, out_shape=out_shape, in_specs=[VMEM], out_specs=VMEM,
        scratch_shapes=scratch, compiler_params=PARAMS,
    )(block)


def body(residual, layer_heights):
    stay = lambda v: pltpu.with_memory_space_constraint(v, pltpu.HBM)
    packed, heights = pl.pallas_call(
        pack_kernel, out_shape=(TIGHT, jax.ShapeDtypeStruct((ROWS, 128), f32)),
        in_specs=[HBM, HBM], out_specs=(VMEM, VMEM),
        scratch_shapes=[
            pltpu.VMEM((7, 14, 512), f32), pltpu.VMEM((1, NY), f32), pltpu.VMEM((8, 128), f32),
            pltpu.SemaphoreType.DMA((2,)),
        ],
        compiler_params=PARAMS,
    )(stay(residual), stay(layer_heights.reshape(1, NY)))
    spans = transform(span_forward_kernel, exchange(packed, SPAN), scratch=LINES)
    modes = exchange(transform(flow_forward_kernel, exchange(spans, FLOW)), LAST)
    solved = exchange(cycle_call(heights, modes), LAST)
    flows = exchange(transform(flow_backward_kernel, solved), FLOW)
    spread = exchange(transform(span_backward_kernel, flows, TIGHT, LINES), SPAN)
    return pl.pallas_call(
        unpack_kernel, out_shape=jax.ShapeDtypeStruct((7, 14, 512), f32),
        in_specs=[VMEM], out_specs=VMEM, compiler_params=PARAMS,
    )(spread)


def solution(mesh):
    split = Mesh(mesh.devices.reshape(4, 2, 2, 2, 2, 4), FLOW + SPAN)
    spec = P(FLOW, SPAN, None)
    return jax.shard_map(
        body, mesh=split, in_specs=(spec, P()), out_specs=spec, check_vma=False
    )
```

```python
import jax
import jax.numpy as jnp
import ml_dtypes
import numpy as np
from jax import lax
from jax.experimental import pallas as pl
from jax.experimental.pallas import tpu as pltpu
from jax.sharding import Mesh
from jax.sharding import PartitionSpec as P


SMOOTH_STEPS = 3
COARSE_STEPS = 12
NX, NZ, NY = 32, 16, 73
DEVICES = 256
ROWS = 80
screen_shift = 0.02
smooth_floor = 0.1
coarse_floor = 0.01
f32 = jnp.float32
bf16 = jnp.bfloat16


def legendre_values(points, degree):
    columns = [np.ones(points.shape), points]
    for n in range(2, degree + 1):
        columns.append(((2 * n - 1) * points * columns[-1] - (n - 1) * columns[-2]) / n)
    return np.stack(columns[: degree + 1], axis=1)


def gll_tables(degree):
    nodes = -np.cos(np.pi * np.arange(degree + 1) / degree)
    for _ in range(100):
        values = legendre_values(nodes, degree)
        nodes = nodes - (nodes * values[:, degree] - values[:, degree - 1]) / (
            (degree + 1) * values[:, degree]
        )
    leading = legendre_values(nodes, degree)[:, degree]
    weights = 2.0 / (degree * (degree + 1) * leading**2)
    differ = np.zeros((degree + 1, degree + 1))
    for i in range(degree + 1):
        for j in range(degree + 1):
            if i != j:
                differ[i, j] = leading[i] / (leading[j] * (nodes[i] - nodes[j]))
    differ[0, 0] = -degree * (degree + 1) / 4.0
    differ[degree, degree] = degree * (degree + 1) / 4.0
    return nodes, weights, differ.T @ (weights[:, None] * differ)


def interp_table(fine_degree, coarse_degree):
    fine_nodes = gll_tables(fine_degree)[0]
    coarse_nodes = gll_tables(coarse_degree)[0]
    lagrange = np.ones((fine_degree + 1, coarse_degree + 1))
    for col in range(coarse_degree + 1):
        for other in range(coarse_degree + 1):
            if other != col:
                lagrange[:, col] *= (fine_nodes - coarse_nodes[other]) / (
                    coarse_nodes[col] - coarse_nodes[other]
                )
    return lagrange


def lane_at(a, b):
    n = 7 * b + a
    return n if n < 25 else n + 7


def lanes_of(values):
    n = values.shape[0]
    out = np.zeros(64)
    for a in range(n):
        for b in range(n):
            out[lane_at(a, b)] = values[a, b]
    return out


def square_of(matrix, n_out, n_in):
    rows = [lane_at(a, b) for a in range(n_out) for b in range(n_out)]
    columns = [lane_at(a, b) for a in range(n_in) for b in range(n_in)]
    out = np.zeros((64, 64))
    out[np.ix_(rows, columns)] = matrix
    return out


def line_basis(q, t):
    u = np.zeros((q, q), complex)
    u[0, 0] = 1.0
    turn = np.exp(-0.5j * t) / np.sqrt(2.0)
    for a in range(1, (q + 1) // 2):
        u[a, a] = u[a, q - a] = turn
        u[q - a, a], u[q - a, q - a] = -1j * turn, 1j * turn
    return u


def closing(q, t):
    out = np.eye(q + 1, q, dtype=complex)
    out[q, 0] = np.exp(1j * t)
    return out


def real_parts(matrix_of, count):
    angles = 0.3 + 0.7 * np.arange(8)
    terms = np.stack([np.ones(8), np.cos(angles / 2), np.sin(angles / 2), np.cos(angles)], 1)[:, :count]
    values = np.stack([matrix_of(t) for t in angles])
    flat = values.reshape(8, -1)
    parts = np.linalg.lstsq(terms, flat.real, rcond=None)[0]
    assert np.abs(terms @ parts - flat).max() < 1e-11 * np.abs(flat).max()
    return parts.reshape((count,) + values.shape[1:])


class Level:
    def __init__(self, q):
        self.q = q
        _, w, s = gll_tables(q)
        self.w, self.s = w, s
        mass = 0.5 * w[:q].copy()
        mass[0] = 0.5 * (w[0] + w[q])
        diag = 2.0 * np.diag(s)[:q].copy()
        diag[0] = 2.0 * (s[0, 0] + s[q, q])
        self.mxz = np.outer(mass, mass)
        a = np.outer(diag, mass) + np.outer(mass, diag) + screen_shift * self.mxz
        self.ratio = lanes_of(a / self.mxz)
        spread = np.abs(s).sum(axis=1)
        self.bound = max(1.0, float(np.max(spread / np.diag(s))))
        base = 2.0 * s[:q, :q].copy()
        base[0, 0] += 2.0 * s[q, q]
        e1 = np.zeros((q, q))
        e1[:, 0] = 2.0 * s[:q, q]
        even, odd = e1 + e1.T, e1 - e1.T
        dm = np.diag(mass)
        scale = np.concatenate([lanes_of(1.0 / self.mxz)] * 2)[None, :]
        sq = lambda m: square_of(m, q, q)
        span = real_parts(
            lambda t: line_basis(q, t) @ closing(q, t).conj().T @ (2.0 * s) @ closing(q, t) @ line_basis(q, t).conj().T, 4
        )
        fixed = sq(np.kron(base, dm) + np.kron(dm, span[0]) + screen_shift * np.kron(dm, dm))
        tables = [np.hstack([fixed, 0.0 * fixed])]
        tables.append(np.hstack([sq(np.kron(even, dm)), -sq(np.kron(odd, dm))]))
        for part in span[1:]:
            part = sq(np.kron(dm, part))
            tables.append(np.hstack([part, 0.0 * part]))
        self.tables = [(t * scale)[: 64 if q > 3 else 24] for t in tables]
        self.weight = 0.5 * w
        self.stiff = s / self.weight[:, None]
        self.mass_lanes = np.concatenate([lanes_of(self.mxz)] * 2)
        self.inv_mass_lanes = np.concatenate([lanes_of(1.0 / self.mxz)] * 2)
        self.ratio_lanes = np.concatenate([self.ratio] * 2)
        self.mask_lanes = (self.mass_lanes > 0).astype(np.float64)


def transfer_tables(fine, coarse):
    j = interp_table(fine, coarse)
    ja = j[:fine, :coarse]
    jb = np.zeros((fine, coarse))
    jb[:, 0] = j[:fine, coarse]
    span = real_parts(
        lambda t: line_basis(fine, t) @ j[:fine] @ closing(coarse, t) @ line_basis(coarse, t).conj().T, 3
    )
    tables = []
    for part in span:
        for flow in (ja, jb):
            b = square_of(np.kron(flow, part), fine, coarse).T[: 24 if coarse > 1 else 8]
            tables.append(np.hstack([b, b if flow is jb else 0.0 * b]))
    return j, tables


def phase_rows():
    rows = np.zeros((80, 2, 64))
    for n in range(16):
        t = 2 * np.pi * n / NX
        if n:
            rows[2 * n], rows[2 * n + 1] = np.cos(t), np.sin(t)
        else:
            rows[0, 0], rows[0, 1] = 1.0, -1.0
    for k in range(8):
        for part in range(2):
            t = 2 * np.pi * k / NZ if k else np.pi * part
            at = 32 + 3 * (2 * k + part)
            rows[at], rows[at + 1], rows[at + 2] = np.cos(t / 2), np.sin(t / 2), np.cos(t)
    return rows.reshape(80, 128)


FINE, MID, LOW = Level(7), Level(3), Level(1)
J7, P7_TABLES = transfer_tables(7, 3)
J3, P3_TABLES = transfer_tables(3, 1)
MATRICES = np.concatenate(FINE.tables + MID.tables + P7_TABLES + P3_TABLES).astype(np.float32)
R7 = FINE.weight[:, None] * J7 / MID.weight
R3 = MID.weight[:, None] * J3 / LOW.weight
G7_AT, G3_AT, P7_AT, P3_AT = 0, 320, 440, 584


LANES = np.zeros((16, 128))
for n, level in enumerate((FINE, MID)):
    LANES[4 * n] = level.mass_lanes
    LANES[4 * n + 1] = level.inv_mass_lanes
    LANES[4 * n + 2] = level.ratio_lanes
    LANES[4 * n + 3] = level.mask_lanes
LANES[8] = LOW.mask_lanes
MATRICES = np.concatenate([MATRICES, LANES, phase_rows()]).astype(np.float32)
LANES_AT, PHASES_AT = 632, 648


def cheb_steps(bound, sweeps, floor):
    centre = bound * (1.0 + floor) / 2.0
    half = bound * (1.0 - floor) / 2.0
    s = centre / half
    p = 1.0 / s
    steps = []
    for _ in range(sweeps - 1):
        p_next = 1.0 / (2.0 * s - p)
        steps.append((p_next * p, 2.0 * p_next / half))
        p = p_next
    return 1.0 / centre, steps


FLOW, SPAN = ("zh", "z0", "xh", "core"), ("xl", "y")
LAST = ("core", "xl", "y")
USED = 8 * 49
SLAB = 13
FIELD = 32 * SLAB


def swap(v):
    return pltpu.roll(v, 64, axis=1)


def mix(first, v, w):
    return jnp.where(first, v, swap(w)), jnp.where(first, swap(v), w)


def pack_kernel(x_hbm, h_hbm, o_ref, rows_ref, x_ref, h_ref, line_ref, sems):
    line = pltpu.make_async_copy(h_hbm, h_ref, sems.at[0])
    line.start()
    field = pltpu.make_async_copy(x_hbm, x_ref, sems.at[1])
    field.start()
    first, _ = lane_tools()
    line_ref[...] = jnp.zeros_like(line_ref)
    line.wait()
    line_ref[0:1, 0:NY] = h_ref[...]
    rows_ref[...] = jnp.broadcast_to(line_ref[0:1, :], (128, 128)).T[:ROWS]
    field.wait()
    for a in range(7):
        for t in range(4):
            part = slice(128 * t, 128 * t + 128)
            low, high = mix(first, x_ref[a, 0:7, part], x_ref[a, 7:14, part])
            o_ref[pl.ds(98 * t + a, 7, stride=7), :] = low
            o_ref[pl.ds(98 * t + 49 + a, 7, stride=7), :] = high


def unpack_kernel(x_ref, o_ref):
    first, _ = lane_tools()
    for a in range(7):
        for t in range(4):
            part = slice(128 * t, 128 * t + 128)
            low, high = mix(
                first,
                x_ref[pl.ds(98 * t + a, 7, stride=7), :],
                x_ref[pl.ds(98 * t + 49 + a, 7, stride=7), :],
            )
            o_ref[a, 0:7, part] = low
            o_ref[a, 7:14, part] = high


def halves(v):
    high = v.astype(bf16)
    return high, (v - high.astype(f32)).astype(bf16)


def dot(a, b):
    return jnp.dot(a, b, preferred_element_type=f32)


HALF = float(np.sqrt(0.5))


def lane_tools():
    first = lax.broadcasted_iota(jnp.int32, (1, 128), 1) < 64
    return first, jnp.where(first, 1.0, -1.0).astype(f32)


def span_modes(x, first, sign, offset, size):
    s = [None] + [x[j] + x[8 - j] for j in (1, 2, 3)]
    d = [None] + [x[j] - x[8 - j] for j in (1, 2, 3)]
    up, down = x[0] + x[4], x[0] - x[4]
    odd, turn = s[1] + s[3], HALF * (s[1] - s[3])
    slope = HALF * (d[1] + d[3])
    re = [up + s[2] + odd, down + turn, up - s[2], down - turn, up + s[2] - odd]
    im = [None, -slope - d[2], d[3] - d[1], d[2] - slope]

    def phases(k):
        t = np.pi * k / 8
        p = 0.0 if offset is None else t / 2 + offset
        return [float(size * v) for v in (np.cos(p), np.sin(p), np.cos(p + t), np.sin(p + t))]

    flip = swap(re[0])
    out = [None] * 8
    out[0] = jnp.where(first, re[0] + flip, flip - re[0])
    c, s, v, w = phases(4)
    out[4] = jnp.where(first, c, -w) * re[4] + jnp.where(first, v, -s) * swap(re[4])
    for f in (1, 2, 3):
        re_swap, im_swap = swap(re[f]), swap(im[f])
        a = jnp.where(first, re[f], im_swap)
        b = jnp.where(first, im[f], -re_swap)
        p = jnp.where(first, re_swap, im[f])
        q = jnp.where(first, im_swap, -re[f])
        c, s, v, w = phases(f)
        out[f] = (c * a + v * p) + (s * b + w * q)
        c, s, v, w = phases(8 - f)
        out[8 - f] = sign * ((c * a + v * p) - (s * b + w * q))
    return out


def span_elements(x, first, sign, offset, size):
    def phases(k):
        t = np.pi * k / 8
        p = 0.0 if offset is None else t / 2 + offset
        return [float(size * v) for v in (np.cos(p), np.sin(p), np.cos(p + t), np.sin(p + t))]

    pick = lambda p, q: jnp.where(first, p, q)
    flip = swap(x[0])
    re = [jnp.where(first, x[0] + flip, flip - x[0])]
    im = [None]
    for f in (1, 2, 3):
        c, s, v, w = [2.0 * n for n in phases(f)]
        near, near_swap = x[f], swap(x[f])
        one = pick(c, -w) * near + pick(-s, v) * near_swap
        two = pick(s, v) * near + pick(c, w) * near_swap
        c, s, v, w = [2.0 * n for n in phases(8 - f)]
        far, far_swap = x[8 - f], swap(x[8 - f])
        re.append(one + (pick(c, -w) * far + pick(-s, v) * far_swap))
        im.append(two - (pick(s, v) * far + pick(c, w) * far_swap))
    c, s, v, w = [2.0 * n for n in phases(4)]
    re.append(pick(c, -w) * x[4] + pick(-s, v) * swap(x[4]))
    up, down = re[0] + re[4], re[0] - re[4]
    odd, turn = re[1] + re[3], HALF * (re[1] - re[3])
    slope = HALF * (im[1] + im[3])
    c = [up + re[2] + odd, down + turn, up - re[2], down - turn, up + re[2] - odd]
    s = [None, slope + im[2], im[1] - im[3], slope - im[2]]
    return [c[0]] + [c[j] - s[j] for j in (1, 2, 3)] + [c[4]] + [c[j] + s[j] for j in (3, 2, 1)]


def mode_rows(k, part):
    return 26 * (4 * (k // 2) + 2 * part + k % 2)


def span_forward_kernel(x_ref, o_ref, v_ref):
    first, sign = lane_tools()
    for k in range(8):
        v_ref[k, 48:56] = jnp.zeros((8, 128), f32)
    nodes = lambda b: [x_ref[49 * j + 7 * b : 49 * j + 7 * b + 7, :] for j in range(8)]
    for k, v in enumerate(span_modes(nodes(0), first, sign, None, 1.0)):
        v_ref[k, 0:7] = v
    for b in (1, 2, 3):
        near, far = nodes(b), nodes(7 - b)
        total = span_modes([p + q for p, q in zip(near, far)], first, sign, 0.0, HALF)
        differ = span_modes([p - q for p, q in zip(near, far)], first, sign, np.pi / 2, HALF)
        total[0], differ[0] = HALF * total[0], -HALF * differ[0]
        for k in range(8):
            v_ref[k, 7 * b : 7 * b + 7] = total[k]
            v_ref[k, 7 * (7 - b) : 7 * (7 - b) + 7] = differ[k]
    for k in range(8):
        re, im = mix(first, v_ref[k, 0:26], v_ref[k, 25:51])
        o_ref[mode_rows(k, 0) : mode_rows(k, 0) + 26, :] = re
        o_ref[mode_rows(k, 1) : mode_rows(k, 1) + 26, :] = im


def span_backward_kernel(x_ref, o_ref, v_ref):
    first, sign = lane_tools()
    for k in range(8):
        near, far = mix(
            first,
            x_ref[mode_rows(k, 0) : mode_rows(k, 0) + 26, :],
            x_ref[mode_rows(k, 1) : mode_rows(k, 1) + 26, :],
        )
        v_ref[k, 0:25] = near[0:25]
        v_ref[k, 25:49] = far[0:24]

    def store(b, planes):
        for j, v in enumerate(planes):
            o_ref[49 * j + 7 * b : 49 * j + 7 * b + 7, :] = v

    store(0, span_elements([v_ref[k, 0:7] for k in range(8)], first, sign, None, 1.0))
    for b in (1, 2, 3):
        total = [v_ref[k, 7 * b : 7 * b + 7] for k in range(8)]
        differ = [v_ref[k, 7 * (7 - b) : 7 * (7 - b) + 7] for k in range(8)]
        total[0], differ[0] = HALF * total[0], -HALF * differ[0]
        total = span_elements(total, first, sign, 0.0, HALF)
        differ = span_elements(differ, first, sign, np.pi / 2, HALF)
        store(b, [p + q for p, q in zip(total, differ)])
        store(7 - b, [p - q for p, q in zip(total, differ)])


def line_modes(x):
    n = len(x)
    if n == 1:
        return [(x[0], None)]
    even, odd = line_modes(x[0::2]), line_modes(x[1::2])
    out = [None] * (n // 2 + 1)
    out[0], out[n // 2] = (even[0][0] + odd[0][0], None), (even[0][0] - odd[0][0], None)
    for k in range(1, n // 4 + 1):
        (p, q), (v, w) = even[k], odd[k]
        if 4 * k == n:
            out[k] = (p, -v)
            continue
        c, s = float(np.cos(2 * np.pi * k / n)), float(np.sin(2 * np.pi * k / n))
        re, im = c * v + s * w, c * w - s * v
        out[k], out[n // 2 - k] = (p + re, q + im), (p - re, im - q)
    return out


def line_elements(modes, n):
    if n == 1:
        return [modes[0][0]]
    even, odd = [None] * (n // 4 + 1), [None] * (n // 4 + 1)
    low, high = modes[0][0], modes[n // 2][0]
    even[0], odd[0] = (low + high, None), (low - high, None)
    for k in range(1, n // 4 + 1):
        (p, q), (v, w) = modes[k], modes[n // 2 - k]
        if 4 * k == n:
            even[k], odd[k] = (2.0 * p, None), (-2.0 * q, None)
            continue
        c, s = float(np.cos(2 * np.pi * k / n)), float(np.sin(2 * np.pi * k / n))
        re, im = p - v, q + w
        even[k], odd[k] = (p + v, q - w), (c * re - s * im, c * im + s * re)
    x, y = line_elements(even, n // 2), line_elements(odd, n // 2)
    return [v for pair in zip(x, y) for v in pair]


def slab(ref, n):
    return ref[n * SLAB : n * SLAB + SLAB, :]


def flow_forward_kernel(x_ref, o_ref):
    modes = line_modes([slab(x_ref, n) for n in range(NX)])
    for n in range(16):
        re, im = modes[n][0], modes[n][1] if n else modes[16][0]
        o_ref[26 * n : 26 * n + 13, :] = re
        o_ref[26 * n + 13 : 26 * n + 26, :] = im


def flow_backward_kernel(x_ref, o_ref):
    modes = [(slab(x_ref, 2 * n), slab(x_ref, 2 * n + 1)) for n in range(16)]
    modes = [(modes[0][0], None)] + modes[1:] + [(modes[0][1], None)]
    for n, v in enumerate(line_elements(modes, NX)):
        o_ref[n * SLAB : n * SLAB + SLAB, :] = v


def table_product(v, t_ref):
    both = dot(jnp.concatenate(halves(v), axis=1), t_ref[...])
    return both[:, :128] + both[:, 128:]


def store_table(t_ref, table):
    high, low = halves(table)
    t_ref[0:128, 0:128] = high
    t_ref[128:256, 0:128] = high
    t_ref[0:128, 128:256] = low
    t_ref[128:256, 128:256] = jnp.zeros((128, 128), bf16)


def roll_up(v):
    return pltpu.roll(v, ROWS - 1, axis=0)


def roll_down(v):
    return pltpu.roll(v, 1, axis=0)


def element_products(s, q, planes):
    parts = list(planes) + [roll_up(planes[0])]
    n = q + 1
    half = n // 2
    even = [parts[l] + parts[q - l] for l in range(half)]
    odd = [parts[l] - parts[q - l] for l in range(half)]
    out = [None] * n
    for k in range(half):
        p = m = None
        for l in range(half):
            ce = 0.5 * (s[k, l] + s[k, q - l])
            co = 0.5 * (s[k, l] - s[k, q - l])
            te, to = float(ce) * even[l], float(co) * odd[l]
            p = te if p is None else p + te
            m = to if m is None else m + to
        out[k] = p + m
        out[q - k] = p - m
    return out


def weighted_sum(coefs, planes):
    total = None
    for c, v in zip(coefs, planes):
        c = float(c)
        if c == 0.0:
            continue
        t = v if c == 1.0 else c * v
        total = t if total is None else total + t
    return total


def restrict_wall(j, fine, coarse, planes, h, inv_pair):
    out = [weighted_sum(j[1:fine, c], planes[1:]) for c in range(coarse)]
    shared = h * out[0] + roll_down(h * weighted_sum(j[1:fine, coarse], planes[1:]))
    out[0] = float(j[0, 0]) * planes[0] + inv_pair * shared
    return out


def prolong_wall(j, fine, coarse, planes):
    closed = list(planes) + [roll_up(planes[0])]
    return [weighted_sum(j[k], closed) for k in range(fine)]


PIECES = [(y, half, part) for y in range(2) for half in range(2) for part in range(2)]


def cycle_kernel(
    h_ref, mats_ref, in_ref, out_ref,
    w_ref, geo_ref,
    u7, r7, x7, d7, u3, r3, x3, d3,
    square, g7_ref, g3_ref, r7_ref, p7_ref, r3_ref, p3_ref,
):
    at_x = PHASES_AT + 2 * lax.axis_index(LAST)
    at_z = PHASES_AT + 32 + 3 * lax.axis_index(("zh", "xh", "z0"))
    cx, sx = mats_ref[pl.ds(at_x, 1), :], mats_ref[pl.ds(at_x + 1, 1), :]
    ch, sh, cz = (mats_ref[pl.ds(at_z + n, 1), :] for n in range(3))
    lane = lax.broadcasted_iota(jnp.int32, (1, 128), 1)
    first = lane < 64
    mass7, inv7, ratio7, mask7 = (mats_ref[n : n + 1, :] for n in range(LANES_AT, LANES_AT + 4))
    mass3, inv3, ratio3, mask3 = (mats_ref[n : n + 1, :] for n in range(LANES_AT + 4, LANES_AT + 8))
    mask1 = mats_ref[LANES_AT + 8 : LANES_AT + 9, :]

    both = (cx, sx)
    alone = lambda c: (c, jnp.zeros_like(c))
    operator = [both, alone(ch), alone(sh), alone(cz)]
    transfer = [both, alone(ch), (cx * ch, sx * ch), alone(sh), (cx * sh, sx * sh)]

    def mode_table(at, rows, phases):
        top = mats_ref[at : at + rows]
        low = pltpu.roll(top, 64, axis=1)
        for c, s in phases:
            at += rows
            t = mats_ref[at : at + rows]
            top = top + jnp.where(first, c, s) * t
            low = low + jnp.where(first, -s, c) * pltpu.roll(t, 64, axis=1)
        if rows == 64:
            return jnp.concatenate([top, low], axis=0)
        square[...] = jnp.zeros((128, 128), f32)
        square[0:rows] = top
        square[64 : 64 + rows] = low
        return square[...]

    store_table(g7_ref, mode_table(G7_AT, 64, operator))
    store_table(g3_ref, mode_table(G3_AT, 24, operator))
    table = mode_table(P7_AT, 24, transfer)
    store_table(p7_ref, table)
    store_table(r7_ref, (table * mass7).T * inv3)
    table = mode_table(P3_AT, 8, transfer)
    store_table(p3_ref, table)
    store_table(r3_ref, (table * mass3).T)

    scale = inv7 * (1.0 / (NX * NZ))
    outer = lane % 64 < 32
    square[...] = jnp.zeros((128, 128), f32)
    for t in range(4):
        for y, half, part in PIECES:
            r, v = 64 * part + 32 * y + 13 * half, 208 * half + 26 * (2 * t + y) + 13 * part
            square[r : r + 13, :] = in_ref[v : v + 13, :]
        both = square[...].T
        low, high = both[:64], both[64:]
        w_ref[128 * t : 128 * t + 64, :] = jnp.where(outer, low, pltpu.roll(high, 32, axis=1)) * scale
        w_ref[128 * t + 64 : 128 * t + 128, :] = jnp.where(outer, pltpu.roll(low, 96, axis=1), high) * scale
    w_ref[512:, :] = jnp.zeros((w_ref.shape[0] - 512, 128), f32)
    h = h_ref[...]
    row = lax.broadcasted_iota(jnp.int32, (ROWS, 128), 0)
    inv = jnp.where(row < NY, 1.0 / jnp.where(row < NY, h, 1.0), 0.0)
    g = 2.0 * inv
    h_pair = h + roll_down(h)
    g_pair = g + roll_down(g)
    inv_pair = jnp.where(row <= NY, 1.0 / jnp.where(row <= NY, h_pair, 1.0), 0.0)
    geo_ref[0] = h
    geo_ref[1] = g
    geo_ref[2] = inv_pair
    geo_ref[3] = g * inv

    def inverse_diags(d, level, ratio, mask):
        start, steps = cheb_steps(level.bound, SMOOTH_STEPS, smooth_floor)
        for k in range(level.q):
            wall = geo_ref[3] if k else g_pair * inv_pair
            total = ratio + float(level.stiff[k, k]) * wall
            used = (row < NY if k else row <= NY) & (mask > 0.0)
            total = jnp.where(used, 1.0 / jnp.where(used, total, 1.0), 0.0)
            for n, factor in enumerate([start] + [beta for _, beta in steps]):
                d[n, k] = factor * total

    inverse_diags(d7, FINE, ratio7, mask7)
    inverse_diags(d3, MID, ratio3, mask3)
    d1_mix = (4.0 + screen_shift) - 2.0 * cx - 2.0 * cz
    d1 = h_pair * (4.0 + screen_shift) + g_pair
    used = (row <= NY) & (mask1 > 0.0)
    d1 = jnp.where(used, 1.0 / jnp.where(used, d1, 1.0), 0.0)

    for k in range(7):
        factor = float(1.0 / FINE.weight[k]) * (inv if k else inv_pair)
        r7[k] = factor * w_ref[pl.ds(k, ROWS, stride=7), :]

    def apply(level, u, table):
        q = level.q
        m = table_product(u[...].reshape(q * ROWS, 128), table)
        wall = element_products(level.stiff, q, [u[k] for k in range(q)])
        shared = geo_ref[1] * wall[0] + roll_down(geo_ref[1] * wall[q])
        out = [m[:ROWS] + geo_ref[2] * shared]
        return out + [m[k * ROWS : (k + 1) * ROWS] + geo_ref[3] * wall[k] for k in range(1, q)]

    def smooth(level, u, r, x, d, table, fresh, keep_residual):
        q = level.q
        steps = cheb_steps(level.bound, SMOOTH_STEPS, smooth_floor)[1]
        for k in range(q):
            t = d[0, k] * r[k]
            u[k] = t
            x[k] = t if fresh else x[k] + t
        for n, (alpha, _) in enumerate(steps):
            au = apply(level, u, table)
            for k in range(q):
                t = r[k] - au[k]
                r[k] = t
                t = alpha * u[k] + d[n + 1, k] * t
                u[k] = t
                x[k] = x[k] + t
        if keep_residual:
            au = apply(level, u, table)
            for k in range(q):
                r[k] = r[k] - au[k]

    def product(planes, table):
        m = table_product(jnp.concatenate(planes, axis=0), table)
        return [m[k * ROWS : (k + 1) * ROWS] for k in range(len(planes))]

    smooth(FINE, u7, r7, x7, d7, g7_ref, True, True)
    down = product(restrict_wall(R7, 7, 3, [r7[k] for k in range(7)], geo_ref[0], geo_ref[2]), r7_ref)
    for k in range(3):
        r3[k] = down[k]

    smooth(MID, u3, r3, x3, d3, g3_ref, True, True)
    r1 = product(restrict_wall(R3, 3, 1, [r3[k] for k in range(3)], geo_ref[0], geo_ref[2]), r3_ref)[0]

    start, steps = cheb_steps(LOW.bound, COARSE_STEPS, coarse_floor)
    middle = d1 * (h_pair * d1_mix + g_pair)
    after, before = d1 * g, d1 * roll_down(g)
    r1 = (d1 * h_pair) * r1
    u1 = start * r1
    x1 = u1
    for alpha, beta in steps:
        r1 = (r1 - middle * u1) + (after * roll_up(u1) + before * roll_down(u1))
        u1 = alpha * u1 + beta * r1
        x1 = x1 + u1

    up = prolong_wall(J3, 3, 1, product([x1], p3_ref))
    for k in range(3):
        u3[k] = up[k]
        x3[k] = x3[k] + up[k]
    au = apply(MID, u3, g3_ref)
    for k in range(3):
        r3[k] = r3[k] - au[k]
    smooth(MID, u3, r3, x3, d3, g3_ref, False, False)

    up = prolong_wall(J7, 7, 3, product([x3[k] for k in range(3)], p7_ref))
    for k in range(7):
        u7[k] = up[k]
        x7[k] = x7[k] + up[k]
    au = apply(FINE, u7, g7_ref)
    for k in range(7):
        r7[k] = r7[k] - au[k]
    smooth(FINE, u7, r7, x7, d7, g7_ref, False, False)

    for k in range(7):
        w_ref[pl.ds(k, ROWS, stride=7), :] = x7[k]
    for t in range(4):
        low, high = w_ref[128 * t : 128 * t + 64, :], w_ref[128 * t + 64 : 128 * t + 128, :]
        square[...] = jnp.concatenate(
            [
                jnp.where(outer, low, pltpu.roll(high, 32, axis=1)),
                jnp.where(outer, pltpu.roll(low, 96, axis=1), high),
            ],
            axis=0,
        ).T
        for y, half, part in PIECES:
            r, v = 64 * part + 32 * y + 13 * half, 208 * half + 26 * (2 * t + y) + 13 * part
            out_ref[v : v + 13, :] = square[r : r + 13, :]


VMEM = pl.BlockSpec(memory_space=pltpu.VMEM)
HBM = pl.BlockSpec(memory_space=pltpu.HBM)
PARAMS = pltpu.CompilerParams(vmem_limit_bytes=32 * 1024 * 1024)
FLAT = jax.ShapeDtypeStruct((FIELD, 128), f32)
TIGHT = jax.ShapeDtypeStruct((USED, 128), f32)
LINES = [pltpu.VMEM((8, 56, 128), f32)]


def exchange(block, axes):
    n, rows = lax.axis_size(axes), block.shape[0]
    block = block.reshape(n, rows // n, 1, 128)
    return lax.all_to_all(block, axes, 0, 0).reshape(rows, 128)


def cycle_call(heights, modes):
    fine = pltpu.VMEM((7, ROWS, 128), f32)
    mid = pltpu.VMEM((3, ROWS, 128), f32)
    table = pltpu.VMEM((256, 256), bf16)
    return pl.pallas_call(
        cycle_kernel, out_shape=FLAT,
        in_specs=[VMEM, VMEM, VMEM], out_specs=VMEM,
        scratch_shapes=[
            pltpu.VMEM((7 * ROWS, 128), f32), pltpu.VMEM((4, ROWS, 128), f32),
            fine, fine, fine, pltpu.VMEM((SMOOTH_STEPS, 7, ROWS, 128), f32),
            mid, mid, mid, pltpu.VMEM((SMOOTH_STEPS, 3, ROWS, 128), f32),
            pltpu.VMEM((128, 128), f32), table, table, table, table, table, table,
        ],
        compiler_params=PARAMS,
    )(
        heights, jnp.asarray(MATRICES), modes,
    )


def transform(kernel, block, out_shape=FLAT, scratch=()):
    return pl.pallas_call(
        kernel, out_shape=out_shape, in_specs=[VMEM], out_specs=VMEM,
        scratch_shapes=scratch, compiler_params=PARAMS,
    )(block)


def body(residual, layer_heights):
    stay = lambda v: pltpu.with_memory_space_constraint(v, pltpu.HBM)
    packed, heights = pl.pallas_call(
        pack_kernel, out_shape=(TIGHT, jax.ShapeDtypeStruct((ROWS, 128), f32)),
        in_specs=[HBM, HBM], out_specs=(VMEM, VMEM),
        scratch_shapes=[
            pltpu.VMEM((7, 14, 512), f32), pltpu.VMEM((1, NY), f32), pltpu.VMEM((8, 128), f32),
            pltpu.SemaphoreType.DMA((2,)),
        ],
        compiler_params=PARAMS,
    )(stay(residual), stay(layer_heights.reshape(1, NY)))
    spans = transform(span_forward_kernel, exchange(packed, SPAN), scratch=LINES)
    modes = exchange(transform(flow_forward_kernel, exchange(spans, FLOW)), LAST)
    solved = exchange(cycle_call(heights, modes), LAST)
    flows = exchange(transform(flow_backward_kernel, solved), FLOW)
    spread = exchange(transform(span_backward_kernel, flows, TIGHT, LINES), SPAN)
    return pl.pallas_call(
        unpack_kernel, out_shape=jax.ShapeDtypeStruct((7, 14, 512), f32),
        in_specs=[VMEM], out_specs=VMEM, compiler_params=PARAMS,
    )(spread)


def solution(mesh):
    split = Mesh(mesh.devices.reshape(4, 2, 2, 2, 2, 4), FLOW + SPAN)
    spec = P(FLOW, SPAN, None)
    return jax.shard_map(
        body, mesh=split, in_specs=(spec, P()), out_specs=spec, check_vma=False
    )
```

```python
import jax
import jax.numpy as jnp
import ml_dtypes
import numpy as np
from jax import lax
from jax.experimental import pallas as pl
from jax.experimental.pallas import tpu as pltpu
from jax.sharding import Mesh
from jax.sharding import PartitionSpec as P


SMOOTH_STEPS = 3
COARSE_STEPS = 12
NX, NZ, NY = 32, 16, 73
DEVICES = 256
ROWS = 80
screen_shift = 0.02
smooth_floor = 0.1
coarse_floor = 0.01
f32 = jnp.float32
bf16 = jnp.bfloat16


def legendre_values(points, degree):
    columns = [np.ones(points.shape), points]
    for n in range(2, degree + 1):
        columns.append(((2 * n - 1) * points * columns[-1] - (n - 1) * columns[-2]) / n)
    return np.stack(columns[: degree + 1], axis=1)


def gll_tables(degree):
    nodes = -np.cos(np.pi * np.arange(degree + 1) / degree)
    for _ in range(100):
        values = legendre_values(nodes, degree)
        nodes = nodes - (nodes * values[:, degree] - values[:, degree - 1]) / (
            (degree + 1) * values[:, degree]
        )
    leading = legendre_values(nodes, degree)[:, degree]
    weights = 2.0 / (degree * (degree + 1) * leading**2)
    differ = np.zeros((degree + 1, degree + 1))
    for i in range(degree + 1):
        for j in range(degree + 1):
            if i != j:
                differ[i, j] = leading[i] / (leading[j] * (nodes[i] - nodes[j]))
    differ[0, 0] = -degree * (degree + 1) / 4.0
    differ[degree, degree] = degree * (degree + 1) / 4.0
    return nodes, weights, differ.T @ (weights[:, None] * differ)


def interp_table(fine_degree, coarse_degree):
    fine_nodes = gll_tables(fine_degree)[0]
    coarse_nodes = gll_tables(coarse_degree)[0]
    lagrange = np.ones((fine_degree + 1, coarse_degree + 1))
    for col in range(coarse_degree + 1):
        for other in range(coarse_degree + 1):
            if other != col:
                lagrange[:, col] *= (fine_nodes - coarse_nodes[other]) / (
                    coarse_nodes[col] - coarse_nodes[other]
                )
    return lagrange


def lane_at(a, b):
    n = 7 * b + a
    return n if n < 25 else n + 7


def lanes_of(values):
    n = values.shape[0]
    out = np.zeros(64)
    for a in range(n):
        for b in range(n):
            out[lane_at(a, b)] = values[a, b]
    return out


def square_of(matrix, n_out, n_in):
    rows = [lane_at(a, b) for a in range(n_out) for b in range(n_out)]
    columns = [lane_at(a, b) for a in range(n_in) for b in range(n_in)]
    out = np.zeros((64, 64))
    out[np.ix_(rows, columns)] = matrix
    return out


def line_basis(q, t):
    u = np.zeros((q, q), complex)
    u[0, 0] = 1.0
    turn = np.exp(-0.5j * t) / np.sqrt(2.0)
    for a in range(1, (q + 1) // 2):
        u[a, a] = u[a, q - a] = turn
        u[q - a, a], u[q - a, q - a] = -1j * turn, 1j * turn
    return u


def closing(q, t):
    out = np.eye(q + 1, q, dtype=complex)
    out[q, 0] = np.exp(1j * t)
    return out


def real_parts(matrix_of, count):
    angles = 0.3 + 0.7 * np.arange(8)
    terms = np.stack([np.ones(8), np.cos(angles / 2), np.sin(angles / 2), np.cos(angles)], 1)[:, :count]
    values = np.stack([matrix_of(t) for t in angles])
    flat = values.reshape(8, -1)
    parts = np.linalg.lstsq(terms, flat.real, rcond=None)[0]
    assert np.abs(terms @ parts - flat).max() < 1e-11 * np.abs(flat).max()
    return parts.reshape((count,) + values.shape[1:])


class Level:
    def __init__(self, q):
        self.q = q
        _, w, s = gll_tables(q)
        self.w, self.s = w, s
        mass = 0.5 * w[:q].copy()
        mass[0] = 0.5 * (w[0] + w[q])
        diag = 2.0 * np.diag(s)[:q].copy()
        diag[0] = 2.0 * (s[0, 0] + s[q, q])
        self.mxz = np.outer(mass, mass)
        a = np.outer(diag, mass) + np.outer(mass, diag) + screen_shift * self.mxz
        self.ratio = lanes_of(a / self.mxz)
        spread = np.abs(s).sum(axis=1)
        self.bound = max(1.0, float(np.max(spread / np.diag(s))))
        base = 2.0 * s[:q, :q].copy()
        base[0, 0] += 2.0 * s[q, q]
        e1 = np.zeros((q, q))
        e1[:, 0] = 2.0 * s[:q, q]
        even, odd = e1 + e1.T, e1 - e1.T
        dm = np.diag(mass)
        scale = np.concatenate([lanes_of(1.0 / self.mxz)] * 2)[None, :]
        sq = lambda m: square_of(m, q, q)
        span = real_parts(
            lambda t: line_basis(q, t) @ closing(q, t).conj().T @ (2.0 * s) @ closing(q, t) @ line_basis(q, t).conj().T, 4
        )
        fixed = sq(np.kron(base, dm) + np.kron(dm, span[0]) + screen_shift * np.kron(dm, dm))
        tables = [np.hstack([fixed, 0.0 * fixed])]
        tables.append(np.hstack([sq(np.kron(even, dm)), -sq(np.kron(odd, dm))]))
        for part in span[1:]:
            part = sq(np.kron(dm, part))
            tables.append(np.hstack([part, 0.0 * part]))
        self.tables = [(t * scale)[: 64 if q > 3 else 24] for t in tables]
        self.weight = 0.5 * w
        self.stiff = s / self.weight[:, None]
        self.mass_lanes = np.concatenate([lanes_of(self.mxz)] * 2)
        self.inv_mass_lanes = np.concatenate([lanes_of(1.0 / self.mxz)] * 2)
        self.ratio_lanes = np.concatenate([self.ratio] * 2)
        self.mask_lanes = (self.mass_lanes > 0).astype(np.float64)


def transfer_tables(fine, coarse):
    j = interp_table(fine, coarse)
    ja = j[:fine, :coarse]
    jb = np.zeros((fine, coarse))
    jb[:, 0] = j[:fine, coarse]
    span = real_parts(
        lambda t: line_basis(fine, t) @ j[:fine] @ closing(coarse, t) @ line_basis(coarse, t).conj().T, 3
    )
    tables = []
    for part in span:
        for flow in (ja, jb):
            b = square_of(np.kron(flow, part), fine, coarse).T[: 24 if coarse > 1 else 8]
            tables.append(np.hstack([b, b if flow is jb else 0.0 * b]))
    return j, tables


def phase_rows():
    rows = np.zeros((80, 2, 64))
    for n in range(16):
        t = 2 * np.pi * n / NX
        if n:
            rows[2 * n], rows[2 * n + 1] = np.cos(t), np.sin(t)
        else:
            rows[0, 0], rows[0, 1] = 1.0, -1.0
    for k in range(8):
        for part in range(2):
            t = 2 * np.pi * k / NZ if k else np.pi * part
            at = 32 + 3 * (2 * k + part)
            rows[at], rows[at + 1], rows[at + 2] = np.cos(t / 2), np.sin(t / 2), np.cos(t)
    return rows.reshape(80, 128)


FINE, MID, LOW = Level(7), Level(3), Level(1)
J7, P7_TABLES = transfer_tables(7, 3)
J3, P3_TABLES = transfer_tables(3, 1)
MATRICES = np.concatenate(FINE.tables + MID.tables + P7_TABLES + P3_TABLES).astype(np.float32)
R7 = FINE.weight[:, None] * J7 / MID.weight
R3 = MID.weight[:, None] * J3 / LOW.weight
G7_AT, G3_AT, P7_AT, P3_AT = 0, 320, 440, 584


LANES = np.zeros((16, 128))
for n, level in enumerate((FINE, MID)):
    LANES[4 * n] = level.mass_lanes
    LANES[4 * n + 1] = level.inv_mass_lanes
    LANES[4 * n + 2] = level.ratio_lanes
    LANES[4 * n + 3] = level.mask_lanes
LANES[8] = LOW.mask_lanes
MATRICES = np.concatenate([MATRICES, LANES, phase_rows()]).astype(np.float32)
LANES_AT, PHASES_AT = 632, 648


def cheb_steps(bound, sweeps, floor):
    centre = bound * (1.0 + floor) / 2.0
    half = bound * (1.0 - floor) / 2.0
    s = centre / half
    p = 1.0 / s
    steps = []
    for _ in range(sweeps - 1):
        p_next = 1.0 / (2.0 * s - p)
        steps.append((p_next * p, 2.0 * p_next / half))
        p = p_next
    return 1.0 / centre, steps


FLOW, SPAN = ("zh", "z0", "xh", "core"), ("xl", "y")
LAST = ("core", "xl", "y")
USED = 8 * 49
SLAB = 13
FIELD = 32 * SLAB


def swap(v):
    return pltpu.roll(v, 64, axis=1)


def mix(first, v, w):
    return jnp.where(first, v, swap(w)), jnp.where(first, swap(v), w)


def pack_kernel(x_hbm, h_hbm, o_ref, rows_ref, x_ref, h_ref, line_ref, sems):
    line = pltpu.make_async_copy(h_hbm, h_ref, sems.at[0])
    line.start()
    field = pltpu.make_async_copy(x_hbm, x_ref, sems.at[1])
    field.start()
    first, _ = lane_tools()
    line_ref[...] = jnp.zeros_like(line_ref)
    line.wait()
    line_ref[0:1, 0:NY] = h_ref[...]
    rows_ref[...] = jnp.broadcast_to(line_ref[0:1, :], (128, 128)).T[:ROWS]
    field.wait()
    for a in range(7):
        for t in range(4):
            part = slice(128 * t, 128 * t + 128)
            low, high = mix(first, x_ref[a, 0:7, part], x_ref[a, 7:14, part])
            o_ref[pl.ds(98 * t + a, 7, stride=7), :] = low
            o_ref[pl.ds(98 * t + 49 + a, 7, stride=7), :] = high


def unpack_kernel(x_ref, o_ref):
    first, _ = lane_tools()
    for a in range(7):
        for t in range(4):
            part = slice(128 * t, 128 * t + 128)
            low, high = mix(
                first,
                x_ref[pl.ds(98 * t + a, 7, stride=7), :],
                x_ref[pl.ds(98 * t + 49 + a, 7, stride=7), :],
            )
            o_ref[a, 0:7, part] = low
            o_ref[a, 7:14, part] = high


def halves(v):
    high = v.astype(bf16)
    return high, (v - high.astype(f32)).astype(bf16)


def dot(a, b):
    return jnp.dot(a, b, preferred_element_type=f32)


HALF = float(np.sqrt(0.5))


def lane_tools():
    first = lax.broadcasted_iota(jnp.int32, (1, 128), 1) < 64
    return first, jnp.where(first, 1.0, -1.0).astype(f32)


def span_modes(x, first, sign, offset, size):
    s = [None] + [x[j] + x[8 - j] for j in (1, 2, 3)]
    d = [None] + [x[j] - x[8 - j] for j in (1, 2, 3)]
    up, down = x[0] + x[4], x[0] - x[4]
    odd, turn = s[1] + s[3], HALF * (s[1] - s[3])
    slope = HALF * (d[1] + d[3])
    re = [up + s[2] + odd, down + turn, up - s[2], down - turn, up + s[2] - odd]
    im = [None, -slope - d[2], d[3] - d[1], d[2] - slope]

    def phases(k):
        t = np.pi * k / 8
        p = 0.0 if offset is None else t / 2 + offset
        return [float(size * v) for v in (np.cos(p), np.sin(p), np.cos(p + t), np.sin(p + t))]

    flip = swap(re[0])
    out = [None] * 8
    out[0] = jnp.where(first, re[0] + flip, flip - re[0])
    c, s, v, w = phases(4)
    out[4] = jnp.where(first, c, -w) * re[4] + jnp.where(first, v, -s) * swap(re[4])
    for f in (1, 2, 3):
        re_swap, im_swap = swap(re[f]), swap(im[f])
        a = jnp.where(first, re[f], im_swap)
        b = jnp.where(first, im[f], -re_swap)
        p = jnp.where(first, re_swap, im[f])
        q = jnp.where(first, im_swap, -re[f])
        c, s, v, w = phases(f)
        out[f] = (c * a + v * p) + (s * b + w * q)
        c, s, v, w = phases(8 - f)
        out[8 - f] = sign * ((c * a + v * p) - (s * b + w * q))
    return out


def span_elements(x, first, sign, offset, size):
    def phases(k):
        t = np.pi * k / 8
        p = 0.0 if offset is None else t / 2 + offset
        return [float(size * v) for v in (np.cos(p), np.sin(p), np.cos(p + t), np.sin(p + t))]

    pick = lambda p, q: jnp.where(first, p, q)
    flip = swap(x[0])
    re = [jnp.where(first, x[0] + flip, flip - x[0])]
    im = [None]
    for f in (1, 2, 3):
        c, s, v, w = [2.0 * n for n in phases(f)]
        near, near_swap = x[f], swap(x[f])
        one = pick(c, -w) * near + pick(-s, v) * near_swap
        two = pick(s, v) * near + pick(c, w) * near_swap
        c, s, v, w = [2.0 * n for n in phases(8 - f)]
        far, far_swap = x[8 - f], swap(x[8 - f])
        re.append(one + (pick(c, -w) * far + pick(-s, v) * far_swap))
        im.append(two - (pick(s, v) * far + pick(c, w) * far_swap))
    c, s, v, w = [2.0 * n for n in phases(4)]
    re.append(pick(c, -w) * x[4] + pick(-s, v) * swap(x[4]))
    up, down = re[0] + re[4], re[0] - re[4]
    odd, turn = re[1] + re[3], HALF * (re[1] - re[3])
    slope = HALF * (im[1] + im[3])
    c = [up + re[2] + odd, down + turn, up - re[2], down - turn, up + re[2] - odd]
    s = [None, slope + im[2], im[1] - im[3], slope - im[2]]
    return [c[0]] + [c[j] - s[j] for j in (1, 2, 3)] + [c[4]] + [c[j] + s[j] for j in (3, 2, 1)]


ORDER = ("core", "zh", "z0", "xh")


def flow_place(n):
    return n % 2 * 16 + n // 2


def mode_rows(k, part, half):
    at = SLAB * (16 * half + 4 * (k // 2) + 2 * part + k % 2)
    return slice(at, at + SLAB)


def span_forward_kernel(x_ref, o_ref, v_ref):
    first, sign = lane_tools()
    for k in range(8):
        v_ref[k, 48:56] = jnp.zeros((8, 128), f32)
    nodes = lambda b: [x_ref[49 * j + 7 * b : 49 * j + 7 * b + 7, :] for j in range(8)]
    for k, v in enumerate(span_modes(nodes(0), first, sign, None, 1.0)):
        v_ref[k, 0:7] = v
    for b in (1, 2, 3):
        near, far = nodes(b), nodes(7 - b)
        total = span_modes([p + q for p, q in zip(near, far)], first, sign, 0.0, HALF)
        differ = span_modes([p - q for p, q in zip(near, far)], first, sign, np.pi / 2, HALF)
        total[0], differ[0] = HALF * total[0], -HALF * differ[0]
        for k in range(8):
            v_ref[k, 7 * b : 7 * b + 7] = total[k]
            v_ref[k, 7 * (7 - b) : 7 * (7 - b) + 7] = differ[k]
    for k in range(8):
        re, im = mix(first, v_ref[k, 0:26], v_ref[k, 25:51])
        for part, v in enumerate((re, im)):
            o_ref[mode_rows(k, part, 0), :] = v[:SLAB]
            o_ref[mode_rows(k, part, 1), :] = v[SLAB:]


def span_backward_kernel(x_ref, o_ref, v_ref):
    first, sign = lane_tools()
    for k in range(8):
        for half, rows in ((0, 13), (1, 12)):
            near, far = mix(first, x_ref[mode_rows(k, 0, half), :], x_ref[mode_rows(k, 1, half), :])
            v_ref[k, 13 * half : 13 * half + rows] = near[:rows]
            v_ref[k, 25 + 13 * half : 37 + 12 * half + (1 - half)] = far[: 13 - 2 * half]

    def store(b, planes):
        for j, v in enumerate(planes):
            o_ref[49 * j + 7 * b : 49 * j + 7 * b + 7, :] = v

    store(0, span_elements([v_ref[k, 0:7] for k in range(8)], first, sign, None, 1.0))
    for b in (1, 2, 3):
        total = [v_ref[k, 7 * b : 7 * b + 7] for k in range(8)]
        differ = [v_ref[k, 7 * (7 - b) : 7 * (7 - b) + 7] for k in range(8)]
        total[0], differ[0] = HALF * total[0], -HALF * differ[0]
        total = span_elements(total, first, sign, 0.0, HALF)
        differ = span_elements(differ, first, sign, np.pi / 2, HALF)
        store(b, [p + q for p, q in zip(total, differ)])
        store(7 - b, [p - q for p, q in zip(total, differ)])


def line_modes(x):
    n = len(x)
    if n == 1:
        return [(x[0], None)]
    even, odd = line_modes(x[0::2]), line_modes(x[1::2])
    out = [None] * (n // 2 + 1)
    out[0], out[n // 2] = (even[0][0] + odd[0][0], None), (even[0][0] - odd[0][0], None)
    for k in range(1, n // 4 + 1):
        (p, q), (v, w) = even[k], odd[k]
        if 4 * k == n:
            out[k] = (p, -v)
            continue
        c, s = float(np.cos(2 * np.pi * k / n)), float(np.sin(2 * np.pi * k / n))
        re, im = c * v + s * w, c * w - s * v
        out[k], out[n // 2 - k] = (p + re, q + im), (p - re, im - q)
    return out


def line_elements(modes, n):
    if n == 1:
        return [modes[0][0]]
    even, odd = [None] * (n // 4 + 1), [None] * (n // 4 + 1)
    low, high = modes[0][0], modes[n // 2][0]
    even[0], odd[0] = (low + high, None), (low - high, None)
    for k in range(1, n // 4 + 1):
        (p, q), (v, w) = modes[k], modes[n // 2 - k]
        if 4 * k == n:
            even[k], odd[k] = (2.0 * p, None), (-2.0 * q, None)
            continue
        c, s = float(np.cos(2 * np.pi * k / n)), float(np.sin(2 * np.pi * k / n))
        re, im = p - v, q + w
        even[k], odd[k] = (p + v, q - w), (c * re - s * im, c * im + s * re)
    x, y = line_elements(even, n // 2), line_elements(odd, n // 2)
    return [v for pair in zip(x, y) for v in pair]


def slab(ref, n):
    return ref[n * SLAB : n * SLAB + SLAB, :]


def flow_forward_kernel(x_ref, o_ref):
    modes = line_modes([slab(x_ref, flow_place(n)) for n in range(NX)])
    for n in range(16):
        re, im = modes[n][0], modes[n][1] if n else modes[16][0]
        o_ref[26 * n : 26 * n + 13, :] = re
        o_ref[26 * n + 13 : 26 * n + 26, :] = im


def flow_backward_kernel(x_ref, o_ref):
    modes = [(slab(x_ref, 2 * n), slab(x_ref, 2 * n + 1)) for n in range(16)]
    modes = [(modes[0][0], None)] + modes[1:] + [(modes[0][1], None)]
    for n, v in enumerate(line_elements(modes, NX)):
        at = SLAB * flow_place(n)
        o_ref[at : at + SLAB, :] = v


def table_product(v, t_ref):
    both = dot(jnp.concatenate(halves(v), axis=1), t_ref[...])
    return both[:, :128] + both[:, 128:]


def store_table(t_ref, table):
    high, low = halves(table)
    t_ref[0:128, 0:128] = high
    t_ref[128:256, 0:128] = high
    t_ref[0:128, 128:256] = low
    t_ref[128:256, 128:256] = jnp.zeros((128, 128), bf16)


def roll_up(v):
    return pltpu.roll(v, ROWS - 1, axis=0)


def roll_down(v):
    return pltpu.roll(v, 1, axis=0)


def element_products(s, q, planes):
    parts = list(planes) + [roll_up(planes[0])]
    n = q + 1
    half = n // 2
    even = [parts[l] + parts[q - l] for l in range(half)]
    odd = [parts[l] - parts[q - l] for l in range(half)]
    out = [None] * n
    for k in range(half):
        p = m = None
        for l in range(half):
            ce = 0.5 * (s[k, l] + s[k, q - l])
            co = 0.5 * (s[k, l] - s[k, q - l])
            te, to = float(ce) * even[l], float(co) * odd[l]
            p = te if p is None else p + te
            m = to if m is None else m + to
        out[k] = p + m
        out[q - k] = p - m
    return out


def weighted_sum(coefs, planes):
    total = None
    for c, v in zip(coefs, planes):
        c = float(c)
        if c == 0.0:
            continue
        t = v if c == 1.0 else c * v
        total = t if total is None else total + t
    return total


def restrict_wall(j, fine, coarse, planes, h, inv_pair):
    out = [weighted_sum(j[1:fine, c], planes[1:]) for c in range(coarse)]
    shared = h * out[0] + roll_down(h * weighted_sum(j[1:fine, coarse], planes[1:]))
    out[0] = float(j[0, 0]) * planes[0] + inv_pair * shared
    return out


def prolong_wall(j, fine, coarse, planes):
    closed = list(planes) + [roll_up(planes[0])]
    return [weighted_sum(j[k], closed) for k in range(fine)]


PIECES = [(y, half, part) for y in range(2) for half in range(2) for part in range(2)]


def cycle_kernel(
    h_ref, mats_ref, in_ref, out_ref,
    w_ref, geo_ref,
    u7, r7, x7, d7, u3, r3, x3, d3,
    square, g7_ref, g3_ref, r7_ref, p7_ref, r3_ref, p3_ref,
):
    at_x = PHASES_AT + 2 * lax.axis_index(LAST)
    at_z = PHASES_AT + 32 + 3 * lax.axis_index(("zh", "xh", "z0"))
    cx, sx = mats_ref[pl.ds(at_x, 1), :], mats_ref[pl.ds(at_x + 1, 1), :]
    ch, sh, cz = (mats_ref[pl.ds(at_z + n, 1), :] for n in range(3))
    lane = lax.broadcasted_iota(jnp.int32, (1, 128), 1)
    first = lane < 64
    mass7, inv7, ratio7, mask7 = (mats_ref[n : n + 1, :] for n in range(LANES_AT, LANES_AT + 4))
    mass3, inv3, ratio3, mask3 = (mats_ref[n : n + 1, :] for n in range(LANES_AT + 4, LANES_AT + 8))
    mask1 = mats_ref[LANES_AT + 8 : LANES_AT + 9, :]

    both = (cx, sx)
    alone = lambda c: (c, jnp.zeros_like(c))
    operator = [both, alone(ch), alone(sh), alone(cz)]
    transfer = [both, alone(ch), (cx * ch, sx * ch), alone(sh), (cx * sh, sx * sh)]

    def mode_table(at, rows, phases):
        top = mats_ref[at : at + rows]
        low = pltpu.roll(top, 64, axis=1)
        for c, s in phases:
            at += rows
            t = mats_ref[at : at + rows]
            top = top + jnp.where(first, c, s) * t
            low = low + jnp.where(first, -s, c) * pltpu.roll(t, 64, axis=1)
        if rows == 64:
            return jnp.concatenate([top, low], axis=0)
        square[...] = jnp.zeros((128, 128), f32)
        square[0:rows] = top
        square[64 : 64 + rows] = low
        return square[...]

    store_table(g7_ref, mode_table(G7_AT, 64, operator))
    store_table(g3_ref, mode_table(G3_AT, 24, operator))
    table = mode_table(P7_AT, 24, transfer)
    store_table(p7_ref, table)
    store_table(r7_ref, (table * mass7).T * inv3)
    table = mode_table(P3_AT, 8, transfer)
    store_table(p3_ref, table)
    store_table(r3_ref, (table * mass3).T)

    scale = inv7 * (1.0 / (NX * NZ))
    outer = lane % 64 < 32
    square[...] = jnp.zeros((128, 128), f32)
    for t in range(4):
        for y, half, part in PIECES:
            r, v = 64 * part + 32 * y + 13 * half, 208 * half + 26 * (2 * t + y) + 13 * part
            square[r : r + 13, :] = in_ref[v : v + 13, :]
        both = square[...].T
        low, high = both[:64], both[64:]
        w_ref[128 * t : 128 * t + 64, :] = jnp.where(outer, low, pltpu.roll(high, 32, axis=1)) * scale
        w_ref[128 * t + 64 : 128 * t + 128, :] = jnp.where(outer, pltpu.roll(low, 96, axis=1), high) * scale
    w_ref[512:, :] = jnp.zeros((w_ref.shape[0] - 512, 128), f32)
    h = h_ref[...]
    row = lax.broadcasted_iota(jnp.int32, (ROWS, 128), 0)
    inv = jnp.where(row < NY, 1.0 / jnp.where(row < NY, h, 1.0), 0.0)
    g = 2.0 * inv
    h_pair = h + roll_down(h)
    g_pair = g + roll_down(g)
    inv_pair = jnp.where(row <= NY, 1.0 / jnp.where(row <= NY, h_pair, 1.0), 0.0)
    geo_ref[0] = h
    geo_ref[1] = g
    geo_ref[2] = inv_pair
    geo_ref[3] = g * inv

    def inverse_diags(d, level, ratio, mask):
        start, steps = cheb_steps(level.bound, SMOOTH_STEPS, smooth_floor)
        for k in range(level.q):
            wall = geo_ref[3] if k else g_pair * inv_pair
            total = ratio + float(level.stiff[k, k]) * wall
            used = (row < NY if k else row <= NY) & (mask > 0.0)
            total = jnp.where(used, 1.0 / jnp.where(used, total, 1.0), 0.0)
            for n, factor in enumerate([start] + [beta for _, beta in steps]):
                d[n, k] = factor * total

    inverse_diags(d7, FINE, ratio7, mask7)
    inverse_diags(d3, MID, ratio3, mask3)
    d1_mix = (4.0 + screen_shift) - 2.0 * cx - 2.0 * cz
    d1 = h_pair * (4.0 + screen_shift) + g_pair
    used = (row <= NY) & (mask1 > 0.0)
    d1 = jnp.where(used, 1.0 / jnp.where(used, d1, 1.0), 0.0)

    for k in range(7):
        factor = float(1.0 / FINE.weight[k]) * (inv if k else inv_pair)
        r7[k] = factor * w_ref[pl.ds(k, ROWS, stride=7), :]

    def apply(level, u, table):
        q = level.q
        m = table_product(u[...].reshape(q * ROWS, 128), table)
        wall = element_products(level.stiff, q, [u[k] for k in range(q)])
        shared = geo_ref[1] * wall[0] + roll_down(geo_ref[1] * wall[q])
        out = [m[:ROWS] + geo_ref[2] * shared]
        return out + [m[k * ROWS : (k + 1) * ROWS] + geo_ref[3] * wall[k] for k in range(1, q)]

    def smooth(level, u, r, x, d, table, fresh, keep_residual):
        q = level.q
        steps = cheb_steps(level.bound, SMOOTH_STEPS, smooth_floor)[1]
        for k in range(q):
            t = d[0, k] * r[k]
            u[k] = t
            x[k] = t if fresh else x[k] + t
        for n, (alpha, _) in enumerate(steps):
            au = apply(level, u, table)
            for k in range(q):
                t = r[k] - au[k]
                r[k] = t
                t = alpha * u[k] + d[n + 1, k] * t
                u[k] = t
                x[k] = x[k] + t
        if keep_residual:
            au = apply(level, u, table)
            for k in range(q):
                r[k] = r[k] - au[k]

    def product(planes, table):
        m = table_product(jnp.concatenate(planes, axis=0), table)
        return [m[k * ROWS : (k + 1) * ROWS] for k in range(len(planes))]

    smooth(FINE, u7, r7, x7, d7, g7_ref, True, True)
    down = product(restrict_wall(R7, 7, 3, [r7[k] for k in range(7)], geo_ref[0], geo_ref[2]), r7_ref)
    for k in range(3):
        r3[k] = down[k]

    smooth(MID, u3, r3, x3, d3, g3_ref, True, True)
    r1 = product(restrict_wall(R3, 3, 1, [r3[k] for k in range(3)], geo_ref[0], geo_ref[2]), r3_ref)[0]

    start, steps = cheb_steps(LOW.bound, COARSE_STEPS, coarse_floor)
    middle = d1 * (h_pair * d1_mix + g_pair)
    after, before = d1 * g, d1 * roll_down(g)
    r1 = (d1 * h_pair) * r1
    u1 = start * r1
    x1 = u1
    for alpha, beta in steps:
        r1 = (r1 - middle * u1) + (after * roll_up(u1) + before * roll_down(u1))
        u1 = alpha * u1 + beta * r1
        x1 = x1 + u1

    up = prolong_wall(J3, 3, 1, product([x1], p3_ref))
    for k in range(3):
        u3[k] = up[k]
        x3[k] = x3[k] + up[k]
    au = apply(MID, u3, g3_ref)
    for k in range(3):
        r3[k] = r3[k] - au[k]
    smooth(MID, u3, r3, x3, d3, g3_ref, False, False)

    up = prolong_wall(J7, 7, 3, product([x3[k] for k in range(3)], p7_ref))
    for k in range(7):
        u7[k] = up[k]
        x7[k] = x7[k] + up[k]
    au = apply(FINE, u7, g7_ref)
    for k in range(7):
        r7[k] = r7[k] - au[k]
    smooth(FINE, u7, r7, x7, d7, g7_ref, False, False)

    for k in range(7):
        w_ref[pl.ds(k, ROWS, stride=7), :] = x7[k]
    for t in range(4):
        low, high = w_ref[128 * t : 128 * t + 64, :], w_ref[128 * t + 64 : 128 * t + 128, :]
        square[...] = jnp.concatenate(
            [
                jnp.where(outer, low, pltpu.roll(high, 32, axis=1)),
                jnp.where(outer, pltpu.roll(low, 96, axis=1), high),
            ],
            axis=0,
        ).T
        for y, half, part in PIECES:
            r, v = 64 * part + 32 * y + 13 * half, 208 * half + 26 * (2 * t + y) + 13 * part
            out_ref[v : v + 13, :] = square[r : r + 13, :]


VMEM = pl.BlockSpec(memory_space=pltpu.VMEM)
HBM = pl.BlockSpec(memory_space=pltpu.HBM)
PARAMS = pltpu.CompilerParams(vmem_limit_bytes=32 * 1024 * 1024)
FLAT = jax.ShapeDtypeStruct((FIELD, 128), f32)
TIGHT = jax.ShapeDtypeStruct((USED, 128), f32)
LINES = [pltpu.VMEM((8, 56, 128), f32)]


def exchange(block, axes):
    n, rows = lax.axis_size(axes), block.shape[0]
    block = block.reshape(n, rows // n, 1, 128)
    return lax.all_to_all(block, axes, 0, 0).reshape(rows, 128)


def cycle_call(heights, modes):
    fine = pltpu.VMEM((7, ROWS, 128), f32)
    mid = pltpu.VMEM((3, ROWS, 128), f32)
    table = pltpu.VMEM((256, 256), bf16)
    return pl.pallas_call(
        cycle_kernel, out_shape=FLAT,
        in_specs=[VMEM, VMEM, VMEM], out_specs=VMEM,
        scratch_shapes=[
            pltpu.VMEM((7 * ROWS, 128), f32), pltpu.VMEM((4, ROWS, 128), f32),
            fine, fine, fine, pltpu.VMEM((SMOOTH_STEPS, 7, ROWS, 128), f32),
            mid, mid, mid, pltpu.VMEM((SMOOTH_STEPS, 3, ROWS, 128), f32),
            pltpu.VMEM((128, 128), f32), table, table, table, table, table, table,
        ],
        compiler_params=PARAMS,
    )(
        heights, jnp.asarray(MATRICES), modes,
    )


def transform(kernel, block, out_shape=FLAT, scratch=()):
    return pl.pallas_call(
        kernel, out_shape=out_shape, in_specs=[VMEM], out_specs=VMEM,
        scratch_shapes=scratch, compiler_params=PARAMS,
    )(block)


def body(residual, layer_heights):
    stay = lambda v: pltpu.with_memory_space_constraint(v, pltpu.HBM)
    packed, heights = pl.pallas_call(
        pack_kernel, out_shape=(TIGHT, jax.ShapeDtypeStruct((ROWS, 128), f32)),
        in_specs=[HBM, HBM], out_specs=(VMEM, VMEM),
        scratch_shapes=[
            pltpu.VMEM((7, 14, 512), f32), pltpu.VMEM((1, NY), f32), pltpu.VMEM((8, 128), f32),
            pltpu.SemaphoreType.DMA((2,)),
        ],
        compiler_params=PARAMS,
    )(stay(residual), stay(layer_heights.reshape(1, NY)))
    spans = transform(span_forward_kernel, exchange(packed, SPAN), scratch=LINES)
    modes = exchange(transform(flow_forward_kernel, exchange(spans, ORDER)), LAST)
    solved = exchange(cycle_call(heights, modes), LAST)
    flows = exchange(transform(flow_backward_kernel, solved), ORDER)
    spread = exchange(transform(span_backward_kernel, flows, TIGHT, LINES), SPAN)
    return pl.pallas_call(
        unpack_kernel, out_shape=jax.ShapeDtypeStruct((7, 14, 512), f32),
        in_specs=[VMEM], out_specs=VMEM, compiler_params=PARAMS,
    )(spread)


def solution(mesh):
    split = Mesh(mesh.devices.reshape(4, 2, 2, 2, 2, 4), FLOW + SPAN)
    spec = P(FLOW, SPAN, None)
    return jax.shard_map(
        body, mesh=split, in_specs=(spec, P()), out_specs=spec, check_vma=False
    )
```
